32 devices in a mesh: batch: 2 (over x), mp: 16 (over z, y, core).
Axes of the slice: x: 2, y: 2, z: 4, core: 2. Of those that a mesh axis runs over, the one named last changes fastest.
Arguments:
- conv_input: bfloat16 [128, 2, 13, 13, 384], P(('batch', 'mp')), may hold values from -6 to 6
- group: int32 [128], P(('batch', 'mp')), may hold values from 0 to 1
- conv_weight: bfloat16 [2, 3456, 256], P(None, 'mp'), may hold values from -0.109375 to 0.109375
- conv_bias: float32 [2, 256], replicated, may hold values from -3 to 3
- stitch_pool: float32 [2, 2, 256], replicated, may hold values from 0.2 to 1
- fc_weight: bfloat16 [2, 9216, 4096], P(None, None, 'mp'), may hold values from -0.0625 to 0.0625
- fc_bias: float32 [2, 4096], P(None, 'mp'), may hold values from -3 to 3
- stitch_fc: float32 [2, 2, 4096], P(None, None, 'mp'), may hold values from 0.2 to 1
- cotangent: bfloat16 [128, 2, 4096], P(('batch', 'mp')), may hold values from -6 to 6
Outputs:
- output: bfloat16 [128, 2, 4096], P(('batch', 'mp'))
- input_grad: bfloat16 [128, 2, 13, 13, 384], P(('batch', 'mp'))
- conv_weight_grad: float32 [2, 3456, 256], P(None, 'mp')
- conv_bias_grad: float32 [2, 256], replicated
- stitch_pool_grad: float32 [2, 2, 256], replicated
- fc_weight_grad: float32 [2, 9216, 4096], P(None, 'batch', 'mp')
- fc_bias_grad: float32 [2, 4096], P(None, 'mp')
- stitch_fc_grad: float32 [2, 2, 4096], P(None, None, 'mp')
The draws below stay inside these ranges and needn't reach their ends.
Inputs may be any that keep to these rules, and one draw needn't show every extreme that they name: `group`: 0 marks a 227-pixel image whose maps fill all 13 x 13 cells; 1 marks a 195-pixel image whose maps fill the first 11 rows and columns.
All inputs are finite; a program needn't handle non-finite values.
Results may differ from the reference program's by a relative error of at most 0.006.
Values may be sent and summed in bfloat16 or wider, within the bound.
No kernel may reach another device: no remote copies, remote signals or barrier semaphores. Data moves between devices by JAX's collectives and lax.ppermute only.
A program may use at most 128 MiB of HBM per device.

```python
import math
import jax
import jax.numpy as jnp
from jax import lax

CIN = 384
COUT = 256
HID = 4096
MAP = 13
POOL = 6
FEAT = 9216
KC = 3456
IMGS = 128


def set_ends(array, own_key, low, largest):
    extent = array.shape
    spot = [jax.random.randint(jax.random.fold_in(own_key, axis), (), 0, extent[axis]) for axis in range(len(extent))]
    array = array.at[tuple(spot)].set(low)
    longest = extent.index(max(extent))
    spot[longest] = (spot[longest] + 1) % extent[longest]
    return array.at[tuple(spot)].set(largest)


def levels(key, shape, shards, low, high):
    def one(position, shards_of):
        heights = jax.random.uniform(jax.random.fold_in(jax.random.fold_in(key, 6), position), (shards_of,), jnp.float32, low / len(shards), high / len(shards))
        return jnp.repeat(jnp.exp(heights), shape[position] // shards_of).reshape((-1,) + (1,) * (len(shape) - position - 1))

    factor_of = one(*shards[0])
    for cut in shards[1:]:
        factor_of = factor_of * one(*cut)
    return factor_of


def gaussian(key, extent, spread, reach, pieces=(), held_as=jnp.bfloat16):
    factor_of = levels(key, extent, pieces, -0.22, 0.18) if pieces else 1.0
    array = jax.random.normal(key, extent, jnp.float32) * spread * factor_of
    return jnp.minimum(jnp.maximum(array, -reach), reach).astype(held_as)


def setup_inputs(seed: int = 0) -> dict:
    splits = jax.random.split(jax.random.key(seed), 10)
    conv_input = gaussian(splits[0], (IMGS, 2, MAP, MAP, CIN), 1.0, 6.0, ((0, 32),))
    group = set_ends(jax.random.randint(splits[1], (IMGS,), 0, 2), jax.random.fold_in(splits[1], 1), 0, 1).astype(jnp.int32)
    conv_weight = gaussian(splits[2], (2, KC, COUT), KC ** -0.5, 0.109375, ((1, 16),))
    conv_bias = gaussian(splits[3], (2, COUT), 0.5, 3.0, (), jnp.float32)
    stitch_pool = jnp.clip(jax.random.uniform(splits[4], (2, 2, COUT), jnp.float32, 0.2, 1.0), 0.2, 1.0)
    fc_weight = gaussian(splits[5], (2, FEAT, HID), FEAT ** -0.5, 0.0625, ((2, 16),))
    fc_bias = gaussian(splits[6], (2, HID), 0.5, 3.0, ((1, 16),), jnp.float32)
    stitch_fc = jnp.clip(0.2 + 0.8 * jax.random.uniform(splits[7], (2, 2, HID), jnp.float32) ** levels(splits[7], (2, 2, HID), ((2, 16),), -0.2, 0.2), 0.2, 1.0)
    cotangent = gaussian(splits[8], (IMGS, 2, HID), 1.0, 6.0, ((0, 32),))
    return dict(conv_input=conv_input, group=group, conv_weight=conv_weight, conv_bias=conv_bias, stitch_pool=stitch_pool, fc_weight=fc_weight, fc_bias=fc_bias, stitch_fc=stitch_fc, cotangent=cotangent)


@jax.custom_vjp
def low(v):
    return lax.optimization_barrier(v.astype(jnp.bfloat16)).astype(jnp.float32)

@jax.custom_vjp
def low_back(v):
    return v

def low_keep(v):
    return (low(v), None)

def low_pass(kept, grad):
    return (grad,)

def back_keep(v):
    return (v, None)

def back_low(kept, grad):
    return (low(grad),)
low.defvjp(low_keep, low_pass)
low_back.defvjp(back_keep, back_low)

def gelu_exact(value):
    return jax.nn.gelu(value, approximate=False)

def forward_block(conv_input, conv_weight, conv_bias, stitch_pool, fc_weight, fc_bias, stitch_fc, inside, kept):
    images = conv_input.shape[0]
    masked = conv_input * inside[:, None, :, :, None]
    kernel = conv_weight.reshape(2, 3, 3, CIN, COUT)
    conv_terms = []
    for task_id in range(2):
        conv_terms.append(lax.conv_general_dilated(masked[:, task_id], kernel[task_id], (1, 1), ((1, 1), (1, 1)), dimension_numbers=('NHWC', 'HWIO', 'NHWC'), precision=lax.Precision.HIGHEST))
    conv_pre = low_back(jnp.stack(conv_terms, axis=1) + conv_bias[None, :, None, None, :])
    conv_act = gelu_exact(conv_pre)
    span = 2 * POOL - 1
    pooled = jnp.zeros((images, 2, POOL, POOL, COUT), jnp.float32)
    for row_at in range(3):
        for col_at in range(3):
            pooled = pooled + conv_act[:, :, row_at:row_at + span:2, col_at:col_at + span:2, :]
    pooled = pooled / 9.0 * kept[:, None, :, :, None]
    stitched = jnp.einsum('tuc,nuyxc->ntyxc', stitch_pool, pooled, precision=lax.Precision.HIGHEST)
    features = low(stitched.reshape(images, 2, FEAT))
    fc_pre = jnp.einsum('ntf,tfh->nth', features, fc_weight, precision=lax.Precision.HIGHEST) + fc_bias[None]
    hidden = gelu_exact(low_back(fc_pre))
    return jnp.einsum('tuh,nuh->nth', stitch_fc, hidden, precision=lax.Precision.HIGHEST)

def forward(conv_input, conv_weight, conv_bias, stitch_pool, fc_weight, fc_bias, stitch_fc, inside, kept):
    images = conv_input.shape[0]
    block_rows = math.gcd(images, 128)
    block_count = images // block_rows

    def run(parts):
        return forward_block(parts[0], conv_weight, conv_bias, stitch_pool, fc_weight, fc_bias, stitch_fc, parts[1], parts[2])
    blocks = (conv_input.reshape((block_count, block_rows) + conv_input.shape[1:]), inside.reshape((block_count, block_rows) + inside.shape[1:]), kept.reshape((block_count, block_rows) + kept.shape[1:]))
    results = lax.map(jax.checkpoint(run), blocks)
    return results.reshape((images,) + results.shape[2:])

def reference(conv_input, group, conv_weight, conv_bias, stitch_pool, fc_weight, fc_bias, stitch_fc, cotangent):
    coords = jnp.arange(MAP, dtype=jnp.int32)
    limits = MAP - 2 * group
    inside = ((coords[None, :, None] < limits[:, None, None]) & (coords[None, None, :] < limits[:, None, None])).astype(jnp.float32)
    pool_coords = jnp.arange(POOL, dtype=jnp.int32)
    pool_limits = POOL - group
    kept = ((pool_coords[None, :, None] < pool_limits[:, None, None]) & (pool_coords[None, None, :] < pool_limits[:, None, None])).astype(jnp.float32)

    def wrapped(values, weights_a, bias_a, stitch_a, weights_b, bias_b, stitch_b):
        return forward(values, weights_a, bias_a, stitch_a, weights_b, bias_b, stitch_b, inside, kept)
    primal, pullback = jax.vjp(wrapped, conv_input.astype(jnp.float32), conv_weight.astype(jnp.float32), conv_bias, stitch_pool, fc_weight.astype(jnp.float32), fc_bias, stitch_fc)
    grads = pullback(cotangent.astype(jnp.float32))
    return (primal.astype(jnp.bfloat16), grads[0].astype(jnp.bfloat16), grads[1], grads[2], grads[3], grads[4], grads[5], grads[6])
```

```python
import functools

import jax
import jax.numpy as jnp
import numpy as np
from jax import lax
from jax.experimental import pallas as pl
from jax.experimental.pallas import tpu as pltpu
from jax.sharding import PartitionSpec as P

BOTH = ("batch", "mp")
WIDTH = 16
ROOT_HALF = 0.7071067811865476
ROOT_TWO_PI_INV = 0.3989422804014327
VMEM = pl.BlockSpec(memory_space=pltpu.VMEM)
LIMIT = 56 * 1024 * 1024


def kernel_call(body, out_shape, count, scratch=(), smem=0):
    return pl.pallas_call(
        body,
        out_shape=out_shape,
        in_specs=[pl.BlockSpec(memory_space=pltpu.SMEM)] * smem + [VMEM] * (count - smem),
        out_specs=jax.tree.map(lambda _: VMEM, out_shape),
        scratch_shapes=scratch,
        compiler_params=pltpu.CompilerParams(vmem_limit_bytes=LIMIT),
    )


def phi_cdf(value):
    return 0.5 * (1.0 + lax.erf(value * ROOT_HALF))


def gelu_slope(value):
    return phi_cdf(value) + value * ROOT_TWO_PI_INV * jnp.exp(-0.5 * value * value)


def window_sum(q_ref, value):
    high = value.astype(jnp.bfloat16)
    low = (value - high.astype(jnp.float32)).astype(jnp.bfloat16)
    return jnp.dot(q_ref[...], high, preferred_element_type=jnp.float32) + jnp.dot(
        q_ref[...], low, preferred_element_type=jnp.float32
    )


def conv_forward(side, pool, images, x_ref, w_ref, b_ref, q_ref, g_ref, pre_ref, pooled_ref):
    slab = images * WIDTH
    depth = x_ref.shape[1]
    channels = w_ref.shape[1]
    acts = {}
    bias = b_ref[...]
    group = g_ref[...]
    starts = list(range(0, side, 4))
    for at in starts:
        rows = min(4, side - at)
        total = None
        for ky in range(3):
            part = jnp.dot(
                x_ref[(at + ky) * slab : (at + ky + rows) * slab, :],
                w_ref[ky * depth : (ky + 1) * depth, :],
                preferred_element_type=jnp.float32,
            )
            total = part if total is None else total + part
        total = total + bias
        pre_ref[at * slab : (at + rows) * slab, :] = total
        act = total * phi_cdf(total)
        for row in range(rows):
            acts[at + row] = act[row * slab : (row + 1) * slab, :]
        for p in range(pool):
            if not (at <= 2 * p + 2 < at + rows):
                continue
            column = acts[2 * p] + acts[2 * p + 1] + acts[2 * p + 2]
            cells = window_sum(q_ref, column)
            for q in range(pool):
                kept = jnp.where(max(p, q) + group < pool, 1.0 / 9.0, 0.0)
                lanes = (p * pool + q) * channels
                pooled_ref[:, lanes : lanes + channels] = (
                    cells[q * images : (q + 1) * images, :] * kept
                ).astype(pooled_ref.dtype)


def conv_slope(side, pool, images, dp_ref, pre_ref, q_ref, g_ref, d_ref, bias_ref):
    slab = images * WIDTH
    channels = pre_ref.shape[1]
    group = g_ref[...]
    spread = []
    for p in range(pool):
        cells = []
        for q in range(pool):
            kept = jnp.where(max(p, q) + group < pool, 1.0 / 9.0, 0.0)
            lanes = (p * pool + q) * channels
            cells.append(dp_ref[:, lanes : lanes + channels] * kept)
        spread.append(window_sum(q_ref, jnp.concatenate(cells, axis=0)))
    total = jnp.zeros((8, channels), jnp.float32)
    for y in range(side):
        act = None
        for p in range(pool):
            if 2 * p <= y <= 2 * p + 2:
                act = spread[p] if act is None else act + spread[p]
        grad = (act * pre_ref[y * slab : (y + 1) * slab, :]).astype(jnp.bfloat16)
        d_ref[y * slab : (y + 1) * slab, :] = grad
        total = total + jnp.sum(grad.astype(jnp.float32).reshape(-1, 8, channels), axis=0)
    bias_ref[...] = jnp.sum(total, axis=0, keepdims=True)


def slope_kernel(pre_ref, out_ref):
    out_ref[...] = gelu_slope(pre_ref[...])


def kernel_grad(rows, slab, order_ref, xt_ref, d_ref, keep_ref, send_ref, scr_ref):
    depth = xt_ref.shape[0]
    half = keep_ref.shape[-1]
    count = d_ref.shape[0]
    for ky in range(3):
        scr_ref[ky * depth : (ky + 1) * depth, :] = jnp.dot(
            xt_ref[:, ky * slab : ky * slab + count],
            d_ref[...],
            preferred_element_type=jnp.float32,
        ).astype(scr_ref.dtype)
    core = order_ref[keep_ref.shape[0]]
    for j in range(keep_ref.shape[0]):
        at = pl.multiple_of(order_ref[j] * rows, 16)
        block = scr_ref[pl.ds(at, rows), :]
        low, high = block[:, :half], block[:, half:]
        keep_ref[j] = jnp.where(core == 0, low, high).astype(keep_ref.dtype)
        send_ref[j] = jnp.where(core == 0, high, low).astype(send_ref.dtype)


def input_grad_kernel(side, slab, d_ref, w_ref, in_ref, out_ref, pad_ref):
    channels = d_ref.shape[1]
    depth = 3 * channels
    blank = jnp.zeros((slab, depth), pad_ref.dtype)
    pad_ref[0:slab, :] = blank
    pad_ref[(side + 1) * slab :, :] = blank
    for y in range(side):
        wide = d_ref[y * slab : (y + 1) * slab, :].astype(jnp.float32)
        at = (y + 1) * slab
        pad_ref[at : at + slab, 0:channels] = pltpu.roll(wide, 1, 0).astype(pad_ref.dtype)
        pad_ref[at : at + slab, channels : 2 * channels] = wide.astype(pad_ref.dtype)
        pad_ref[at : at + slab, 2 * channels :] = pltpu.roll(wide, slab - 1, 0).astype(
            pad_ref.dtype
        )
    for at in range(0, side, 4):
        rows = min(4, side - at)
        total = None
        for ky in range(3):
            part = jnp.dot(
                pad_ref[(at + ky) * slab : (at + ky + rows) * slab, :],
                w_ref[ky * depth : (ky + 1) * depth, :],
                preferred_element_type=jnp.float32,
            )
            total = part if total is None else total + part
        out_ref[at * slab : (at + rows) * slab, :] = (
            total * in_ref[at * slab : (at + rows) * slab, :]
        ).astype(out_ref.dtype)


def on_device(pairs, planes, *operands):
    (
        conv_input,
        group,
        conv_weight,
        conv_bias,
        stitch_pool,
        fc_weight,
        fc_bias,
        stitch_fc,
        cotangent,
    ) = operands
    chips = 2 * planes
    batch_at, mp_at = lax.axis_index("batch"), lax.axis_index("mp")
    task = batch_at // pairs
    core = mp_at % 2
    y_at = (mp_at // 2) % 2
    z_at = mp_at // 4
    few = conv_input.shape[0]
    images = 2 * few
    side = conv_input.shape[2]
    channels_in = conv_input.shape[4]
    channels = conv_bias.shape[1]
    pool = (side - 3) // 2 + 1
    units = fc_bias.shape[1]
    features = pool * pool * channels
    part = features // 2
    slab = images * WIDTH
    own_rows = conv_weight.shape[1]
    bf16, f32 = jnp.bfloat16, jnp.float32

    def move(value, dx=0, dz=0, dy=0, dc=0):
        links = []
        for b in range(2 * pairs):
            for m in range(4 * planes):
                z, y, c = m // 4, (m // 2) % 2, m % 2
                far_b = (b + pairs * dx) % (2 * pairs)
                far_m = (((z + dz) % planes) * 2 + (y ^ dy)) * 2 + (c ^ dc)
                links.append((b * 4 * planes + m, far_b * 4 * planes + far_m))
        return lax.ppermute(value, BOTH, links)

    def pick(array, at, axis=0):
        return lax.dynamic_index_in_dim(array, at, axis, keepdims=False)

    def ordered(flag, mine, other, axis=0):
        return jnp.where(
            flag == 0,
            jnp.concatenate([mine, other], axis=axis),
            jnp.concatenate([other, mine], axis=axis),
        )

    def turned(blocks):
        blocks = jnp.where(y_at == 0, blocks, blocks[:, ::-1])
        return jnp.roll(blocks[::-1], z_at + 1, axis=0)

    shifts = []
    for near in range(1, planes // 2 + 1):
        shifts.extend(sorted({near, planes - near}))

    def gather_chips(block):
        rows = [[block, move(block, dy=1)]] + [None] * (planes - 1)
        here = {k: move(block, dz=k) for k in shifts}
        for k in shifts:
            rows[k] = [here[k], move(here[k], dy=1)]
        return [piece for pair in rows for piece in pair]

    def scatter_chips(blocks):
        total = None
        sums = {}
        for k in shifts[::-1] + [0]:
            sums[k] = blocks[2 * k].astype(f32) + move(blocks[2 * k + 1].astype(bf16), dy=1).astype(f32)
        total = sums[0]
        for k in shifts[::-1]:
            total = total + move(sums[k].astype(bf16), dz=-k).astype(f32)
        return total

    weight_blocks = gather_chips(pick(conv_weight, task))
    received = move(pick(conv_input, 1 - task, 1), dx=1)
    group_far = move(group, dx=1)
    weight_blocks = jnp.stack(weight_blocks)
    weight_far = move(weight_blocks, dc=1)
    groups = ordered(task, group, group_far)
    pictures = ordered(task, pick(conv_input, task, 1), received)
    limits = side - 2 * groups
    coords = jnp.arange(side, dtype=jnp.int32)
    inside = (coords[:, None, None] < limits[None, :, None]) & (
        coords[None, None, :] < limits[None, :, None]
    )
    pictures = jnp.transpose(pictures, (1, 0, 2, 3)) * inside.astype(bf16)[..., None]
    stacked = jnp.concatenate(
        [
            lax.pad(
                pictures,
                jnp.zeros((), bf16),
                ((1, 1, 0), (0, 0, 0), (1 - kx, WIDTH - side - 1 + kx, 0), (0, 0, 0)),
            )
            for kx in range(3)
        ],
        axis=-1,
    ).reshape((side + 2) * slab, 3 * channels_in)
    stacked_t = stacked.T
    kernel = ordered(core, weight_blocks, weight_far, axis=1)
    kernel = turned(kernel.reshape(planes, 2, 2 * own_rows, channels)).reshape(-1, channels)
    group_rows = jnp.broadcast_to(groups[:, None], (images, channels))
    window = np.zeros((pool * images, slab), np.float32)
    for q in range(pool):
        for n in range(images):
            window[q * images + n, n * WIDTH + 2 * q : n * WIDTH + 2 * q + 3] = 1.0
    window_t = jnp.asarray(window.T, bf16)
    window = jnp.asarray(window, bf16)
    bias_row = pick(conv_bias, task)[None]
    conv_pre, pooled = kernel_call(
        functools.partial(conv_forward, side, pool, images),
        (
            jax.ShapeDtypeStruct((side * slab, channels), f32),
            jax.ShapeDtypeStruct((images, features), bf16),
        ),
        5,
    )(stacked, kernel, bias_row, window, group_rows)

    pooled_halves = pooled.reshape(images, 2, part)
    pooled_mine = pick(pooled_halves, core, 1)
    pooled_other = pick(pooled_halves, 1 - core, 1)
    pooled_x = move(pooled_mine, dx=1)
    pooled_xc = move(pooled_other, dx=1, dc=1)
    pooled_c = move(pooled_other, dc=1)
    pooled_own = ordered(core, pooled_mine, pooled_c)
    pooled_far = ordered(core, pooled_x, pooled_xc)
    stitch = jnp.where(task == 0, stitch_pool, stitch_pool[::-1, ::-1])

    def spread(weights, value):
        rows = value.shape[0]
        return value.reshape(rows, -1, channels).astype(f32) * weights

    block = (spread(stitch[0, 0], pooled_own) + spread(stitch[0, 1], pooled_far)).astype(bf16)
    block = block.reshape(2 * images, part)
    rows_all = chips * 2 * images
    gathered = jnp.concatenate(gather_chips(block), axis=0)

    slope = kernel_call(
        slope_kernel, jax.ShapeDtypeStruct(conv_pre.shape, f32), 1
    )(conv_pre)

    up = lax.all_to_all(cotangent, "mp", split_axis=2, concat_axis=0, tiled=True)
    up_far = move(up, dx=1)
    up = ordered(
        task,
        up.reshape(planes, 2, 2, 1, few, 2, units),
        up_far.reshape(planes, 2, 2, 1, few, 2, units),
        axis=3,
    )
    up = turned(up).reshape(rows_all, 2, units).astype(f32)

    weight_task = pick(fc_weight, task).reshape(2, part, units)
    fc_mine = pick(weight_task, core)
    fc_far = move(pick(weight_task, 1 - core), dc=1)
    far_term = jnp.dot(gathered, fc_far, preferred_element_type=f32)
    far_back = move(far_term, dc=1)
    fc_pre = jnp.dot(gathered, fc_mine, preferred_element_type=f32) + far_back
    fc_pre = fc_pre + pick(fc_bias, task)[None]
    hidden = fc_pre * phi_cdf(fc_pre)
    mixes = jnp.where(task == 0, stitch_fc, stitch_fc[::-1, ::-1])
    up_mine = jnp.where(task == 0, up[:, 0], up[:, 1])
    up_other = jnp.where(task == 0, up[:, 1], up[:, 0])
    d_hidden = mixes[0, 0] * up_mine + mixes[1, 0] * up_other
    d_fc = (gelu_slope(fc_pre) * d_hidden).astype(bf16)
    d_fc_far = move(d_fc, dc=1)
    d_feat = (
        lax.dot_general(d_fc, fc_mine, (((1,), (1,)), ((), ())), preferred_element_type=f32)
        + lax.dot_general(d_fc_far, fc_far, (((1,), (1,)), ((), ())), preferred_element_type=f32)
    )
    d_feat = d_feat.reshape(chips, 2 * images, part)
    d_block = scatter_chips([d_feat[j] for j in range(chips)])
    d_block_low = d_block.astype(bf16)

    d_mine = pick(d_block_low.reshape(2, images, part), core)
    d_other = pick(d_block_low.reshape(2, images, part), 1 - core)
    d_x = move(d_mine, dx=1)
    d_xc = move(d_other, dx=1, dc=1)
    d_c = move(d_other, dc=1)
    d_pool_mine = spread(stitch[0, 0], pick(d_block.reshape(2, images, part), core)) + spread(stitch[1, 0], d_x)
    d_pool_other = spread(stitch[0, 0], d_c) + spread(stitch[1, 0], d_xc)
    d_pool = ordered(
        core, d_pool_mine.reshape(images, part), d_pool_other.reshape(images, part), axis=1
    )
    d_conv, d_bias = kernel_call(
        functools.partial(conv_slope, side, pool, images),
        (
            jax.ShapeDtypeStruct((side * slab, channels), bf16),
            jax.ShapeDtypeStruct((1, channels), f32),
        ),
        4,
    )(d_pool, slope, window_t, group_rows)

    half = channels // 2
    order = [
        ((z_at - kz) % planes) * 2 + (y_at ^ ky) for kz in range(planes) for ky in range(2)
    ] + [core]
    order = jnp.stack([jnp.asarray(o, jnp.int32) for o in order])
    chip_rows = 2 * own_rows
    keep, send = kernel_call(
        functools.partial(kernel_grad, chip_rows, slab),
        (
            jax.ShapeDtypeStruct((chips, chip_rows, half), f32),
            jax.ShapeDtypeStruct((chips, chip_rows, half), bf16),
        ),
        3,
        (pltpu.VMEM((chips * chip_rows, channels), f32),),
        1,
    )(order, stacked_t, d_conv)
    summed = keep + move(send, dc=1).astype(f32)
    kernel_part = scatter_chips([summed[j] for j in range(chips)]).astype(bf16)
    kernel_part = kernel_part.reshape(2, own_rows, half)
    k_mine = pick(kernel_part, core)
    k_other = pick(kernel_part, 1 - core)
    k_x = move(k_mine, dx=1)
    k_xc = move(k_other, dx=1, dc=1)
    k_c = move(k_other, dc=1)
    kernel_own = ordered(core, k_mine, k_c, axis=1)
    kernel_far = ordered(core, k_x, k_xc, axis=1)
    conv_weight_grad = ordered(task, kernel_own[None], kernel_far[None]).astype(f32)

    kernel_back = jnp.transpose(kernel.reshape(9, channels_in, channels)[::-1], (0, 2, 1))
    kernel_back = kernel_back.reshape(9 * channels, channels_in)
    inside_rows = lax.pad(
        inside.astype(f32), jnp.zeros((), f32), ((0, 0, 0), (0, 0, 0), (0, WIDTH - side, 0))
    ).reshape(side * slab, 1)
    d_pictures = kernel_call(
        functools.partial(input_grad_kernel, side, slab),
        jax.ShapeDtypeStruct((side * slab, channels_in), bf16),
        3,
        (pltpu.VMEM(((side + 2) * slab, 3 * channels), bf16),),
    )(d_conv, kernel_back, inside_rows)
    d_pictures = d_pictures.reshape(side, 2, few, WIDTH, channels_in)[:, :, :, :side]
    d_pictures = jnp.transpose(d_pictures, (1, 2, 0, 3, 4))
    picture_own = pick(d_pictures, task)
    picture_far = move(pick(d_pictures, 1 - task), dx=1)
    input_grad = ordered(task, picture_own[:, None], picture_far[:, None], axis=1)

    cells = hidden.reshape(chips * 2, 2, few, units)
    hidden_here = pick(cells, task, 1)
    hidden_far = move(pick(cells, 1 - task, 1).astype(bf16), dx=1).astype(f32)
    mixed_own = mixes[0, 0] * hidden_here + mixes[0, 1] * hidden_far
    mixed_other = mixes[1, 0] * hidden_here + mixes[1, 1] * hidden_far
    mixed = ordered(
        task, mixed_own[:, :, None].astype(bf16), mixed_other[:, :, None].astype(bf16), axis=2
    )
    mixed = turned(mixed.reshape(planes, 2, 2 * few, 2, units))
    output = lax.all_to_all(
        mixed.reshape(chips * 2 * few, 2, units), "mp", split_axis=0, concat_axis=2, tiled=True
    )

    def both(own, axis=0):
        blank = jnp.zeros_like(own)
        return ordered(task, jnp.expand_dims(own, axis), jnp.expand_dims(blank, axis), axis=axis)

    fc_bias_term = both(jnp.sum(d_fc.astype(f32), axis=0))
    stitch_fc_term = both(jnp.sum(up * hidden[:, None], axis=0), axis=1)
    fc_bias_grad, stitch_fc_grad = lax.psum((fc_bias_term, stitch_fc_term), "batch")
    links = []
    for b in range(2 * pairs):
        for m in range(4 * planes):
            if m % 2 != b // pairs:
                links.append((b * 4 * planes + m, ((b + pairs) % (2 * pairs)) * 4 * planes + m))
    features_x = lax.ppermute(gathered, BOTH, links)
    same = core == task
    feat_c = move(gathered, dc=1)
    features_xc = move(features_x, dc=1)
    feat_own = jnp.where(same, gathered, feat_c)
    feat_far = jnp.where(same, features_x, features_xc)
    d_fc_x = move(d_fc, dx=1)
    terms = []
    for t in range(2):
        feat = jnp.where(task == t, feat_own, feat_far)
        grad = jnp.where(task == t, d_fc, d_fc_x)
        terms.append(
            lax.dot_general(feat, grad, (((0,), (0,)), ((), ())), preferred_element_type=f32)
        )
    fc_weight_grad = jnp.stack(terms)
    if pairs > 1:
        blank = jnp.zeros_like(fc_weight_grad)
        fc_weight_grad = lax.psum_scatter(
            ordered(task, fc_weight_grad, blank, axis=1), "batch", scatter_dimension=1, tiled=True
        )
        mine = pick(conv_weight_grad, task)
        conv_weight_grad = lax.psum(both(mine), "batch")

    d_rows = d_block.reshape(2 * images, -1, channels)
    own_pool = jnp.sum(d_rows * pooled_own.reshape(d_rows.shape).astype(f32), axis=(0, 1))
    far_pool = jnp.sum(d_rows * pooled_far.reshape(d_rows.shape).astype(f32), axis=(0, 1))
    stitch_term = both(ordered(task, own_pool[None], far_pool[None]))
    conv_bias_grad, stitch_pool_grad = lax.psum((both(d_bias[0]), stitch_term), BOTH)
    return (
        output,
        input_grad,
        conv_weight_grad,
        conv_bias_grad,
        stitch_pool_grad,
        fc_weight_grad,
        fc_bias_grad,
        stitch_fc_grad,
    )


def solution(mesh):
    pairs = mesh.shape["batch"] // 2
    planes = mesh.shape["mp"] // 4
    in_specs = (
        P(BOTH, None, None, None, None),
        P(BOTH),
        P(None, "mp", None),
        P(),
        P(),
        P(None, None, "mp"),
        P(None, "mp"),
        P(None, None, "mp"),
        P(BOTH, None, None),
    )
    out_specs = (
        P(BOTH, None, None),
        P(BOTH, None, None, None, None),
        P(None, "mp", None),
        P(),
        P(),
        P(None, "batch", "mp"),
        P(None, "mp"),
        P(None, None, "mp"),
    )
    return jax.shard_map(
        functools.partial(on_device, pairs, planes),
        mesh=mesh,
        in_specs=in_specs,
        out_specs=out_specs,
        check_vma=False,
    )
```

```python
import functools

import jax
import jax.numpy as jnp
import numpy as np
from jax import lax
from jax.experimental import pallas as pl
from jax.experimental.pallas import tpu as pltpu
from jax.sharding import PartitionSpec as P

BOTH = ("batch", "mp")
WIDTH = 16
EXTRA = 16
ROOT_HALF = 0.7071067811865476
ROOT_TWO_PI_INV = 0.3989422804014327
VMEM = pl.BlockSpec(memory_space=pltpu.VMEM)
SMEM = pl.BlockSpec(memory_space=pltpu.SMEM)
MIB = 1024 * 1024
bf16, f32 = jnp.bfloat16, jnp.float32
shape_of = jax.ShapeDtypeStruct


def call(body, out_shape, operands, scratch=(), scalars=0, mib=24):
    return pl.pallas_call(
        body,
        out_shape=out_shape,
        in_specs=[SMEM] * scalars + [VMEM] * (len(operands) - scalars),
        out_specs=jax.tree.map(lambda _: VMEM, out_shape),
        scratch_shapes=scratch,
        compiler_params=pltpu.CompilerParams(vmem_limit_bytes=mib * MIB),
    )(*operands)


class Place:
    def __init__(self, pairs, planes):
        batch_at, mp_at = lax.axis_index("batch"), lax.axis_index("mp")
        self.planes = planes
        self.task = lax.div(batch_at, pairs)
        self.core = lax.rem(mp_at, 2)
        self.y = lax.rem(lax.div(mp_at, 2), 2)
        self.z = lax.div(mp_at, 4)

    def chip(self, kz, ky):
        y = self.y if ky == 0 else 1 - self.y
        return lax.rem(self.z + (self.planes - kz), self.planes) * 2 + y


def phi_cdf(value):
    return 0.5 * (1.0 + lax.erf(value * ROOT_HALF))


def gelu_slope(value):
    return phi_cdf(value) + value * ROOT_TWO_PI_INV * jnp.exp(-0.5 * value * value)


def split_high_low(value):
    high = value.astype(bf16)
    return high, (value - high.astype(f32)).astype(bf16)


def window_sum(q_ref, value):
    high, low = split_high_low(value)
    return jnp.dot(q_ref[...], high, preferred_element_type=f32) + jnp.dot(
        q_ref[...], low, preferred_element_type=f32
    )


def split_inputs(place, g_ref, x_ref, cot_ref, own_ref, far_ref, out_ref):
    at = place()
    few, _, side, _, depth = x_ref.shape
    units = out_ref.shape[2]
    own_ref[...] = jnp.zeros_like(own_ref)
    far_ref[...] = jnp.zeros_like(far_ref)
    columns = lax.broadcasted_iota(jnp.int32, (side, depth), 0)
    for n in range(few):
        limit = side - 2 * g_ref[n]
        for y in range(side):
            reach = jnp.where(y < limit, limit, 0)
            mask = jnp.where(columns < reach, 1.0, 0.0).astype(bf16)
            own_ref[y, n, 0:side, :] = x_ref[n, at.task, y] * mask
            far_ref[y, n, 0:side, :] = x_ref[n, 1 - at.task, y] * mask
    for i in range(few):
        for t in range(2):
            pass
    value = cot_ref[...].astype(f32)
    rows = jnp.concatenate([value[i, t : t + 1] for t in range(2) for i in range(few)], axis=0)
    for m in range(out_ref.shape[0]):
        out_ref[m] = rows[:, m * units : (m + 1) * units].astype(bf16)


def widen(place, own_ref, far_ref, x3_ref, xt_ref):
    at = place()
    side, few, _, depth = own_ref.shape
    block = few * WIDTH
    slab = 2 * block
    for edge in (0, side + 1):
        x3_ref[edge * slab : (edge + 1) * slab, :] = jnp.zeros((slab, 3 * depth), bf16)
        xt_ref[:, edge * slab : (edge + 1) * slab] = jnp.zeros((3 * depth, slab), bf16)
    for y in range(side):
        own = own_ref[y].reshape(block, depth).astype(f32)
        far = far_ref[y].reshape(block, depth).astype(f32)
        first = at.task == 0
        wide = jnp.concatenate(
            [jnp.where(first, own, far), jnp.where(first, far, own)], axis=0
        )
        rows = slice((y + 1) * slab, (y + 2) * slab)
        turned = wide.T
        for kx in range(3):
            lanes = slice(kx * depth, (kx + 1) * depth)
            shift = (1 - kx) % slab
            x3_ref[rows, lanes] = (pltpu.roll(wide, shift, 0) if shift else wide).astype(bf16)
            xt_ref[lanes, rows] = (pltpu.roll(turned, shift, 1) if shift else turned).astype(bf16)


def group_column(at, own_ref, far_ref, images, channels):
    few = images // 2
    rows = lax.broadcasted_iota(jnp.int32, (images, channels), 0)
    value = jnp.zeros((images, channels), jnp.int32)
    for n in range(images):
        own, far = own_ref[n % few], far_ref[n % few]
        value = jnp.where(rows == n, jnp.where(at.task == n // few, own, far), value)
    return value


def conv_forward(place, side, pool, images, *refs):
    own_ref, far_ref, x_ref, b_ref, q_ref = refs[:5]
    blocks = refs[5:-3]
    pre_ref, pooled_ref, w_ref = refs[-3:]
    at = place()
    chips = len(blocks) // 2
    rows, half = blocks[0].shape
    here = pl.ds(pl.multiple_of(at.core * half, half), half)
    there = pl.ds(pl.multiple_of((1 - at.core) * half, half), half)
    for j in range(chips):
        to = pl.ds(pl.multiple_of(at.chip(j // 2, j % 2) * rows, 16), rows)
        w_ref[to, here] = blocks[j][...]
        w_ref[to, there] = blocks[chips + j][...]
    slab = images * WIDTH
    depth = x_ref.shape[1]
    channels = w_ref.shape[1]
    acts = {}
    bias = jnp.where(at.task == 0, b_ref[0:1, :], b_ref[1:2, :])
    group = group_column(at, own_ref, far_ref, images, channels)
    for start in range(0, side, 4):
        rows = min(4, side - start)
        total = None
        for ky in range(3):
            part = jnp.dot(
                x_ref[(start + ky) * slab : (start + ky + rows) * slab, :],
                w_ref[ky * depth : (ky + 1) * depth, :],
                preferred_element_type=f32,
            )
            total = part if total is None else total + part
        total = total + bias
        pre_ref[start * slab : (start + rows) * slab, :] = total
        act = total * phi_cdf(total)
        for row in range(rows):
            acts[start + row] = act[row * slab : (row + 1) * slab, :]
        for p in range(pool):
            if not (start <= 2 * p + 2 < start + rows):
                continue
            cells = window_sum(q_ref, acts[2 * p] + acts[2 * p + 1] + acts[2 * p + 2])
            side_at = jnp.where(at.core == (2 * p) // pool, 0, 1)
            for q in range(pool):
                kept = jnp.where(max(p, q) + group < pool, 1.0 / 9.0, 0.0)
                lanes = ((p % (pool // 2)) * pool + q) * channels
                pooled_ref[side_at, :, lanes : lanes + channels] = (
                    cells[q * images : (q + 1) * images, :] * kept
                ).astype(bf16)


def slope_and_back(pre_ref, w_ref, slope_ref, back_ref):
    slope_ref[...] = gelu_slope(pre_ref[...])
    taps = 9
    depth = w_ref.shape[0] // taps
    channels = w_ref.shape[1]
    for tap in range(taps):
        far = taps - 1 - tap
        back_ref[tap * channels : (tap + 1) * channels, :] = (
            w_ref[far * depth : (far + 1) * depth, :].astype(f32).T.astype(bf16)
        )


def cot_rows(place, own_ref, far_ref, up_ref):
    at = place()
    first = at.task == 0
    rows = own_ref.shape[1]
    few = rows // 2
    low_rows = lax.broadcasted_iota(jnp.int32, own_ref.shape[1:], 0) < few
    for j in range(own_ref.shape[0] // 2):
        chip = at.chip(j // 2, j % 2)
        for c in range(2):
            own = own_ref[2 * chip + c].astype(f32)
            far = far_ref[2 * chip + c].astype(f32)
            low = jnp.where(first, own, far)
            high = jnp.where(first, far, own)
            zero = jnp.where(low_rows, low, pltpu.roll(high, few, 0))
            one = jnp.where(low_rows, pltpu.roll(low, few, 0), high)
            here = slice((2 * j + c) * rows, (2 * j + c + 1) * rows)
            up_ref[0, here, :] = jnp.where(first, zero, one)
            up_ref[1, here, :] = jnp.where(first, one, zero)


def fc_far(*refs):
    blocks = refs[:-3]
    w_ref, all_ref, out_ref = refs[-3:]
    rows = blocks[0].shape[0]
    for j, block in enumerate(blocks):
        all_ref[j * rows : (j + 1) * rows, :] = block[...]
    out_ref[...] = jnp.dot(all_ref[...], w_ref[...], preferred_element_type=f32)


def fc_own(x_ref, w_ref, out_ref):
    out_ref[...] = jnp.dot(x_ref[...], w_ref[...], preferred_element_type=f32)


def fc_middle(place, own_ref, back_ref, bias_ref, mix_ref, up_ref, d_ref, hidden_ref, sums_ref):
    at = place()
    first = at.task == 0
    bias = jnp.where(first, bias_ref[0:1, :], bias_ref[1:2, :])
    pre = own_ref[...] + back_ref[...] + bias
    cdf = phi_cdf(pre)
    hidden = pre * cdf
    hidden_ref[...] = hidden
    slope = cdf + pre * ROOT_TWO_PI_INV * jnp.exp(-0.5 * pre * pre)

    def mix(t, u):
        row = mix_ref[t]
        return jnp.where(u == 0, row[0:1, :], row[1:2, :])

    mine, other = up_ref[0], up_ref[1]
    d_hidden = mix(at.task, at.task) * mine + mix(1 - at.task, at.task) * other
    d_fc = (slope * d_hidden).astype(bf16)
    d_ref[...] = d_fc
    by_mine = jnp.sum(mine * hidden, axis=0, keepdims=True)
    by_other = jnp.sum(other * hidden, axis=0, keepdims=True)
    sums_ref[...] = jnp.concatenate(
        [
            jnp.sum(d_fc.astype(f32), axis=0, keepdims=True),
            jnp.where(first, by_mine, by_other),
            jnp.where(first, by_other, by_mine),
            jnp.zeros((5, by_mine.shape[1]), f32),
        ],
        axis=0,
    )


def fc_back(d_ref, far_ref, w_ref, wf_ref, *outs):
    chips = len(outs)
    rows = outs[0].shape[0]
    contract = (((1,), (1,)), ((), ()))
    total = lax.dot_general(d_ref[...], w_ref[...], contract, preferred_element_type=f32)
    total += lax.dot_general(far_ref[...], wf_ref[...], contract, preferred_element_type=f32)
    for j, out in enumerate(outs):
        out[...] = total[j * rows : (j + 1) * rows, :].astype(out.dtype)


def add_rows(keep_ref, got_ref, *outs):
    total = keep_ref[...] + got_ref[...].astype(f32)
    for out in outs:
        out[...] = total.astype(out.dtype)


def block_total(place, keep_ref, *refs):
    at = place()
    total_ref, mine_ref, mine_low_ref, other_ref = refs[-4:]
    total = keep_ref[...]
    for ref in refs[:-4]:
        total = total + ref[...].astype(f32)
    total_ref[...] = total
    images = mine_ref.shape[0]
    low, high = total[:images], total[images:]
    mine = jnp.where(at.core == 0, low, high)
    mine_ref[...] = mine
    mine_low_ref[...] = mine.astype(bf16)
    other_ref[...] = jnp.where(at.core == 0, high, low).astype(bf16)


def stitch_terms(total_ref, own_ref, far_ref, out_ref):
    channels = out_ref.shape[1]
    own = far = None
    for cell in range(total_ref.shape[1] // channels):
        lanes = slice(cell * channels, (cell + 1) * channels)
        grad = total_ref[:, lanes]
        one = grad * own_ref[:, lanes].astype(f32)
        two = grad * far_ref[:, lanes].astype(f32)
        own = one if own is None else own + one
        far = two if far is None else far + two
    out_ref[...] = jnp.concatenate(
        [
            jnp.sum(own, axis=0, keepdims=True),
            jnp.sum(far, axis=0, keepdims=True),
            jnp.zeros((6, channels), f32),
        ],
        axis=0,
    )


def conv_slope(place, side, pool, images, *refs):
    (og_ref, fg_ref, mine_ref, c_ref, x_ref, xc_ref, st_ref, slope_ref, q_ref) = refs[:9]
    d_ref, bias_ref = refs[9:]
    at = place()
    slab = images * WIDTH
    channels = slope_ref.shape[1]
    group = group_column(at, og_ref, fg_ref, images, channels)

    def mix(t, u):
        row = st_ref[t]
        return jnp.where(u == 0, row[0:1, :], row[1:2, :])

    near, far = mix(at.task, at.task), mix(1 - at.task, at.task)
    spread = []
    for p in range(pool):
        mine_here = at.core == (2 * p) // pool
        cells = []
        for q in range(pool):
            lanes = ((p % (pool // 2)) * pool + q) * channels
            lanes = slice(lanes, lanes + channels)
            kept = jnp.where(max(p, q) + group < pool, 1.0 / 9.0, 0.0)
            one = near * mine_ref[:, lanes] + far * x_ref[:, lanes].astype(f32)
            two = near * c_ref[:, lanes].astype(f32) + far * xc_ref[:, lanes].astype(f32)
            cells.append(jnp.where(mine_here, one, two) * kept)
        spread.append(window_sum(q_ref, jnp.concatenate(cells, axis=0)))
    total = jnp.zeros((8, channels), f32)
    for y in range(side):
        act = None
        for p in range(pool):
            if 2 * p <= y <= 2 * p + 2:
                act = spread[p] if act is None else act + spread[p]
        grad = (act * slope_ref[y * slab : (y + 1) * slab, :]).astype(bf16)
        d_ref[y * slab : (y + 1) * slab, :] = grad
        total = total + jnp.sum(grad.astype(f32).reshape(-1, 8, channels), axis=0)
    bias_ref[...] = jnp.sum(total, axis=0, keepdims=True)


def kernel_grad(place, slab, xt_ref, d_ref, bias_ref, st_ref, *refs):
    keep1_ref, keep0_ref, send1_ref, send0_ref, scr_ref = refs
    at = place()
    depth = xt_ref.shape[0]
    planes, full, half = keep1_ref.shape
    rows = full - EXTRA
    count = d_ref.shape[0]
    for ky in range(3):
        scr_ref[ky * depth : (ky + 1) * depth, :] = jnp.dot(
            xt_ref[:, ky * slab : ky * slab + count], d_ref[...], preferred_element_type=f32
        )
    small = jnp.concatenate([bias_ref[...], st_ref[0:2, :]], axis=0)
    small = jnp.concatenate(
        [small[:, :half], jnp.zeros((1, half), f32), small[:, half:], jnp.zeros((1, half), f32)],
        axis=0,
    )
    high, low = split_high_low(small)
    extra = jnp.concatenate([high.astype(f32), low.astype(f32)], axis=0)
    here = pl.ds(pl.multiple_of(at.core * half, half), half)
    there = pl.ds(pl.multiple_of((1 - at.core) * half, half), half)
    for ky, keep_ref, send_ref in ((1, keep1_ref, send1_ref), (0, keep0_ref, send0_ref)):
        for kz in range(planes):
            to = pl.ds(pl.multiple_of(at.chip(kz, ky) * rows, 16), rows)
            keep_ref[kz, 0:rows, :] = scr_ref[to, here]
            send_ref[kz, 0:rows, :] = scr_ref[to, there].astype(bf16)
            keep_ref[kz, rows:full, :] = extra
            send_ref[kz, rows:full, :] = extra.astype(bf16)


def folded(extra):
    value = extra[:8] + extra[8:]
    high, low = split_high_low(value)
    return jnp.concatenate([high.astype(f32), low.astype(f32)], axis=0)


def sum_pieces(keep_ref, got_ref, *outs):
    rows = keep_ref.shape[1] - EXTRA
    for kz, out in enumerate(outs):
        total = keep_ref[kz] + got_ref[kz].astype(f32)
        out[0:rows, :] = total[:rows].astype(out.dtype)
        out[rows:, :] = folded(total[rows:]).astype(out.dtype)


def sum_pair(keep_ref, got_ref, out_ref):
    rows = keep_ref.shape[0] - EXTRA
    total = keep_ref[...] + got_ref[...].astype(f32)
    out_ref[0:rows, :] = total[:rows].astype(out_ref.dtype)
    out_ref[rows:, :] = folded(total[rows:]).astype(out_ref.dtype)


def kernel_total(place, *refs):
    parts, (mine_ref, other_ref, scr_ref, small_ref) = refs[:-4], refs[-4:]
    at = place()
    full, half = parts[0].shape
    rows = full - EXTRA
    total = None
    for k, part in enumerate(parts):
        value = part[...].astype(f32)
        total = value[:rows] if total is None else total + value[:rows]
        small_ref[k] = value[rows : rows + 8] + value[rows + 8 :]
    scr_ref[...] = total
    small = None
    for z in range(len(parts)):
        piece = small_ref[lax.rem(at.z + (len(parts) - z), len(parts))]
        small = piece if small is None else small + piece
    high, low = split_high_low(small)
    tail = jnp.zeros((mine_ref.shape[0] - rows // 2 - EXTRA, half), f32)
    for ref, c in ((mine_ref, at.core), (other_ref, 1 - at.core)):
        piece = scr_ref[pl.ds(pl.multiple_of(c * (rows // 2), 8), rows // 2), :]
        ref[...] = jnp.concatenate(
            [high.astype(f32), low.astype(f32), piece, tail][: 4 if tail.shape[0] else 3], axis=0
        ).astype(bf16)


def kernel_finish(place, mine_ref, c_ref, x_ref, xc_ref, grad_ref, bias_ref, stitch_ref):
    at = place()
    rows = grad_ref.shape[1]
    half = grad_ref.shape[2] // 2
    first = at.task == 0
    low_core = at.core == 0

    def lanes(one, two):
        return jnp.concatenate(
            [jnp.where(low_core, one, two), jnp.where(low_core, two, one)], axis=1
        )

    own = lanes(mine_ref[...].astype(f32), c_ref[...].astype(f32))
    far = lanes(x_ref[...].astype(f32), xc_ref[...].astype(f32))
    grad_ref[0] = jnp.where(first, own, far)[EXTRA : EXTRA + rows, :]
    grad_ref[1] = jnp.where(first, far, own)[EXTRA : EXTRA + rows, :]

    def small(ref):
        value = ref[...].astype(f32)
        value = value[0:8] + value[8:16]
        return jnp.concatenate([value[0:4], value[4:8]], axis=1)

    own, far = small(mine_ref), small(x_ref)
    bias_ref[0:1, :] = jnp.where(first, own, far)[0:1, :]
    bias_ref[1:2, :] = jnp.where(first, far, own)[0:1, :]
    own_pair = jnp.where(first, own[1:3], jnp.concatenate([own[2:3], own[1:2]], axis=0))
    far_pair = jnp.where(first, jnp.concatenate([far[2:3], far[1:2]], axis=0), far[1:3])
    stitch_ref[0] = jnp.where(first, own_pair, far_pair)
    stitch_ref[1] = jnp.where(first, far_pair, own_pair)


def picture_grad(place, side, slab, d_ref, w_ref, own_ref, far_ref, pad_ref):
    at = place()
    channels = d_ref.shape[1]
    depth = 3 * channels
    block = slab // 2
    blank = jnp.zeros((slab, depth), bf16)
    pad_ref[0:slab, :] = blank
    pad_ref[(side + 1) * slab :, :] = blank
    for y in range(side):
        wide = d_ref[y * slab : (y + 1) * slab, :].astype(f32)
        rows = slice((y + 1) * slab, (y + 2) * slab)
        pad_ref[rows, 0:channels] = pltpu.roll(wide, 1, 0).astype(bf16)
        pad_ref[rows, channels : 2 * channels] = wide.astype(bf16)
        pad_ref[rows, 2 * channels :] = pltpu.roll(wide, slab - 1, 0).astype(bf16)
    for start in range(0, side, 4):
        rows = min(4, side - start)
        total = None
        for ky in range(3):
            part = jnp.dot(
                pad_ref[(start + ky) * slab : (start + ky + rows) * slab, :],
                w_ref[ky * depth : (ky + 1) * depth, :],
                preferred_element_type=f32,
            )
            total = part if total is None else total + part
        for row in range(rows):
            zero = total[row * slab : row * slab + block]
            one = total[row * slab + block : (row + 1) * slab]
            own = jnp.where(at.task == 0, zero, one).astype(bf16)
            far = jnp.where(at.task == 0, one, zero).astype(bf16)
            own_ref[start + row] = own.reshape(own_ref.shape[1:])
            far_ref[start + row] = far.reshape(far_ref.shape[1:])


def picture_finish(place, g_ref, own_ref, far_ref, out_ref):
    at = place()
    side, few, _, depth = own_ref.shape
    columns = lax.broadcasted_iota(jnp.int32, (side, depth), 0)
    for n in range(few):
        limit = side - 2 * g_ref[n]
        for y in range(side):
            reach = jnp.where(y < limit, limit, 0)
            mask = jnp.where(columns < reach, 1.0, 0.0).astype(bf16)
            out_ref[n, at.task, y] = own_ref[y, n, 0:side, :] * mask
            out_ref[n, 1 - at.task, y] = far_ref[y, n, 0:side, :] * mask


def fc_grad(place, own_ref, oc_ref, x_ref, xc_ref, d_ref, dx_ref, out_ref):
    at = place()
    same = at.core == at.task
    own = jnp.where(same, own_ref[...], oc_ref[...])
    far = jnp.where(same, x_ref[...], xc_ref[...])
    contract = (((0,), (0,)), ((), ()))
    out_ref[at.task] = lax.dot_general(own, d_ref[...], contract, preferred_element_type=f32)
    out_ref[1 - at.task] = lax.dot_general(far, dx_ref[...], contract, preferred_element_type=f32)


def on_device(pairs, planes, *operands):
    (
        conv_input,
        group,
        conv_weight,
        conv_bias,
        stitch_pool,
        fc_weight,
        fc_bias,
        stitch_fc,
        cotangent,
    ) = operands
    chips = 2 * planes
    at = Place(pairs, planes)
    place = functools.partial(Place, pairs, planes)
    task, core = at.task, at.core
    few = conv_input.shape[0]
    images = 2 * few
    side = conv_input.shape[2]
    channels_in = conv_input.shape[4]
    channels = conv_bias.shape[1]
    pool = (side - 3) // 2 + 1
    units = fc_bias.shape[1]
    features = pool * pool * channels
    part = features // 2
    slab = images * WIDTH
    own_rows = conv_weight.shape[1]
    chip_rows = 2 * own_rows
    half = channels // 2

    def links(where):
        pairs_of = []
        for b in range(2 * pairs):
            for m in range(4 * planes):
                to = where(b, m // 4, (m // 2) % 2, m % 2)
                if to is not None:
                    far_b, z, y, c = to
                    far_m = ((z % planes) * 2 + y) * 2 + c
                    pairs_of.append((b * 4 * planes + m, far_b * 4 * planes + far_m))
        return pairs_of

    def move(value, dx=0, dz=0, dy=0, dc=0):
        where = lambda b, z, y, c: ((b + pairs * dx) % (2 * pairs), z + dz, y ^ dy, c ^ dc)
        return lax.ppermute(value, BOTH, links(where))

    def pick(array, index, axis=0):
        return lax.dynamic_index_in_dim(array, index, axis, keepdims=False)

    def ordered(flag, mine, other, axis=0):
        return jnp.where(
            flag == 0,
            jnp.concatenate([mine, other], axis=axis),
            jnp.concatenate([other, mine], axis=axis),
        )

    def after(value, *others):
        return lax.optimization_barrier((value, *others))[0]

    shifts = []
    for near in range(1, planes // 2 + 1):
        shifts.extend(sorted({near, planes - near}))

    def gather_chips(block):
        rows = [[block, move(block, dy=1)]] + [None] * (planes - 1)
        here = {k: move(block, dz=k) for k in shifts}
        for k in shifts:
            rows[k] = [here[k], move(here[k], dy=1)]
        return [piece for pair in rows for piece in pair]

    weight = pick(conv_weight, task)
    weight_other = move(lax.dynamic_slice_in_dim(weight, (1 - core) * half, half, 1), dc=1)
    weight_mine = lax.dynamic_slice_in_dim(weight, core * half, half, 1)
    weight_block = ordered(core, weight_mine, weight_other)
    weight_blocks = gather_chips(weight_block)
    weight_far = [move(block, dc=1) for block in weight_blocks]

    wide = (side, few, WIDTH, channels_in)
    picture_own, picture_send, cot_send = call(
        functools.partial(split_inputs, place),
        (
            shape_of(wide, bf16),
            shape_of(wide, bf16),
            shape_of((4 * planes, images, units), bf16),
        ),
        (group, conv_input, cotangent),
        scalars=1,
    )
    picture_far = move(picture_send, dx=1)
    group_far = move(group, dx=1)
    stacked, stacked_t = call(
        functools.partial(widen, place),
        (
            shape_of(((side + 2) * slab, 3 * channels_in), bf16),
            shape_of((3 * channels_in, (side + 2) * slab), bf16),
        ),
        (picture_own, picture_far),
    )

    fc_parts = fc_weight.reshape(4, part, units)
    fc_mine = pick(fc_parts, 2 * task + core)
    fc_other = move(pick(fc_parts, 2 * task + 1 - core), dc=1)

    cot_own = lax.all_to_all(cot_send, "mp", split_axis=0, concat_axis=0, tiled=True)
    cot_far = move(cot_own, dx=1)
    rows_all = chips * 2 * images
    up = call(
        functools.partial(cot_rows, place), shape_of((2, rows_all, units), f32), (cot_own, cot_far)
    )

    window = np.zeros((pool * images, slab), np.float32)
    for q in range(pool):
        for n in range(images):
            window[q * images + n, n * WIDTH + 2 * q : n * WIDTH + 2 * q + 3] = 1.0
    window_t = jnp.asarray(window.T, bf16)
    window = jnp.asarray(window, bf16)
    stacked = after(stacked, stacked_t, up, fc_mine)
    conv_pre, pooled, kernel = call(
        functools.partial(conv_forward, place, side, pool, images),
        (
            shape_of((side * slab, channels), f32),
            shape_of((2, images, part), bf16),
            shape_of((chips * chip_rows, channels), bf16),
        ),
        (group, group_far, stacked, conv_bias, window, *weight_blocks, *weight_far),
        scalars=2,
        mib=32,
    )

    pooled_mine, pooled_other = pooled[0], pooled[1]
    pooled_x = move(pooled_mine, dx=1)
    pooled_xc = move(pooled_other, dx=1, dc=1)
    pooled_c = move(pooled_other, dc=1)
    pooled_own = ordered(core, pooled_mine, pooled_c)
    pooled_far = ordered(core, pooled_x, pooled_xc)
    stitch = jnp.where(task == 0, stitch_pool, stitch_pool[::-1, ::-1])

    def spread(weights, value):
        return value.reshape(2 * images, -1, channels).astype(f32) * weights

    block = (spread(stitch[0, 0], pooled_own) + spread(stitch[0, 1], pooled_far)).astype(bf16)
    blocks = gather_chips(block.reshape(2 * images, part))

    slope, kernel_back = call(
        slope_and_back,
        (
            shape_of(conv_pre.shape, f32),
            shape_of((9 * channels, channels_in), bf16),
        ),
        (after(conv_pre, blocks[1]), kernel),
    )

    gathered, far_term = call(
        fc_far,
        (shape_of((rows_all, part), bf16), shape_of((rows_all, units), f32)),
        (*blocks, fc_other),
    )
    far_back = move(far_term, dc=1)
    own_term = call(fc_own, shape_of((rows_all, units), f32), (gathered, fc_mine))
    d_fc, hidden, fc_sums = call(
        functools.partial(fc_middle, place),
        (
            shape_of((rows_all, units), bf16),
            shape_of((rows_all, units), f32),
            shape_of((8, units), f32),
        ),
        (own_term, far_back, fc_bias, stitch_fc, up),
    )
    d_fc_far = move(d_fc, dc=1)
    piece = (2 * images, part)
    outs = call(
        fc_back,
        tuple(shape_of(piece, bf16 if j % 2 else f32) for j in range(chips)),
        (d_fc, d_fc_far, fc_mine, fc_other),
    )
    kept, sent = outs[0::2], outs[1::2]

    order = shifts[::-1] + [0]
    arrived = {k: move(sent[k], dy=1) for k in order}
    passed = {}
    for k in order[:-1]:
        low = call(add_rows, (shape_of(piece, bf16),), (kept[k], arrived[k]))[0]
        passed[k] = move(low, dz=-k)
    d_total, d_mine, d_mine_low, d_other = call(
        functools.partial(block_total, place),
        (
            shape_of(piece, f32),
            shape_of((images, part), f32),
            shape_of((images, part), bf16),
            shape_of((images, part), bf16),
        ),
        (kept[0], arrived[0], *[passed[k] for k in order[:-1]]),
    )

    d_x = move(d_mine_low, dx=1)
    d_xc = move(d_other, dx=1, dc=1)
    d_c = move(d_other, dc=1)
    stitch_sums = call(
        stitch_terms, shape_of((8, channels), f32), (d_total, pooled_own, pooled_far)
    )
    d_conv, d_bias = call(
        functools.partial(conv_slope, place, side, pool, images),
        (shape_of((side * slab, channels), bf16), shape_of((1, channels), f32)),
        (group, group_far, d_mine, d_c, d_x, d_xc, stitch_pool, slope, window_t),
        scalars=2,
    )

    full = chip_rows + EXTRA
    stack = (planes, full, half)
    keep1, keep0, send1, send0 = call(
        functools.partial(kernel_grad, place, slab),
        (shape_of(stack, f32), shape_of(stack, f32), shape_of(stack, bf16), shape_of(stack, bf16)),
        (stacked_t, d_conv, d_bias, stitch_sums),
        (pltpu.VMEM((chips * chip_rows, channels), f32),),
        mib=32,
    )
    got1, got0 = move(send1, dc=1), move(send0, dc=1)
    flat = (full, half)
    sent = call(sum_pieces, tuple(shape_of(flat, bf16) for _ in range(planes)), (keep1, got1))
    arrived = {k: move(sent[k], dy=1) for k in order}
    kept = call(sum_pieces, tuple(shape_of(flat, f32) for _ in range(planes)), (keep0, got0))
    parts = {}
    for k in order[:-1]:
        parts[k] = move(call(sum_pair, shape_of(flat, bf16), (kept[k], arrived[k])), dz=-k)
    parts[0] = call(sum_pair, shape_of(flat, f32), (kept[0], arrived[0]))
    tall = -(-(own_rows + EXTRA) // 16) * 16
    k_mine, k_other = call(
        functools.partial(kernel_total, place),
        (shape_of((tall, half), bf16), shape_of((tall, half), bf16)),
        tuple(parts[(planes - k) % planes] for k in range(planes)),
        (pltpu.VMEM((chip_rows, half), f32), pltpu.VMEM((planes, 8, half), f32)),
    )
    k_x = move(k_mine, dx=1)
    k_xc = move(k_other, dx=1, dc=1)
    k_c = move(k_other, dc=1)
    conv_weight_grad, conv_bias_grad, stitch_pool_grad = call(
        functools.partial(kernel_finish, place),
        (
            shape_of((2, own_rows, channels), f32),
            shape_of((2, channels), f32),
            shape_of((2, 2, channels), f32),
        ),
        (k_mine, k_c, k_x, k_xc),
    )

    back_own, back_send = call(
        functools.partial(picture_grad, place, side, slab),
        (shape_of(wide, bf16), shape_of(wide, bf16)),
        (after(d_conv, send1), kernel_back),
        (pltpu.VMEM(((side + 2) * slab, 3 * channels), bf16),),
    )
    back_far = move(back_send, dx=1)
    input_grad = call(
        functools.partial(picture_finish, place),
        shape_of(conv_input.shape, bf16),
        (group, back_own, back_far),
        scalars=1,
    )

    hidden_late = after(hidden, outs[0])
    cells = hidden_late.reshape(chips * 2, 2, few, units)
    hidden_here = pick(cells, task, 1)
    hidden_far = move(pick(cells, 1 - task, 1).astype(bf16), dx=1).astype(f32)
    mixes = jnp.where(task == 0, stitch_fc, stitch_fc[::-1, ::-1])
    mixed_own = mixes[0, 0] * hidden_here + mixes[0, 1] * hidden_far
    mixed_other = mixes[1, 0] * hidden_here + mixes[1, 1] * hidden_far
    mixed = ordered(
        task, mixed_own[:, None].astype(bf16), mixed_other[:, None].astype(bf16), axis=1
    )
    mixed = mixed.reshape(planes, 2, 2, 2, few, units)
    mixed = jnp.where(at.y == 0, mixed, mixed[:, ::-1])
    mixed = jnp.roll(mixed[::-1], at.z + 1, axis=0).reshape(chips * 2, images, units)
    mixed = lax.all_to_all(mixed, "mp", split_axis=0, concat_axis=0, tiled=True)
    output = jnp.transpose(mixed.reshape(chips * 2, 2, few, units), (2, 1, 0, 3))
    output = output.reshape(cotangent.shape)

    def both(own, axis=0):
        own = jnp.expand_dims(own, axis)
        return ordered(task, own, jnp.zeros_like(own), axis=axis)

    gathered_late = after(gathered, outs[1])
    d_fc_late = after(d_fc, outs[1])
    sums_late = after(fc_sums, outs[1])
    if pairs > 1:
        fc_bias_grad, stitch_fc_grad = lax.psum(
            (both(sums_late[0]), both(sums_late[1:3], axis=1)), "batch"
        )
    else:
        sums_far = move(sums_late, dx=1)
        fc_bias_grad = ordered(task, sums_late[0:1], sums_far[0:1])
        stitch_fc_grad = ordered(task, sums_late[1:3][:, None], sums_far[1:3][:, None], axis=1)
    cross = lambda b, z, y, c: ((b + pairs) % (2 * pairs), z, y, c) if c != b // pairs else None
    features_x = lax.ppermute(gathered_late, BOTH, links(cross))
    features_c = move(gathered_late, dc=1)
    d_fc_x = move(d_fc_late, dx=1)
    features_xc = move(features_x, dc=1)
    steps = part // 512
    wide_spec = pl.BlockSpec((rows_all, part // steps), lambda i: (0, i))
    whole_spec = pl.BlockSpec((rows_all, units), lambda i: (0, 0))
    fc_weight_grad = pl.pallas_call(
        functools.partial(fc_grad, place),
        out_shape=shape_of((2, part, units), f32),
        grid=(steps,),
        in_specs=[wide_spec] * 4 + [whole_spec] * 2,
        out_specs=pl.BlockSpec((2, part // steps, units), lambda i: (0, i, 0)),
        compiler_params=pltpu.CompilerParams(vmem_limit_bytes=24 * MIB),
    )(gathered_late, features_c, features_x, features_xc, d_fc_late, d_fc_x)
    if pairs > 1:
        fc_weight_grad = lax.psum_scatter(
            ordered(task, fc_weight_grad, jnp.zeros_like(fc_weight_grad), axis=1),
            "batch",
            scatter_dimension=1,
            tiled=True,
        )
        conv_weight_grad, conv_bias_grad, stitch_pool_grad = lax.psum(
            tuple(
                both(pick(value, task))
                for value in (conv_weight_grad, conv_bias_grad, stitch_pool_grad)
            ),
            "batch",
        )
    return (
        output,
        input_grad,
        conv_weight_grad,
        conv_bias_grad,
        stitch_pool_grad,
        fc_weight_grad,
        fc_bias_grad,
        stitch_fc_grad,
    )


def solution(mesh):
    pairs = mesh.shape["batch"] // 2
    planes = mesh.shape["mp"] // 4
    in_specs = (
        P(BOTH, None, None, None, None),
        P(BOTH),
        P(None, "mp", None),
        P(),
        P(),
        P(None, None, "mp"),
        P(None, "mp"),
        P(None, None, "mp"),
        P(BOTH, None, None),
    )
    out_specs = (
        P(BOTH, None, None),
        P(BOTH, None, None, None, None),
        P(None, "mp", None),
        P(),
        P(),
        P(None, "batch", "mp"),
        P(None, "mp"),
        P(None, None, "mp"),
    )
    return jax.shard_map(
        functools.partial(on_device, pairs, planes),
        mesh=mesh,
        in_specs=in_specs,
        out_specs=out_specs,
        check_vma=False,
    )
```

```python
import functools

import jax
import jax.numpy as jnp
import numpy as np
from jax import lax
from jax.experimental import pallas as pl
from jax.experimental.pallas import tpu as pltpu
from jax.sharding import PartitionSpec as P

BOTH = ("batch", "mp")
WIDTH = 16
EXTRA = 16
ROOT_HALF = 0.7071067811865476
ROOT_TWO_PI_INV = 0.3989422804014327
VMEM = pl.BlockSpec(memory_space=pltpu.VMEM)
SMEM = pl.BlockSpec(memory_space=pltpu.SMEM)
ANY = pl.BlockSpec(memory_space=pl.ANY)
DMA = pltpu.SemaphoreType.DMA
MIB = 1024 * 1024
FLOPS_PER_US = 1100000000
bf16, f32 = jnp.bfloat16, jnp.float32
shape_of = jax.ShapeDtypeStruct


MICROS = dict(
    split_weights=0.3,
    join_cores=0.3,
    split_fc=1.5,
    split_inputs=1.0,
    cot_cores=0.3,
    cot_join=0.3,
    cot_planes=0.3,
    widen=2,
    conv_forward=7.5,
    stitch_block=0.3,
    cot_rows=0.3,
    slope_and_back=1.7,
    fc_far=0.5,
    fc_own=0.5,
    fc_middle=0.3,
    fc_back=1.6,
    add_rows=0.3,
    block_total=0.3,
    mix_output=0.3,
    stitch_terms=0.3,
    conv_slope=0.6,
    kernel_grad=3.7,
    picture_grad=2.2,
    sum_pieces=0.3,
    sum_three=0.3,
    output_aside=0.3,
    output_cores=0.3,
    picture_finish=0.8,
    output_finish=0.8,
    kernel_total=0.4,
    kernel_finish=0.8,
    fc_grad=4.8,
)


def cost(body):
    name = getattr(body, "func", body).__name__
    return pl.CostEstimate(
        flops=int(MICROS[name] * FLOPS_PER_US), bytes_accessed=1, transcendentals=0
    )


def call(body, out_shape, operands, scratch=(), scalars=0, room=4, blocks=None, any_first=False):
    held = [*operands[scalars + any_first :], *jax.tree.leaves(out_shape), *scratch]
    held = [a for a in held if hasattr(a, "shape") and jnp.issubdtype(a.dtype, jnp.number)]
    need = sum(int(np.prod(a.shape)) * jnp.dtype(a.dtype).itemsize for a in held)
    need = min(need, 40 * MIB)
    steps = {}
    out_specs = jax.tree.map(lambda _: VMEM, out_shape)
    if blocks is not None:
        steps = dict(grid=(1,))
        out_specs = pl.BlockSpec(out_shape.shape, lambda i: (0,) * len(out_shape.shape))
    return pl.pallas_call(
        body,
        out_shape=out_shape,
        **steps,
        in_specs=blocks
        or [SMEM] * scalars + [ANY] * any_first + [VMEM] * (len(operands) - scalars - any_first),
        out_specs=out_specs,
        scratch_shapes=scratch,
        cost_estimate=cost(body),
        compiler_params=pltpu.CompilerParams(vmem_limit_bytes=need * 5 // 4 + room * MIB),
    )(*operands)


class Place:
    def __init__(self, pairs, planes):
        batch_at, mp_at = lax.axis_index("batch"), lax.axis_index("mp")
        self.planes = planes
        self.task = lax.div(batch_at, pairs)
        self.core = lax.rem(mp_at, 2)
        self.y = lax.rem(lax.div(mp_at, 2), 2)
        self.z = lax.div(mp_at, 4)

    def chip(self, kz, ky):
        y = self.y if ky == 0 else 1 - self.y
        return lax.rem(self.z + (self.planes - kz), self.planes) * 2 + y


def phi_cdf(value):
    return 0.5 * (1.0 + lax.erf(value * ROOT_HALF))


def gelu_slope(value):
    return phi_cdf(value) + value * ROOT_TWO_PI_INV * jnp.exp(-0.5 * value * value)


def split_high_low(value):
    high = value.astype(bf16)
    return high, (value - high.astype(f32)).astype(bf16)


def window_sum(q_ref, value):
    high, low = split_high_low(value)
    return jnp.dot(q_ref[...], high, preferred_element_type=f32) + jnp.dot(
        q_ref[...], low, preferred_element_type=f32
    )


def split_weights(place, w_ref, mine_ref, other_ref):
    at = place()
    half = mine_ref.shape[1]
    for ref, core in ((mine_ref, at.core), (other_ref, 1 - at.core)):
        lanes = pl.ds(pl.multiple_of(core * half, half), half)
        ref[...] = w_ref[at.task, :, lanes]


def join_cores(place, mine_ref, other_ref, out_ref):
    at = place()
    mine, other = mine_ref[...].astype(f32), other_ref[...].astype(f32)
    low, high = jnp.where(at.core == 0, mine, other), jnp.where(at.core == 0, other, mine)
    out_ref[...] = jnp.concatenate([low, high], axis=0).astype(bf16)


def split_fc(place, w_ref, mine_ref, other_ref, sems):
    at = place()
    part = mine_ref.shape[0]
    copies = []
    for i, (ref, core) in enumerate(((mine_ref, at.core), (other_ref, 1 - at.core))):
        rows = pl.ds(pl.multiple_of(core * part, part), part)
        copies.append(pltpu.make_async_copy(w_ref.at[at.task, rows, :], ref, sems.at[i]))
        copies[-1].start()
    for copy in copies:
        copy.wait()


def split_inputs(place, g_ref, x_ref, cot_ref, own_ref, far_ref, out_ref):
    at = place()
    few, _, side, _, depth = x_ref.shape
    units = out_ref.shape[2]
    columns = lax.broadcasted_iota(jnp.int32, (side, depth), 0)
    value = cot_ref[...].astype(f32)
    rows = jnp.concatenate([value[i, t : t + 1] for t in range(2) for i in range(few)], axis=0)
    for ref in (own_ref, far_ref):
        ref[...] = jnp.zeros_like(ref)
    for n in range(few):
        limit = side - 2 * g_ref[n]
        mark = jnp.broadcast_to(g_ref[n], (1, depth)).astype(f32)
        for y in range(side):
            reach = jnp.where(y < limit, limit, 0)
            mask = jnp.where(columns < reach, 1.0, 0.0).astype(bf16)
            for ref, task in ((own_ref, at.task), (far_ref, 1 - at.task)):
                picture = x_ref[n, task, y] * mask
                if y:
                    ref[y, n, 0:side, :] = picture
                else:
                    gap = jnp.zeros((WIDTH - side - 1, depth), f32)
                    ref[y, n] = jnp.concatenate(
                        [picture.astype(f32), gap, mark], axis=0
                    ).astype(bf16)
    for m in range(out_ref.shape[0]):
        out_ref[m] = rows[:, m * units : (m + 1) * units].astype(bf16)


def widen(place, side, own_ref, far_ref, x3_ref, xt_ref, group_ref):
    at = place()
    _, few, _, depth = own_ref.shape
    channels = group_ref.shape[1]
    marks = []
    for ref in (own_ref, far_ref):
        last = [ref[0, n].astype(f32)[WIDTH - 1 :, :channels] for n in range(few)]
        marks.append(jnp.concatenate(last, axis=0))
    group_ref[...] = jnp.where(
        at.task == 0, jnp.concatenate(marks, axis=0), jnp.concatenate(marks[::-1], axis=0)
    )
    inside = lax.rem(lax.broadcasted_iota(jnp.int32, (few * WIDTH, depth), 0), WIDTH) < side
    block = few * WIDTH
    slab = 2 * block
    for edge in (0, side + 1):
        x3_ref[edge * slab : (edge + 1) * slab, :] = jnp.zeros((slab, 3 * depth), bf16)
        xt_ref[:, edge * slab : (edge + 1) * slab] = jnp.zeros((3 * depth, slab), bf16)
    for y in range(side):
        own = own_ref[y].reshape(block, depth).astype(f32)
        far = far_ref[y].reshape(block, depth).astype(f32)
        first = at.task == 0
        if y == 0:
            own, far = jnp.where(inside, own, 0.0), jnp.where(inside, far, 0.0)
        wide = jnp.concatenate(
            [jnp.where(first, own, far), jnp.where(first, far, own)], axis=0
        )
        rows = slice((y + 1) * slab, (y + 2) * slab)
        turned = wide.T
        for kx in range(3):
            lanes = slice(kx * depth, (kx + 1) * depth)
            shift = (1 - kx) % slab
            x3_ref[rows, lanes] = (pltpu.roll(wide, shift, 0) if shift else wide).astype(bf16)
            xt_ref[lanes, rows] = (pltpu.roll(turned, shift, 1) if shift else turned).astype(bf16)


def conv_forward(place, side, pool, images, *refs):
    g_ref, x_ref, b_ref, q_ref = refs[:4]
    blocks = refs[4:-4]
    pre_ref, mine_ref, other_ref, w_ref = refs[-4:]
    at = place()
    chips = len(blocks) // 2
    rows, half = blocks[0].shape
    here = pl.ds(pl.multiple_of(at.core * half, half), half)
    there = pl.ds(pl.multiple_of((1 - at.core) * half, half), half)
    for j in range(chips):
        to = pl.ds(pl.multiple_of(at.chip(j // 2, j % 2) * rows, 16), rows)
        w_ref[to, here] = blocks[j][...]
        w_ref[to, there] = blocks[chips + j][...]
    slab = images * WIDTH
    depth = x_ref.shape[1]
    channels = w_ref.shape[1]
    acts = {}
    bias = jnp.where(at.task == 0, b_ref[0:1, :], b_ref[1:2, :])
    group = g_ref[...]
    for start in range(0, side, 4):
        rows = min(4, side - start)
        total = None
        for ky in range(3):
            part = jnp.dot(
                x_ref[(start + ky) * slab : (start + ky + rows) * slab, :],
                w_ref[ky * depth : (ky + 1) * depth, :],
                preferred_element_type=f32,
            )
            total = part if total is None else total + part
        total = total + bias
        pre_ref[start * slab : (start + rows) * slab, :] = total
        act = total * phi_cdf(total)
        for row in range(rows):
            acts[start + row] = act[row * slab : (row + 1) * slab, :]
        for p in range(pool):
            if not (start <= 2 * p + 2 < start + rows):
                continue
            cells = window_sum(q_ref, acts[2 * p] + acts[2 * p + 1] + acts[2 * p + 2])
            row = []
            for q in range(pool):
                kept = jnp.where(max(p, q) + group < pool, 1.0 / 9.0, 0.0)
                row.append((cells[q * images : (q + 1) * images, :] * kept).astype(bf16))
            lanes = (p % (pool // 2)) * pool * channels
            lanes = slice(lanes, lanes + pool * channels)
            row = jnp.concatenate(row, axis=1)

            @pl.when(at.core == (2 * p) // pool)
            def _(row=row, lanes=lanes):
                mine_ref[:, lanes] = row

            @pl.when(at.core != (2 * p) // pool)
            def _(row=row, lanes=lanes):
                other_ref[:, lanes] = row


def slope_and_back(pre_ref, w_ref, slope_ref, back_ref):
    slope_ref[...] = gelu_slope(pre_ref[...])
    taps = 9
    depth = w_ref.shape[0] // taps
    channels = w_ref.shape[1]
    for tap in range(taps):
        far = taps - 1 - tap
        back_ref[tap * channels : (tap + 1) * channels, :] = (
            w_ref[far * depth : (far + 1) * depth, :].astype(f32).T.astype(bf16)
        )


def cot_rows(place, own_ref, far_ref, up_ref):
    at = place()
    first = at.task == 0
    low_rows = lax.broadcasted_iota(jnp.int32, own_ref.shape[1:], 0) < 4
    for j in range(own_ref.shape[0] // 2):
        chip = at.chip(j // 2, j % 2)
        for c in range(2):
            own = own_ref[2 * chip + c].astype(f32)
            far = far_ref[2 * chip + c].astype(f32)
            low = jnp.where(first, own, far)
            high = jnp.where(first, far, own)
            zero = jnp.where(low_rows, low, pltpu.roll(high, 4, 0))
            one = jnp.where(low_rows, pltpu.roll(low, 4, 0), high)
            here = slice((2 * j + c) * 8, (2 * j + c + 1) * 8)
            up_ref[0, here, :] = jnp.where(first, zero, one)
            up_ref[1, here, :] = jnp.where(first, one, zero)


def stitch_mix(at, ref, t, u):
    row = ref[t]
    return jnp.where(u == 0, row[0:1, :], row[1:2, :])


def core_rows(at, mine, other):
    mine, other = mine.astype(f32), other.astype(f32)
    first = at.core == 0
    return jnp.concatenate(
        [jnp.where(first, mine, other), jnp.where(first, other, mine)], axis=0
    )


def stitch_block(place, mine_ref, c_ref, x_ref, xc_ref, st_ref, out_ref):
    at = place()
    channels = st_ref.shape[2]
    near = stitch_mix(at, st_ref, at.task, at.task)
    far = stitch_mix(at, st_ref, at.task, 1 - at.task)
    for cell in range(out_ref.shape[1] // channels):
        lanes = slice(cell * channels, (cell + 1) * channels)
        own = core_rows(at, mine_ref[:, lanes], c_ref[:, lanes])
        other = core_rows(at, x_ref[:, lanes], xc_ref[:, lanes])
        out_ref[:, lanes] = (near * own + far * other).astype(bf16)


def fc_far(*refs):
    blocks = refs[:-3]
    w_ref, all_ref, out_ref = refs[-3:]
    rows = blocks[0].shape[0]
    for j, block in enumerate(blocks):
        all_ref[j * rows : (j + 1) * rows, :] = block[...]
    out_ref[...] = jnp.dot(all_ref[...], w_ref[...], preferred_element_type=f32)


def fc_own(x_ref, w_ref, out_ref):
    out_ref[...] = jnp.dot(x_ref[...], w_ref[...], preferred_element_type=f32)


def four_rows(task, value, groups):
    rows = lax.broadcasted_iota(jnp.int32, (8, value.shape[1]), 0) < 4
    packed = []
    for g in range(0, groups, 2):
        one, two = value[g * 8 : g * 8 + 8], value[g * 8 + 8 : g * 8 + 16]
        zero = jnp.where(rows, one, pltpu.roll(two, 4, 0))
        last = jnp.where(rows, pltpu.roll(one, 4, 0), two)
        packed.append(jnp.where(task == 0, zero, last))
    return jnp.concatenate(packed, axis=0)


def fc_middle(
    place, own_ref, back_ref, bias_ref, mix_ref, up_ref, d_ref, hidden_ref, pack_ref, sums_ref
):
    at = place()
    first = at.task == 0
    bias = jnp.where(first, bias_ref[0:1, :], bias_ref[1:2, :])
    pre = own_ref[...] + back_ref[...] + bias
    cdf = phi_cdf(pre)
    hidden = pre * cdf
    groups = hidden.shape[0] // 8
    hidden_ref[...] = four_rows(at.task, hidden, groups)
    slope = cdf + pre * ROOT_TWO_PI_INV * jnp.exp(-0.5 * pre * pre)
    mine, other = up_ref[0], up_ref[1]
    d_hidden = stitch_mix(at, mix_ref, at.task, at.task) * mine
    d_hidden += stitch_mix(at, mix_ref, 1 - at.task, at.task) * other
    d_fc = (slope * d_hidden).astype(bf16)
    d_ref[...] = d_fc
    by_mine = jnp.sum(mine * hidden, axis=0, keepdims=True)
    by_other = jnp.sum(other * hidden, axis=0, keepdims=True)
    sums = jnp.concatenate(
        [
            jnp.sum(d_fc.astype(f32), axis=0, keepdims=True),
            jnp.where(first, by_mine, by_other),
            jnp.where(first, by_other, by_mine),
            jnp.zeros((5, by_mine.shape[1]), f32),
        ],
        axis=0,
    )
    high, low = split_high_low(sums)
    sums = jnp.concatenate([high.astype(f32), low.astype(f32)], axis=0)
    sums_ref[...] = sums
    rows = d_ref.shape[0]
    pack_ref[0 : rows // 2, :] = four_rows(1 - at.task, hidden, groups).astype(bf16)
    pack_ref[rows // 2 : rows // 2 + rows, :] = d_fc
    pack_ref[rows // 2 + rows :, :] = sums.astype(bf16)


def folded_lanes(value, lanes):
    return jnp.concatenate(
        [value[:, at : at + lanes] for at in range(0, value.shape[1], lanes)], axis=0
    )


def mix_output(place, own_ref, far_ref, mix_ref, keep_ref, send_ref):
    at = place()
    rows = lax.broadcasted_iota(jnp.int32, (8, own_ref.shape[1]), 0) < 4
    own_all = own_ref[...]
    far_all = far_ref[0 : own_all.shape[0], :].astype(f32)
    sums = []
    for t in range(2):
        sums.append(
            stitch_mix(at, mix_ref, t, at.task) * own_all
            + stitch_mix(at, mix_ref, t, 1 - at.task) * far_all
        )
    for kz in range(keep_ref.shape[0]):
        for ky, out in enumerate((keep_ref, send_ref)):
            here = slice((2 * kz + ky) * 8, (2 * kz + ky) * 8 + 8)
            zero, one = sums[0][here], sums[1][here]
            value = jnp.concatenate(
                [
                    jnp.where(rows, zero, pltpu.roll(one, 4, 0)),
                    jnp.where(rows, pltpu.roll(zero, 4, 0), one),
                ],
                axis=0,
            )
            out[kz] = folded_lanes(value, out.shape[2]).astype(bf16)


def output_finish(place, keep_ref, came_ref, sums_ref, far_ref, out_ref, bias_ref, st_ref, all_ref):
    at = place()
    units = keep_ref.shape[2]
    folds = units // came_ref.shape[1]
    first_row = came_ref.shape[0] - 8 * folds * keep_ref.shape[0]
    came_all = came_ref[first_row:, :].astype(f32)
    for j in range(keep_ref.shape[0]):
        chip = at.chip(j // 2, j % 2)
        mine = pl.ds(pl.multiple_of((2 * chip + at.core) * units, units), units)
        all_ref[:, mine] = keep_ref[j]
        other = pl.ds(pl.multiple_of((2 * chip + 1 - at.core) * units, units), units)
        rows = [8 * (folds * j + f) for f in range(folds)]
        all_ref[:, other] = jnp.concatenate([came_all[i : i + 8] for i in rows], axis=1)
    for i in range(4):
        out_ref[i] = jnp.concatenate(
            [all_ref[i : i + 1, :], all_ref[4 + i : 5 + i, :]], axis=0
        ).astype(bf16)
    first = at.task == 0
    own, far = sums_ref[...], far_ref[far_ref.shape[0] - 16 :, :].astype(f32)
    own, far = own[0:8] + own[8:16], far[0:8] + far[8:16]
    zero, one = jnp.where(first, own, far), jnp.where(first, far, own)
    bias_ref[0:1, :] = zero[0:1]
    bias_ref[1:2, :] = one[0:1]
    for t in range(2):
        st_ref[t] = jnp.concatenate([zero[1 + t : 2 + t], one[1 + t : 2 + t]], axis=0)


def fc_back(d_ref, far_ref, w_ref, wf_ref, *outs):
    chips = len(outs)
    rows = outs[0].shape[0]
    contract = (((1,), (1,)), ((), ()))
    total = lax.dot_general(d_ref[...], w_ref[...], contract, preferred_element_type=f32)
    total += lax.dot_general(far_ref[...], wf_ref[...], contract, preferred_element_type=f32)
    for j, out in enumerate(outs):
        out[...] = total[j * rows : (j + 1) * rows, :].astype(out.dtype)


def add_rows(keep_ref, got_ref, *outs):
    total = keep_ref[...] + got_ref[...].astype(f32)
    for out in outs:
        out[...] = total.astype(out.dtype)


def block_total(place, keep_ref, *refs):
    at = place()
    total_ref, mine_ref, mine_low_ref, other_ref = refs[-4:]
    total = keep_ref[...]
    for ref in refs[:-4]:
        total = total + ref[...].astype(f32)
    total_ref[...] = total
    images = mine_ref.shape[0]
    low, high = total[:images], total[images:]
    mine = jnp.where(at.core == 0, low, high)
    mine_ref[...] = mine
    mine_low_ref[...] = mine.astype(bf16)
    other_ref[...] = jnp.where(at.core == 0, high, low).astype(bf16)


def stitch_terms(place, total_ref, mine_ref, c_ref, x_ref, xc_ref, out_ref):
    at = place()
    channels = out_ref.shape[1]
    own = far = None
    for cell in range(total_ref.shape[1] // channels):
        lanes = slice(cell * channels, (cell + 1) * channels)
        grad = total_ref[:, lanes]
        one = grad * core_rows(at, mine_ref[:, lanes], c_ref[:, lanes])
        two = grad * core_rows(at, x_ref[:, lanes], xc_ref[:, lanes])
        own = one if own is None else own + one
        far = two if far is None else far + two
    out_ref[...] = jnp.concatenate(
        [
            jnp.sum(own, axis=0, keepdims=True),
            jnp.sum(far, axis=0, keepdims=True),
            jnp.zeros((6, channels), f32),
        ],
        axis=0,
    )


def conv_slope(place, side, pool, images, *refs):
    (g_ref, mine_ref, c_ref, x_ref, xc_ref, st_ref, slope_ref, q_ref) = refs[:8]
    d_ref, bias_ref = refs[8:]
    at = place()
    slab = images * WIDTH
    channels = slope_ref.shape[1]
    group = g_ref[...]

    near = stitch_mix(at, st_ref, at.task, at.task)
    far = stitch_mix(at, st_ref, 1 - at.task, at.task)
    spread = []
    for p in range(pool):
        mine_here = at.core == (2 * p) // pool
        cells = []
        for q in range(pool):
            lanes = ((p % (pool // 2)) * pool + q) * channels
            lanes = slice(lanes, lanes + channels)
            kept = jnp.where(max(p, q) + group < pool, 1.0 / 9.0, 0.0)
            one = near * mine_ref[:, lanes] + far * x_ref[:, lanes].astype(f32)
            two = near * c_ref[:, lanes].astype(f32) + far * xc_ref[:, lanes].astype(f32)
            cells.append(jnp.where(mine_here, one, two) * kept)
        spread.append(window_sum(q_ref, jnp.concatenate(cells, axis=0)))
    total = jnp.zeros((8, channels), f32)
    for y in range(side):
        act = None
        for p in range(pool):
            if 2 * p <= y <= 2 * p + 2:
                act = spread[p] if act is None else act + spread[p]
        grad = (act * slope_ref[y * slab : (y + 1) * slab, :]).astype(bf16)
        d_ref[y * slab : (y + 1) * slab, :] = grad
        total = total + jnp.sum(grad.astype(f32).reshape(-1, 8, channels), axis=0)
    bias_ref[...] = jnp.sum(total, axis=0, keepdims=True)


def kernel_grad(place, slab, xt_ref, d_ref, bias_ref, st_ref, *refs):
    keep_ref, send_ref, scr_ref = refs
    at = place()
    depth = xt_ref.shape[0]
    chips, full, half = keep_ref.shape
    rows = full - EXTRA
    count = d_ref.shape[0]
    for ky in range(3):
        scr_ref[ky * depth : (ky + 1) * depth, :] = jnp.dot(
            xt_ref[:, ky * slab : ky * slab + count], d_ref[...], preferred_element_type=f32
        )
    small = jnp.concatenate([bias_ref[...], st_ref[0:2, :]], axis=0)
    small = jnp.concatenate(
        [small[:, :half], jnp.zeros((1, half), f32), small[:, half:], jnp.zeros((1, half), f32)],
        axis=0,
    )
    high, low = split_high_low(small)
    extra = jnp.concatenate([high.astype(f32), low.astype(f32)], axis=0)
    here = pl.ds(pl.multiple_of(at.core * half, half), half)
    there = pl.ds(pl.multiple_of((1 - at.core) * half, half), half)
    for j in range(chips):
        to = pl.ds(pl.multiple_of(at.chip(j // 2, j % 2) * rows, 16), rows)
        keep_ref[j, 0:rows, :] = scr_ref[to, here]
        send_ref[j, 0:rows, :] = scr_ref[to, there].astype(bf16)
        keep_ref[j, rows:full, :] = extra
        send_ref[j, rows:full, :] = extra.astype(bf16)


def folded(extra):
    value = extra[:8] + extra[8:]
    high, low = split_high_low(value)
    return jnp.concatenate([high.astype(f32), low.astype(f32)], axis=0)


def sum_pieces(keep_ref, got_ref, output_ref, *outs):
    full = keep_ref.shape[1]
    rows = full - EXTRA
    for kz, out in enumerate(outs):
        total = keep_ref[2 * kz + 1] + got_ref[2 * kz + 1].astype(f32)
        out[0:rows, :] = total[:rows].astype(bf16)
        out[rows:full, :] = folded(total[rows:]).astype(bf16)
        out[full:, :] = output_ref[kz]


def sum_three(k, keep_ref, got_ref, came_ref, output_ref, out_ref):
    full = keep_ref.shape[1]
    rows = full - EXTRA
    more = output_ref.shape[1]
    total = keep_ref[2 * k] + got_ref[2 * k].astype(f32)
    total = jnp.concatenate([total[:rows], folded(total[rows:])], axis=0)
    total = total + came_ref[0:full, :].astype(f32)
    out_ref[0:rows, :] = total[:rows].astype(out_ref.dtype)
    out_ref[rows:full, :] = folded(total[rows:]).astype(out_ref.dtype)
    out_ref[full : full + more, :] = output_ref[k].astype(out_ref.dtype)
    out_ref[full + more :, :] = came_ref[full:, :].astype(out_ref.dtype)


def kernel_total(place, *refs):
    parts, (mine_ref, other_ref, pack_ref, keep_ref, scr_ref, small_ref) = refs[:-6], refs[-6:]
    at = place()
    rows, half = scr_ref.shape
    full = rows + EXTRA
    total = None
    riders = []
    for k, part in enumerate(parts):
        value = part[...].astype(f32)
        total = value[:rows] if total is None else total + value[:rows]
        small_ref[k] = value[rows : rows + 8] + value[rows + 8 : full]
        more = (value.shape[0] - full) // 2
        for y in range(2):
            piece = value[full + more * y : full + more * (y + 1)]
            low = [piece[i : i + 8] for i in range(0, more, 16)]
            high = [piece[i + 8 : i + 16] for i in range(0, more, 16)]
            zero = at.core == 0
            keep_ref[2 * k + y] = jnp.concatenate(
                [jnp.where(zero, a, b) for a, b in zip(low, high, strict=True)], axis=1
            )
            riders += [jnp.where(zero, b, a) for a, b in zip(low, high, strict=True)]
    scr_ref[...] = total
    small = None
    for z in range(len(parts)):
        piece = small_ref[lax.rem(at.z + (len(parts) - z), len(parts))]
        small = piece if small is None else small + piece
    high, low = split_high_low(small)
    tail = jnp.zeros((mine_ref.shape[0] - rows // 2 - EXTRA, half), f32)
    for ref, c in ((mine_ref, at.core), (other_ref, 1 - at.core)):
        piece = scr_ref[pl.ds(pl.multiple_of(c * (rows // 2), 8), rows // 2), :]
        value = [high.astype(f32), low.astype(f32), piece] + [tail] * (tail.shape[0] > 0)
        ref[...] = jnp.concatenate(value, axis=0).astype(bf16)
    pack_ref[0 : other_ref.shape[0], :] = other_ref[...]
    pack_ref[other_ref.shape[0] :, :] = jnp.concatenate(riders, axis=0).astype(bf16)


def kernel_finish(place, mine_ref, c_ref, x_ref, xc_ref, grad_ref, bias_ref, stitch_ref):
    at = place()
    rows = grad_ref.shape[1]
    half = grad_ref.shape[2] // 2
    first = at.task == 0
    low_core = at.core == 0

    def lanes(one, two):
        return jnp.concatenate(
            [jnp.where(low_core, one, two), jnp.where(low_core, two, one)], axis=1
        )

    own = lanes(mine_ref[...].astype(f32), c_ref[0 : mine_ref.shape[0], :].astype(f32))
    far = lanes(x_ref[...].astype(f32), xc_ref[...].astype(f32))
    grad_ref[0] = jnp.where(first, own, far)[EXTRA : EXTRA + rows, :]
    grad_ref[1] = jnp.where(first, far, own)[EXTRA : EXTRA + rows, :]

    def small(ref):
        value = ref[...].astype(f32)
        value = value[0:8] + value[8:16]
        return jnp.concatenate([value[0:4], value[4:8]], axis=1)

    own, far = small(mine_ref), small(x_ref)
    bias_ref[0:1, :] = jnp.where(first, own, far)[0:1, :]
    bias_ref[1:2, :] = jnp.where(first, far, own)[0:1, :]
    own_pair = jnp.where(first, own[1:3], jnp.concatenate([own[2:3], own[1:2]], axis=0))
    far_pair = jnp.where(first, jnp.concatenate([far[2:3], far[1:2]], axis=0), far[1:3])
    stitch_ref[0] = jnp.where(first, own_pair, far_pair)
    stitch_ref[1] = jnp.where(first, far_pair, own_pair)


def picture_grad(place, far, side, slab, d_ref, w_ref, out_ref, pad_ref):
    at = place()
    channels = d_ref.shape[1]
    depth = 3 * channels
    block = slab // 2
    first = (1 - at.task if far else at.task) * block
    blank = jnp.zeros((block, depth), bf16)
    pad_ref[0:block, :] = blank
    pad_ref[(side + 1) * block :, :] = blank
    for y in range(side):
        here = pl.ds(pl.multiple_of(y * slab + first, 16), block)
        wide = d_ref[here, :].astype(f32)
        rows = slice((y + 1) * block, (y + 2) * block)
        pad_ref[rows, 0:channels] = pltpu.roll(wide, 1, 0).astype(bf16)
        pad_ref[rows, channels : 2 * channels] = wide.astype(bf16)
        pad_ref[rows, 2 * channels :] = pltpu.roll(wide, block - 1, 0).astype(bf16)
    for start in range(0, side, 7):
        rows = min(7, side - start)
        total = None
        for ky in range(3):
            part = jnp.dot(
                pad_ref[(start + ky) * block : (start + ky + rows) * block, :],
                w_ref[ky * depth : (ky + 1) * depth, :],
                preferred_element_type=f32,
            )
            total = part if total is None else total + part
        for row in range(rows):
            value = total[row * block : (row + 1) * block].astype(bf16)
            out_ref[start + row] = value.reshape(out_ref.shape[1:])


def picture_finish(place, g_ref, own_ref, far_ref, out_ref):
    at = place()
    side, few, _, depth = own_ref.shape
    columns = lax.broadcasted_iota(jnp.int32, (side, depth), 0)
    for n in range(few):
        limit = side - 2 * g_ref[n]
        for y in range(side):
            reach = jnp.where(y < limit, limit, 0)
            mask = jnp.where(columns < reach, 1.0, 0.0).astype(bf16)
            out_ref[n, at.task, y] = own_ref[y, n, 0:side, :] * mask
            out_ref[n, 1 - at.task, y] = far_ref[y, n, 0:side, :] * mask


def fc_grad(place, own_ref, oc_ref, x_ref, xc_ref, d_ref, dx_ref, out_ref):
    at = place()
    same = at.core == at.task
    own = jnp.where(same, own_ref[...], oc_ref[...])
    far = jnp.where(same, x_ref[...], xc_ref[...])
    contract = (((0,), (0,)), ((), ()))
    out_ref[at.task] = lax.dot_general(own, d_ref[...], contract, preferred_element_type=f32)
    rows = d_ref.shape[0]
    d_far = dx_ref[rows // 2 : rows // 2 + rows, :]
    out_ref[1 - at.task] = lax.dot_general(far, d_far, contract, preferred_element_type=f32)


def on_device(pairs, planes, *operands):
    (
        conv_input,
        group,
        conv_weight,
        conv_bias,
        stitch_pool,
        fc_weight,
        fc_bias,
        stitch_fc,
        cotangent,
    ) = operands
    chips = 2 * planes
    place = functools.partial(Place, pairs, planes)
    task = Place(pairs, planes).task
    few = conv_input.shape[0]
    images = 2 * few
    side = conv_input.shape[2]
    channels_in = conv_input.shape[4]
    channels = conv_bias.shape[1]
    pool = (side - 3) // 2 + 1
    units = fc_bias.shape[1]
    features = pool * pool * channels
    part = features // 2
    slab = images * WIDTH
    own_rows = conv_weight.shape[1]
    chip_rows = 2 * own_rows
    half = channels // 2

    def links(where):
        pairs_of = []
        for b in range(2 * pairs):
            for m in range(4 * planes):
                to = where(b, m // 4, (m // 2) % 2, m % 2)
                if to is not None:
                    far_b, z, y, c = to
                    far_m = ((z % planes) * 2 + y) * 2 + c
                    pairs_of.append((b * 4 * planes + m, far_b * 4 * planes + far_m))
        return pairs_of

    def move(value, dx=0, dz=0, dy=0, dc=0):
        where = lambda b, z, y, c: ((b + pairs * dx) % (2 * pairs), z + dz, y ^ dy, c ^ dc)
        return lax.ppermute(value, BOTH, links(where))

    def pick(array, index, axis=0):
        return lax.dynamic_index_in_dim(array, index, axis, keepdims=False)

    def ordered(flag, mine, other, axis=0):
        return jnp.where(
            flag == 0,
            jnp.concatenate([mine, other], axis=axis),
            jnp.concatenate([other, mine], axis=axis),
        )

    def after(value, *others):
        return lax.optimization_barrier((value, *others))[0]

    shifts = []
    for near in range(1, planes // 2 + 1):
        shifts.extend(sorted({near, planes - near}))

    def gather_chips(block):
        rows = [[block, move(block, dy=1)]] + [None] * (planes - 1)
        here = {k: move(block, dz=k) for k in shifts}
        for k in shifts:
            rows[k] = [here[k], move(here[k], dy=1)]
        return [piece for pair in rows for piece in pair]

    weight_mine, weight_other = call(
        functools.partial(split_weights, place),
        (shape_of((own_rows, half), bf16), shape_of((own_rows, half), bf16)),
        (conv_weight,),
    )
    weight_block = call(
        functools.partial(join_cores, place),
        shape_of((chip_rows, half), bf16),
        (weight_mine, move(weight_other, dc=1)),
    )
    wide = (side, few, WIDTH, channels_in)
    picture_own, picture_send, cot_send = call(
        functools.partial(split_inputs, place),
        (
            shape_of(wide, bf16),
            shape_of(wide, bf16),
            shape_of((4 * planes, images, units), bf16),
        ),
        (group, conv_input, cotangent),
        scalars=1,
    )
    picture_far = move(picture_send, dx=1)
    weight_blocks = gather_chips(after(weight_block, picture_send))
    weight_far = [move(block, dc=1) for block in weight_blocks]
    stacked, stacked_t, groups = call(
        functools.partial(widen, place, side),
        (
            shape_of(((side + 2) * slab, 3 * channels_in), bf16),
            shape_of((3 * channels_in, (side + 2) * slab), bf16),
            shape_of((images, channels), f32),
        ),
        (picture_own, picture_far),
    )

    cot_send = after(cot_send, weight_blocks[1])
    cot_own = lax.all_to_all(cot_send, "mp", split_axis=0, concat_axis=0, tiled=True)
    cot_far = move(after(cot_own, picture_far), dx=1)

    window = np.zeros((pool * images, slab), np.float32)
    for q in range(pool):
        for n in range(images):
            window[q * images + n, n * WIDTH + 2 * q : n * WIDTH + 2 * q + 3] = 1.0
    window_t = jnp.asarray(window.T, bf16)
    window = jnp.asarray(window, bf16)
    stacked = after(stacked, stacked_t)
    conv_pre, pooled_mine, pooled_other, kernel = call(
        functools.partial(conv_forward, place, side, pool, images),
        (
            shape_of((side * slab, channels), f32),
            shape_of((images, part), bf16),
            shape_of((images, part), bf16),
            shape_of((chips * chip_rows, channels), bf16),
        ),
        (groups, stacked, conv_bias, window, *weight_blocks, *weight_far),
    )

    pooled_mine = after(pooled_mine, cot_far)
    pooled_x = move(pooled_mine, dx=1)
    pooled_xc = move(pooled_other, dx=1, dc=1)
    pooled_c = move(pooled_other, dc=1)
    pooled = (pooled_mine, pooled_c, pooled_x, pooled_xc)
    piece = (2 * images, part)
    rows_all = chips * 2 * images
    blocks = gather_chips(
        call(functools.partial(stitch_block, place), shape_of(piece, bf16), (*pooled, stitch_pool))
    )

    up = call(
        functools.partial(cot_rows, place),
        shape_of((2, rows_all, units), f32),
        (cot_own, after(cot_far, *blocks[2::2])),
    )

    fc_mine, fc_other = call(
        functools.partial(split_fc, place),
        (shape_of((part, units), bf16), shape_of((part, units), bf16)),
        (after(fc_weight, *blocks[2::2]),),
        (DMA((2,)),),
        blocks=None,
        any_first=True,
    )
    fc_other = move(fc_other, dc=1)

    slope, kernel_back = call(
        slope_and_back,
        (
            shape_of(conv_pre.shape, f32),
            shape_of((9 * channels, channels_in), bf16),
        ),
        (after(conv_pre, *blocks[2::2]), kernel),
    )

    gathered, far_term = call(
        fc_far,
        (shape_of((rows_all, part), bf16), shape_of((rows_all, units), f32)),
        (*blocks, after(fc_other, slope, kernel_back, up)),
    )
    far_back = move(far_term, dc=1)
    own_term = call(fc_own, shape_of((rows_all, units), f32), (gathered, fc_mine))
    d_fc, hidden, x_pack, fc_sums = call(
        functools.partial(fc_middle, place),
        (
            shape_of((rows_all, units), bf16),
            shape_of((rows_all // 2, units), f32),
            shape_of((rows_all // 2 + rows_all + 16, units), bf16),
            shape_of((16, units), f32),
        ),
        (own_term, far_back, fc_bias, stitch_fc, up),
    )
    d_fc_far = move(d_fc, dc=1)
    outs = call(
        fc_back,
        tuple(shape_of(piece, bf16 if j % 2 else f32) for j in range(chips)),
        (d_fc, d_fc_far, fc_mine, fc_other),
    )
    kept, sent = outs[0::2], outs[1::2]

    order = shifts[::-1] + [0]
    arrived = {k: move(sent[k], dy=1) for k in order}
    passed = {}
    for k in order[:-1]:
        low = call(add_rows, (shape_of(piece, bf16),), (kept[k], arrived[k]))[0]
        passed[k] = move(low, dz=-k)
    x_came = move(after(x_pack, *arrived.values()), dx=1)
    cross = lambda b, z, y, c: ((b + pairs) % (2 * pairs), z, y, c) if c != b // pairs else None
    features_x = lax.ppermute(gathered, BOTH, links(cross))
    features_c = move(after(gathered, *arrived.values()), dc=1)
    d_total, d_mine, d_mine_low, d_other = call(
        functools.partial(block_total, place),
        (
            shape_of(piece, f32),
            shape_of((images, part), f32),
            shape_of((images, part), bf16),
            shape_of((images, part), bf16),
        ),
        (after(kept[0], features_x, features_c), arrived[0], *[passed[k] for k in order[:-1]]),
    )

    d_x = move(d_mine_low, dx=1)
    d_xc = move(d_other, dx=1, dc=1)
    d_c = move(d_other, dc=1)
    ride = 2 * images * units // half
    riding = shape_of((planes, ride, half), bf16)
    out_keep, out_send = call(
        functools.partial(mix_output, place),
        (riding, riding),
        (hidden, after(x_came, d_xc), stitch_fc),
    )
    stitch_sums = call(
        functools.partial(stitch_terms, place),
        shape_of((8, channels), f32),
        (after(d_total, d_other), *pooled),
    )
    d_conv, d_bias = call(
        functools.partial(conv_slope, place, side, pool, images),
        (shape_of((side * slab, channels), bf16), shape_of((1, channels), f32)),
        (groups, d_mine, d_c, d_x, d_xc, stitch_pool, slope, window_t),
    )

    full = chip_rows + EXTRA
    stack = (chips, full, half)
    keep, send = call(
        functools.partial(kernel_grad, place, slab),
        (shape_of(stack, f32), shape_of(stack, bf16)),
        (stacked_t, after(d_conv, out_send), d_bias, stitch_sums),
        (pltpu.VMEM((chips * chip_rows, channels), f32),),
    )
    got = move(send, dc=1)
    thin = (side, few, WIDTH, channels_in)
    pad = (pltpu.VMEM(((side + 2) * slab // 2, 3 * channels), bf16),)
    back_send = call(
        functools.partial(picture_grad, place, True, side, slab),
        shape_of(thin, bf16),
        (after(d_conv, send), kernel_back),
        pad,
    )
    flat = (full + ride, half)
    sent = call(
        sum_pieces,
        tuple(shape_of(flat, bf16) for _ in range(planes)),
        (keep, after(got, back_send), out_send),
    )
    arrived = {k: move(sent[k], dy=1) for k in order}
    parts = {}
    for k in order:
        parts[k] = call(
            functools.partial(sum_three, k),
            shape_of((full + 2 * ride, half), bf16 if k else f32),
            (keep, got, arrived[k], out_keep),
        )
        if k:
            parts[k] = move(parts[k], dz=-k)
    late = arrived[order[0]]

    back_far = move(back_send, dx=1)
    back_own = call(
        functools.partial(picture_grad, place, False, side, slab),
        shape_of(thin, bf16),
        (after(d_conv, *[arrived[k] for k in order]), kernel_back),
        pad,
    )
    input_grad = call(
        functools.partial(picture_finish, place),
        shape_of(conv_input.shape, bf16),
        (group, back_own, back_far),
        scalars=1,
    )

    def both(own, axis=0):
        own = jnp.expand_dims(own, axis)
        return ordered(task, own, jnp.zeros_like(own), axis=axis)

    d_fc_last = after(d_fc, parts[order[0]])
    features_xc = move(after(features_x, late), dc=1)
    steps = 3
    wide_spec = pl.BlockSpec((rows_all, part // steps), lambda i: (0, i))
    whole_spec = [pl.BlockSpec(a.shape, lambda i: (0, 0)) for a in (d_fc, x_came)]
    fc_weight_grad = pl.pallas_call(
        functools.partial(fc_grad, place),
        out_shape=shape_of((2, part, units), f32),
        grid=(steps,),
        in_specs=[wide_spec] * 4 + whole_spec,
        out_specs=pl.BlockSpec((2, part // steps, units), lambda i: (0, i, 0)),
        cost_estimate=cost(fc_grad),
        compiler_params=pltpu.CompilerParams(vmem_limit_bytes=24 * MIB),
    )(gathered, features_c, features_x, features_xc, d_fc_last, x_came)
    tall = -(-(own_rows + EXTRA) // 16) * 16
    k_mine, k_other, k_pack, out_own = call(
        functools.partial(kernel_total, place),
        (
            shape_of((tall, half), bf16),
            shape_of((tall, half), bf16),
            shape_of((tall + chips * ride // 2, half), bf16),
            shape_of((chips, images, units), f32),
        ),
        (after(parts[0], fc_weight_grad, back_own), *[parts[planes - k] for k in range(1, planes)]),
        (pltpu.VMEM((chip_rows, half), f32), pltpu.VMEM((planes, 8, half), f32)),
    )
    k_x = move(k_mine, dx=1)
    k_xc = move(k_other, dx=1, dc=1)
    k_c = move(k_pack, dc=1)
    output, fc_bias_grad, stitch_fc_grad = call(
        functools.partial(output_finish, place),
        (
            shape_of(cotangent.shape, bf16),
            shape_of((2, units), f32),
            shape_of((2, 2, units), f32),
        ),
        (out_own, k_c, fc_sums, x_came),
        (pltpu.VMEM((images, cotangent.shape[2]), f32),),
    )
    conv_weight_grad, conv_bias_grad, stitch_pool_grad = call(
        functools.partial(kernel_finish, place),
        (
            shape_of((2, own_rows, channels), f32),
            shape_of((2, channels), f32),
            shape_of((2, 2, channels), f32),
        ),
        (k_mine, k_c, k_x, k_xc),
    )

    if pairs > 1:
        fc_weight_grad = lax.psum_scatter(
            ordered(task, fc_weight_grad, jnp.zeros_like(fc_weight_grad), axis=1),
            "batch",
            scatter_dimension=1,
            tiled=True,
        )
        conv_weight_grad, conv_bias_grad, stitch_pool_grad, fc_bias_grad = lax.psum(
            tuple(
                both(pick(value, task))
                for value in (conv_weight_grad, conv_bias_grad, stitch_pool_grad, fc_bias_grad)
            ),
            "batch",
        )
        stitch_fc_grad = lax.psum(both(pick(stitch_fc_grad, task, 1), axis=1), "batch")
    return (
        output,
        input_grad,
        conv_weight_grad,
        conv_bias_grad,
        stitch_pool_grad,
        fc_weight_grad,
        fc_bias_grad,
        stitch_fc_grad,
    )


def solution(mesh):
    pairs = mesh.shape["batch"] // 2
    planes = mesh.shape["mp"] // 4
    in_specs = (
        P(BOTH, None, None, None, None),
        P(BOTH),
        P(None, "mp", None),
        P(),
        P(),
        P(None, None, "mp"),
        P(None, "mp"),
        P(None, None, "mp"),
        P(BOTH, None, None),
    )
    out_specs = (
        P(BOTH, None, None),
        P(BOTH, None, None, None, None),
        P(None, "mp", None),
        P(),
        P(),
        P(None, "batch", "mp"),
        P(None, "mp"),
        P(None, None, "mp"),
    )
    return jax.shard_map(
        functools.partial(on_device, pairs, planes),
        mesh=mesh,
        in_specs=in_specs,
        out_specs=out_specs,
        check_vma=False,
    )
```

```python
import functools

import jax
import jax.numpy as jnp
import numpy as np
from jax import lax
from jax.experimental import pallas as pl
from jax.experimental.pallas import tpu as pltpu
from jax.sharding import PartitionSpec as P

BOTH = ("batch", "mp")
WIDTH = 16
EXTRA = 16
ROOT_HALF = 0.7071067811865476
ROOT_TWO_PI_INV = 0.3989422804014327
VMEM = pl.BlockSpec(memory_space=pltpu.VMEM)
SMEM = pl.BlockSpec(memory_space=pltpu.SMEM)
ANY = pl.BlockSpec(memory_space=pl.ANY)
DMA = pltpu.SemaphoreType.DMA
MIB = 1024 * 1024
FLOPS_PER_US = 1100000000
bf16, f32 = jnp.bfloat16, jnp.float32
shape_of = jax.ShapeDtypeStruct


MICROS = dict(
    split_weights=0.3,
    join_cores=0.3,
    split_fc=1.5,
    split_inputs=1.0,
    cot_cores=0.3,
    cot_join=0.3,
    cot_planes=0.3,
    widen=2,
    conv_forward=7.5,
    stitch_block=0.3,
    cot_rows=0.3,
    slope_and_back=1.7,
    fc_far=0.5,
    fc_own=0.5,
    fc_middle=0.3,
    fc_back=1.6,
    add_rows=0.3,
    block_total=0.3,
    mix_output=0.3,
    stitch_terms=0.3,
    conv_slope=0.6,
    kernel_grad=3.7,
    picture_grad=2.2,
    sum_pieces=0.3,
    sum_three=0.3,
    output_aside=0.3,
    output_cores=0.3,
    picture_finish=0.8,
    output_finish=0.8,
    kernel_total=0.4,
    kernel_finish=0.8,
    fc_grad=4.8,
)


def cost(body):
    name = getattr(body, "func", body).__name__
    return pl.CostEstimate(
        flops=int(MICROS[name] * FLOPS_PER_US), bytes_accessed=1, transcendentals=0
    )


def call(body, out_shape, operands, scratch=(), scalars=0, room=4, blocks=None, any_first=False):
    held = [*operands[scalars + any_first :], *jax.tree.leaves(out_shape), *scratch]
    held = [a for a in held if hasattr(a, "shape") and jnp.issubdtype(a.dtype, jnp.number)]
    need = sum(int(np.prod(a.shape)) * jnp.dtype(a.dtype).itemsize for a in held)
    need = min(need, 40 * MIB)
    steps = {}
    out_specs = jax.tree.map(lambda _: VMEM, out_shape)
    if blocks is not None:
        steps = dict(grid=(1,))
        out_specs = pl.BlockSpec(out_shape.shape, lambda i: (0,) * len(out_shape.shape))
    return pl.pallas_call(
        body,
        out_shape=out_shape,
        **steps,
        in_specs=blocks
        or [SMEM] * scalars + [ANY] * any_first + [VMEM] * (len(operands) - scalars - any_first),
        out_specs=out_specs,
        scratch_shapes=scratch,
        cost_estimate=cost(body),
        compiler_params=pltpu.CompilerParams(vmem_limit_bytes=need * 5 // 4 + room * MIB),
    )(*operands)


class Place:
    def __init__(self, pairs, planes):
        batch_at, mp_at = lax.axis_index("batch"), lax.axis_index("mp")
        self.planes = planes
        self.task = lax.div(batch_at, pairs)
        self.core = lax.rem(mp_at, 2)
        self.y = lax.rem(lax.div(mp_at, 2), 2)
        self.z = lax.div(mp_at, 4)

    def chip(self, kz, ky):
        y = self.y if ky == 0 else 1 - self.y
        return lax.rem(self.z + (self.planes - kz), self.planes) * 2 + y


def phi_cdf(value):
    return 0.5 * (1.0 + lax.erf(value * ROOT_HALF))


def gelu_slope(value):
    return phi_cdf(value) + value * ROOT_TWO_PI_INV * jnp.exp(-0.5 * value * value)


def split_high_low(value):
    high = value.astype(bf16)
    return high, (value - high.astype(f32)).astype(bf16)


def window_sum(q_ref, value):
    high, low = split_high_low(value)
    return jnp.dot(q_ref[...], high, preferred_element_type=f32) + jnp.dot(
        q_ref[...], low, preferred_element_type=f32
    )


def split_weights(place, w_ref, mine_ref, other_ref):
    at = place()
    half = mine_ref.shape[1]
    for ref, core in ((mine_ref, at.core), (other_ref, 1 - at.core)):
        lanes = pl.ds(pl.multiple_of(core * half, half), half)
        ref[...] = w_ref[at.task, :, lanes]


def join_cores(place, mine_ref, other_ref, out_ref):
    at = place()
    mine, other = mine_ref[...].astype(f32), other_ref[...].astype(f32)
    low, high = jnp.where(at.core == 0, mine, other), jnp.where(at.core == 0, other, mine)
    out_ref[...] = jnp.concatenate([low, high], axis=0).astype(bf16)


def split_fc(place, w_ref, mine_ref, other_ref, sems):
    at = place()
    part = mine_ref.shape[0]
    copies = []
    for i, (ref, core) in enumerate(((mine_ref, at.core), (other_ref, 1 - at.core))):
        rows = pl.ds(pl.multiple_of(core * part, part), part)
        copies.append(pltpu.make_async_copy(w_ref.at[at.task, rows, :], ref, sems.at[i]))
        copies[-1].start()
    for copy in copies:
        copy.wait()


def split_inputs(place, g_ref, x_ref, cot_ref, own_ref, far_ref, out_ref):
    at = place()
    few, _, side, _, depth = x_ref.shape
    units = out_ref.shape[2]
    columns = lax.broadcasted_iota(jnp.int32, (side, depth), 0)
    value = cot_ref[...].astype(f32)
    rows = jnp.concatenate([value[i, t : t + 1] for t in range(2) for i in range(few)], axis=0)
    for ref in (own_ref, far_ref):
        ref[...] = jnp.zeros_like(ref)
    for n in range(few):
        limit = side - 2 * g_ref[n]
        mark = jnp.broadcast_to(g_ref[n], (1, depth)).astype(f32)
        for y in range(side):
            reach = jnp.where(y < limit, limit, 0)
            mask = jnp.where(columns < reach, 1.0, 0.0).astype(bf16)
            for ref, task in ((own_ref, at.task), (far_ref, 1 - at.task)):
                picture = x_ref[n, task, y] * mask
                if y:
                    ref[y, n, 0:side, :] = picture
                else:
                    gap = jnp.zeros((WIDTH - side - 1, depth), f32)
                    ref[y, n] = jnp.concatenate(
                        [picture.astype(f32), gap, mark], axis=0
                    ).astype(bf16)
    for m in range(out_ref.shape[0]):
        out_ref[m] = rows[:, m * units : (m + 1) * units].astype(bf16)


def widen(place, side, own_ref, far_ref, x3_ref, xt_ref, group_ref):
    at = place()
    _, few, _, depth = own_ref.shape
    channels = group_ref.shape[1]
    marks = []
    for ref in (own_ref, far_ref):
        last = [ref[0, n].astype(f32)[WIDTH - 1 :, :channels] for n in range(few)]
        marks.append(jnp.concatenate(last, axis=0))
    group_ref[...] = jnp.where(
        at.task == 0, jnp.concatenate(marks, axis=0), jnp.concatenate(marks[::-1], axis=0)
    )
    inside = lax.rem(lax.broadcasted_iota(jnp.int32, (few * WIDTH, depth), 0), WIDTH) < side
    block = few * WIDTH
    slab = 2 * block
    for edge in (0, side + 1):
        x3_ref[edge * slab : (edge + 1) * slab, :] = jnp.zeros((slab, 3 * depth), bf16)
        xt_ref[:, edge * slab : (edge + 1) * slab] = jnp.zeros((3 * depth, slab), bf16)
    for y in range(side):
        own = own_ref[y].reshape(block, depth).astype(f32)
        far = far_ref[y].reshape(block, depth).astype(f32)
        first = at.task == 0
        if y == 0:
            own, far = jnp.where(inside, own, 0.0), jnp.where(inside, far, 0.0)
        wide = jnp.concatenate(
            [jnp.where(first, own, far), jnp.where(first, far, own)], axis=0
        )
        rows = slice((y + 1) * slab, (y + 2) * slab)
        turned = wide.T
        for kx in range(3):
            lanes = slice(kx * depth, (kx + 1) * depth)
            shift = (1 - kx) % slab
            x3_ref[rows, lanes] = (pltpu.roll(wide, shift, 0) if shift else wide).astype(bf16)
            xt_ref[lanes, rows] = (pltpu.roll(turned, shift, 1) if shift else turned).astype(bf16)


def conv_forward(place, side, pool, images, *refs):
    g_ref, x_ref, b_ref = refs[:3]
    blocks = refs[3:-5]
    pre_ref, mine_ref, other_ref, w_ref, sum_ref = refs[-5:]
    at = place()
    chips = len(blocks) // 2
    rows, half = blocks[0].shape
    here = pl.ds(pl.multiple_of(at.core * half, half), half)
    there = pl.ds(pl.multiple_of((1 - at.core) * half, half), half)
    for j in range(chips):
        to = pl.ds(pl.multiple_of(at.chip(j // 2, j % 2) * rows, 16), rows)
        w_ref[to, here] = blocks[j][...]
        w_ref[to, there] = blocks[chips + j][...]
    slab = images * WIDTH
    depth = x_ref.shape[1]
    channels = w_ref.shape[1]
    acts, pooled = {}, {}
    bias = jnp.where(at.task == 0, b_ref[0:1, :], b_ref[1:2, :])
    group = g_ref[...]
    for start in range(0, side, 4):
        rows = min(4, side - start)
        total = None
        for ky in range(3):
            part = jnp.dot(
                x_ref[(start + ky) * slab : (start + ky + rows) * slab, :],
                w_ref[ky * depth : (ky + 1) * depth, :],
                preferred_element_type=f32,
            )
            total = part if total is None else total + part
        total = total + bias
        pre_ref[start * slab : (start + rows) * slab, :] = total
        act = total * phi_cdf(total)
        for row in range(rows):
            acts[start + row] = act[row * slab : (row + 1) * slab, :]
        for p in range(pool):
            if not (start <= 2 * p + 2 < start + rows):
                continue
            rows_sum = acts[2 * p] + acts[2 * p + 1] + acts[2 * p + 2]
            for tile in range(channels // 128):
                sum_ref[p, tile] = rows_sum[:, tile * 128 : (tile + 1) * 128]
            for q in range(pool):
                kept = jnp.where(max(p, q) + group < pool, 1.0 / 9.0, 0.0)
                cell = None
                for x in range(2 * q, 2 * q + 3):
                    spot = pl.ds(x, images, stride=WIDTH)
                    column = jnp.concatenate(
                        [sum_ref[p, tile, spot, :] for tile in range(channels // 128)], axis=1
                    )
                    cell = column if cell is None else cell + column
                pooled[p, q] = cell * kept
    low = at.core == 0
    for p in range(pool // 2):
        for q in range(pool):
            zero, one = pooled[p, q], pooled[p + pool // 2, q]
            lanes = slice((p * pool + q) * channels, (p * pool + q + 1) * channels)
            mine_ref[:, lanes] = jnp.where(low, zero, one).astype(bf16)
            other_ref[:, lanes] = jnp.where(low, one, zero).astype(bf16)


def slope_and_back(pre_ref, w_ref, slope_ref, back_ref):
    slope_ref[...] = gelu_slope(pre_ref[...])
    taps = 9
    depth = w_ref.shape[0] // taps
    channels = w_ref.shape[1]
    for tap in range(taps):
        far = taps - 1 - tap
        back_ref[tap * channels : (tap + 1) * channels, :] = (
            w_ref[far * depth : (far + 1) * depth, :].astype(f32).T.astype(bf16)
        )


def cot_rows(place, own_ref, far_ref, up_ref):
    at = place()
    first = at.task == 0
    low_rows = lax.broadcasted_iota(jnp.int32, own_ref.shape[1:], 0) < 4
    for j in range(own_ref.shape[0] // 2):
        chip = at.chip(j // 2, j % 2)
        for c in range(2):
            own = own_ref[2 * chip + c].astype(f32)
            far = far_ref[2 * chip + c].astype(f32)
            low = jnp.where(first, own, far)
            high = jnp.where(first, far, own)
            zero = jnp.where(low_rows, low, pltpu.roll(high, 4, 0))
            one = jnp.where(low_rows, pltpu.roll(low, 4, 0), high)
            here = slice((2 * j + c) * 8, (2 * j + c + 1) * 8)
            up_ref[0, here, :] = jnp.where(first, zero, one)
            up_ref[1, here, :] = jnp.where(first, one, zero)


def stitch_mix(at, ref, t, u):
    row = ref[t]
    return jnp.where(u == 0, row[0:1, :], row[1:2, :])


def core_rows(at, mine, other):
    mine, other = mine.astype(f32), other.astype(f32)
    first = at.core == 0
    return jnp.concatenate(
        [jnp.where(first, mine, other), jnp.where(first, other, mine)], axis=0
    )


def stitch_block(place, mine_ref, c_ref, x_ref, xc_ref, st_ref, out_ref):
    at = place()
    channels = st_ref.shape[2]
    near = stitch_mix(at, st_ref, at.task, at.task)
    far = stitch_mix(at, st_ref, at.task, 1 - at.task)
    for cell in range(out_ref.shape[1] // channels):
        lanes = slice(cell * channels, (cell + 1) * channels)
        own = core_rows(at, mine_ref[:, lanes], c_ref[:, lanes])
        other = core_rows(at, x_ref[:, lanes], xc_ref[:, lanes])
        out_ref[:, lanes] = (near * own + far * other).astype(bf16)


def fc_far(*refs):
    blocks = refs[:-3]
    w_ref, all_ref, out_ref = refs[-3:]
    rows = blocks[0].shape[0]
    for j, block in enumerate(blocks):
        all_ref[j * rows : (j + 1) * rows, :] = block[...]
    out_ref[...] = jnp.dot(all_ref[...], w_ref[...], preferred_element_type=f32)


def fc_own(x_ref, w_ref, out_ref):
    out_ref[...] = jnp.dot(x_ref[...], w_ref[...], preferred_element_type=f32)


def four_rows(task, value, groups):
    rows = lax.broadcasted_iota(jnp.int32, (8, value.shape[1]), 0) < 4
    packed = []
    for g in range(0, groups, 2):
        one, two = value[g * 8 : g * 8 + 8], value[g * 8 + 8 : g * 8 + 16]
        zero = jnp.where(rows, one, pltpu.roll(two, 4, 0))
        last = jnp.where(rows, pltpu.roll(one, 4, 0), two)
        packed.append(jnp.where(task == 0, zero, last))
    return jnp.concatenate(packed, axis=0)


def fc_middle(
    place, own_ref, back_ref, bias_ref, mix_ref, up_ref, d_ref, hidden_ref, pack_ref, sums_ref
):
    at = place()
    first = at.task == 0
    bias = jnp.where(first, bias_ref[0:1, :], bias_ref[1:2, :])
    pre = own_ref[...] + back_ref[...] + bias
    cdf = phi_cdf(pre)
    hidden = pre * cdf
    groups = hidden.shape[0] // 8
    hidden_ref[...] = four_rows(at.task, hidden, groups)
    slope = cdf + pre * ROOT_TWO_PI_INV * jnp.exp(-0.5 * pre * pre)
    mine, other = up_ref[0], up_ref[1]
    d_hidden = stitch_mix(at, mix_ref, at.task, at.task) * mine
    d_hidden += stitch_mix(at, mix_ref, 1 - at.task, at.task) * other
    d_fc = (slope * d_hidden).astype(bf16)
    d_ref[...] = d_fc
    by_mine = jnp.sum(mine * hidden, axis=0, keepdims=True)
    by_other = jnp.sum(other * hidden, axis=0, keepdims=True)
    sums = jnp.concatenate(
        [
            jnp.sum(d_fc.astype(f32), axis=0, keepdims=True),
            jnp.where(first, by_mine, by_other),
            jnp.where(first, by_other, by_mine),
            jnp.zeros((5, by_mine.shape[1]), f32),
        ],
        axis=0,
    )
    high, low = split_high_low(sums)
    sums = jnp.concatenate([high.astype(f32), low.astype(f32)], axis=0)
    sums_ref[...] = sums
    rows = d_ref.shape[0]
    pack_ref[0 : rows // 2, :] = four_rows(1 - at.task, hidden, groups).astype(bf16)
    pack_ref[rows // 2 : rows // 2 + rows, :] = d_fc
    pack_ref[rows // 2 + rows :, :] = sums.astype(bf16)


def folded_lanes(value, lanes):
    return jnp.concatenate(
        [value[:, at : at + lanes] for at in range(0, value.shape[1], lanes)], axis=0
    )


def mix_output(place, own_ref, far_ref, mix_ref, keep_ref, send_ref):
    at = place()
    rows = lax.broadcasted_iota(jnp.int32, (8, own_ref.shape[1]), 0) < 4
    own_all = own_ref[...]
    far_all = far_ref[0 : own_all.shape[0], :].astype(f32)
    sums = []
    for t in range(2):
        sums.append(
            stitch_mix(at, mix_ref, t, at.task) * own_all
            + stitch_mix(at, mix_ref, t, 1 - at.task) * far_all
        )
    for kz in range(keep_ref.shape[0]):
        for ky, out in enumerate((keep_ref, send_ref)):
            here = slice((2 * kz + ky) * 8, (2 * kz + ky) * 8 + 8)
            zero, one = sums[0][here], sums[1][here]
            value = jnp.concatenate(
                [
                    jnp.where(rows, zero, pltpu.roll(one, 4, 0)),
                    jnp.where(rows, pltpu.roll(zero, 4, 0), one),
                ],
                axis=0,
            )
            out[kz] = folded_lanes(value, out.shape[2]).astype(bf16)


def output_finish(place, keep_ref, came_ref, sums_ref, far_ref, out_ref, bias_ref, st_ref, all_ref):
    at = place()
    units = keep_ref.shape[2]
    folds = units // came_ref.shape[1]
    first_row = came_ref.shape[0] - 8 * folds * keep_ref.shape[0]
    came_all = came_ref[first_row:, :].astype(f32)
    for j in range(keep_ref.shape[0]):
        chip = at.chip(j // 2, j % 2)
        mine = pl.ds(pl.multiple_of((2 * chip + at.core) * units, units), units)
        all_ref[:, mine] = keep_ref[j]
        other = pl.ds(pl.multiple_of((2 * chip + 1 - at.core) * units, units), units)
        rows = [8 * (folds * j + f) for f in range(folds)]
        all_ref[:, other] = jnp.concatenate([came_all[i : i + 8] for i in rows], axis=1)
    for i in range(4):
        out_ref[i] = jnp.concatenate(
            [all_ref[i : i + 1, :], all_ref[4 + i : 5 + i, :]], axis=0
        ).astype(bf16)
    first = at.task == 0
    own, far = sums_ref[...], far_ref[far_ref.shape[0] - 16 :, :].astype(f32)
    own, far = own[0:8] + own[8:16], far[0:8] + far[8:16]
    zero, one = jnp.where(first, own, far), jnp.where(first, far, own)
    bias_ref[0:1, :] = zero[0:1]
    bias_ref[1:2, :] = one[0:1]
    for t in range(2):
        st_ref[t] = jnp.concatenate([zero[1 + t : 2 + t], one[1 + t : 2 + t]], axis=0)


def fc_back(d_ref, far_ref, w_ref, wf_ref, *outs):
    chips = len(outs)
    rows = outs[0].shape[0]
    contract = (((1,), (1,)), ((), ()))
    total = lax.dot_general(d_ref[...], w_ref[...], contract, preferred_element_type=f32)
    total += lax.dot_general(far_ref[...], wf_ref[...], contract, preferred_element_type=f32)
    for j, out in enumerate(outs):
        out[...] = total[j * rows : (j + 1) * rows, :].astype(out.dtype)


def add_rows(keep_ref, got_ref, *outs):
    total = keep_ref[...] + got_ref[...].astype(f32)
    for out in outs:
        out[...] = total.astype(out.dtype)


def block_total(place, keep_ref, *refs):
    at = place()
    total_ref, mine_ref, mine_low_ref, other_ref = refs[-4:]
    total = keep_ref[...]
    for ref in refs[:-4]:
        total = total + ref[...].astype(f32)
    total_ref[...] = total
    images = mine_ref.shape[0]
    low, high = total[:images], total[images:]
    mine = jnp.where(at.core == 0, low, high)
    mine_ref[...] = mine
    mine_low_ref[...] = mine.astype(bf16)
    other_ref[...] = jnp.where(at.core == 0, high, low).astype(bf16)


def stitch_terms(place, total_ref, mine_ref, c_ref, x_ref, xc_ref, out_ref):
    at = place()
    channels = out_ref.shape[1]
    own = far = None
    for cell in range(total_ref.shape[1] // channels):
        lanes = slice(cell * channels, (cell + 1) * channels)
        grad = total_ref[:, lanes]
        one = grad * core_rows(at, mine_ref[:, lanes], c_ref[:, lanes])
        two = grad * core_rows(at, x_ref[:, lanes], xc_ref[:, lanes])
        own = one if own is None else own + one
        far = two if far is None else far + two
    out_ref[...] = jnp.concatenate(
        [
            jnp.sum(own, axis=0, keepdims=True),
            jnp.sum(far, axis=0, keepdims=True),
            jnp.zeros((6, channels), f32),
        ],
        axis=0,
    )


def conv_slope(place, side, pool, images, *refs):
    (g_ref, mine_ref, c_ref, x_ref, xc_ref, st_ref, slope_ref, q_ref) = refs[:8]
    d_ref, bias_ref = refs[8:]
    at = place()
    slab = images * WIDTH
    channels = slope_ref.shape[1]
    group = g_ref[...]

    near = stitch_mix(at, st_ref, at.task, at.task)
    far = stitch_mix(at, st_ref, 1 - at.task, at.task)
    spread = []
    for p in range(pool):
        mine_here = at.core == (2 * p) // pool
        cells = []
        for q in range(pool):
            lanes = ((p % (pool // 2)) * pool + q) * channels
            lanes = slice(lanes, lanes + channels)
            kept = jnp.where(max(p, q) + group < pool, 1.0 / 9.0, 0.0)
            one = near * mine_ref[:, lanes] + far * x_ref[:, lanes].astype(f32)
            two = near * c_ref[:, lanes].astype(f32) + far * xc_ref[:, lanes].astype(f32)
            cells.append(jnp.where(mine_here, one, two) * kept)
        spread.append(window_sum(q_ref, jnp.concatenate(cells, axis=0)))
    total = jnp.zeros((8, channels), f32)
    for y in range(side):
        act = None
        for p in range(pool):
            if 2 * p <= y <= 2 * p + 2:
                act = spread[p] if act is None else act + spread[p]
        grad = (act * slope_ref[y * slab : (y + 1) * slab, :]).astype(bf16)
        d_ref[y * slab : (y + 1) * slab, :] = grad
        total = total + jnp.sum(grad.astype(f32).reshape(-1, 8, channels), axis=0)
    bias_ref[...] = jnp.sum(total, axis=0, keepdims=True)


def kernel_grad(place, slab, xt_ref, d_ref, bias_ref, st_ref, *refs):
    keep_ref, send_ref, scr_ref = refs
    at = place()
    depth = xt_ref.shape[0]
    chips, full, half = keep_ref.shape
    rows = full - EXTRA
    count = d_ref.shape[0]
    for ky in range(3):
        scr_ref[ky * depth : (ky + 1) * depth, :] = jnp.dot(
            xt_ref[:, ky * slab : ky * slab + count], d_ref[...], preferred_element_type=f32
        )
    small = jnp.concatenate([bias_ref[...], st_ref[0:2, :]], axis=0)
    small = jnp.concatenate(
        [small[:, :half], jnp.zeros((1, half), f32), small[:, half:], jnp.zeros((1, half), f32)],
        axis=0,
    )
    high, low = split_high_low(small)
    extra = jnp.concatenate([high.astype(f32), low.astype(f32)], axis=0)
    here = pl.ds(pl.multiple_of(at.core * half, half), half)
    there = pl.ds(pl.multiple_of((1 - at.core) * half, half), half)
    for j in range(chips):
        to = pl.ds(pl.multiple_of(at.chip(j // 2, j % 2) * rows, 16), rows)
        keep_ref[j, 0:rows, :] = scr_ref[to, here]
        send_ref[j, 0:rows, :] = scr_ref[to, there].astype(bf16)
        keep_ref[j, rows:full, :] = extra
        send_ref[j, rows:full, :] = extra.astype(bf16)


def folded(extra):
    value = extra[:8] + extra[8:]
    high, low = split_high_low(value)
    return jnp.concatenate([high.astype(f32), low.astype(f32)], axis=0)


def sum_pieces(keep_ref, got_ref, output_ref, *outs):
    full = keep_ref.shape[1]
    rows = full - EXTRA
    for kz, out in enumerate(outs):
        total = keep_ref[2 * kz + 1] + got_ref[2 * kz + 1].astype(f32)
        out[0:rows, :] = total[:rows].astype(bf16)
        out[rows:full, :] = folded(total[rows:]).astype(bf16)
        out[full:, :] = output_ref[kz]


def sum_three(k, keep_ref, got_ref, came_ref, output_ref, out_ref):
    full = keep_ref.shape[1]
    rows = full - EXTRA
    more = output_ref.shape[1]
    total = keep_ref[2 * k] + got_ref[2 * k].astype(f32)
    total = jnp.concatenate([total[:rows], folded(total[rows:])], axis=0)
    total = total + came_ref[0:full, :].astype(f32)
    out_ref[0:rows, :] = total[:rows].astype(out_ref.dtype)
    out_ref[rows:full, :] = folded(total[rows:]).astype(out_ref.dtype)
    out_ref[full : full + more, :] = output_ref[k].astype(out_ref.dtype)
    out_ref[full + more :, :] = came_ref[full:, :].astype(out_ref.dtype)


def kernel_total(place, *refs):
    parts, (mine_ref, other_ref, pack_ref, keep_ref, scr_ref, small_ref) = refs[:-6], refs[-6:]
    at = place()
    rows, half = scr_ref.shape
    full = rows + EXTRA
    total = None
    riders = []
    for k, part in enumerate(parts):
        value = part[...].astype(f32)
        total = value[:rows] if total is None else total + value[:rows]
        small_ref[k] = value[rows : rows + 8] + value[rows + 8 : full]
        more = (value.shape[0] - full) // 2
        for y in range(2):
            piece = value[full + more * y : full + more * (y + 1)]
            low = [piece[i : i + 8] for i in range(0, more, 16)]
            high = [piece[i + 8 : i + 16] for i in range(0, more, 16)]
            zero = at.core == 0
            keep_ref[2 * k + y] = jnp.concatenate(
                [jnp.where(zero, a, b) for a, b in zip(low, high, strict=True)], axis=1
            )
            riders += [jnp.where(zero, b, a) for a, b in zip(low, high, strict=True)]
    scr_ref[...] = total
    small = None
    for z in range(len(parts)):
        piece = small_ref[lax.rem(at.z + (len(parts) - z), len(parts))]
        small = piece if small is None else small + piece
    high, low = split_high_low(small)
    tail = jnp.zeros((mine_ref.shape[0] - rows // 2 - EXTRA, half), f32)
    for ref, c in ((mine_ref, at.core), (other_ref, 1 - at.core)):
        piece = scr_ref[pl.ds(pl.multiple_of(c * (rows // 2), 8), rows // 2), :]
        value = [high.astype(f32), low.astype(f32), piece] + [tail] * (tail.shape[0] > 0)
        ref[...] = jnp.concatenate(value, axis=0).astype(bf16)
    pack_ref[0 : other_ref.shape[0], :] = other_ref[...]
    pack_ref[other_ref.shape[0] :, :] = jnp.concatenate(riders, axis=0).astype(bf16)


def kernel_finish(place, mine_ref, c_ref, x_ref, xc_ref, grad_ref, bias_ref, stitch_ref):
    at = place()
    rows = grad_ref.shape[1]
    half = grad_ref.shape[2] // 2
    first = at.task == 0
    low_core = at.core == 0

    def lanes(one, two):
        return jnp.concatenate(
            [jnp.where(low_core, one, two), jnp.where(low_core, two, one)], axis=1
        )

    own = lanes(mine_ref[...].astype(f32), c_ref[0 : mine_ref.shape[0], :].astype(f32))
    far = lanes(x_ref[...].astype(f32), xc_ref[...].astype(f32))
    grad_ref[0] = jnp.where(first, own, far)[EXTRA : EXTRA + rows, :]
    grad_ref[1] = jnp.where(first, far, own)[EXTRA : EXTRA + rows, :]

    def small(ref):
        value = ref[...].astype(f32)
        value = value[0:8] + value[8:16]
        return jnp.concatenate([value[0:4], value[4:8]], axis=1)

    own, far = small(mine_ref), small(x_ref)
    bias_ref[0:1, :] = jnp.where(first, own, far)[0:1, :]
    bias_ref[1:2, :] = jnp.where(first, far, own)[0:1, :]
    own_pair = jnp.where(first, own[1:3], jnp.concatenate([own[2:3], own[1:2]], axis=0))
    far_pair = jnp.where(first, jnp.concatenate([far[2:3], far[1:2]], axis=0), far[1:3])
    stitch_ref[0] = jnp.where(first, own_pair, far_pair)
    stitch_ref[1] = jnp.where(first, far_pair, own_pair)


def picture_grad(place, far, side, slab, d_ref, w_ref, out_ref, pad_ref):
    at = place()
    channels = d_ref.shape[1]
    depth = 3 * channels
    block = slab // 2
    first = (1 - at.task if far else at.task) * block
    blank = jnp.zeros((block, depth), bf16)
    pad_ref[0:block, :] = blank
    pad_ref[(side + 1) * block :, :] = blank
    for y in range(side):
        here = pl.ds(pl.multiple_of(y * slab + first, 16), block)
        wide = d_ref[here, :].astype(f32)
        rows = slice((y + 1) * block, (y + 2) * block)
        pad_ref[rows, 0:channels] = pltpu.roll(wide, 1, 0).astype(bf16)
        pad_ref[rows, channels : 2 * channels] = wide.astype(bf16)
        pad_ref[rows, 2 * channels :] = pltpu.roll(wide, block - 1, 0).astype(bf16)
    for start in range(0, side, 7):
        rows = min(7, side - start)
        total = None
        for ky in range(3):
            part = jnp.dot(
                pad_ref[(start + ky) * block : (start + ky + rows) * block, :],
                w_ref[ky * depth : (ky + 1) * depth, :],
                preferred_element_type=f32,
            )
            total = part if total is None else total + part
        for row in range(rows):
            value = total[row * block : (row + 1) * block].astype(bf16)
            out_ref[start + row] = value.reshape(out_ref.shape[1:])


def picture_finish(place, g_ref, own_ref, far_ref, out_ref):
    at = place()
    side, few, _, depth = own_ref.shape
    columns = lax.broadcasted_iota(jnp.int32, (side, depth), 0)
    for n in range(few):
        limit = side - 2 * g_ref[n]
        for y in range(side):
            reach = jnp.where(y < limit, limit, 0)
            mask = jnp.where(columns < reach, 1.0, 0.0).astype(bf16)
            out_ref[n, at.task, y] = own_ref[y, n, 0:side, :] * mask
            out_ref[n, 1 - at.task, y] = far_ref[y, n, 0:side, :] * mask


def fc_grad(place, own_ref, oc_ref, x_ref, xc_ref, d_ref, dx_ref, out_ref):
    at = place()
    same = at.core == at.task
    own = jnp.where(same, own_ref[...], oc_ref[...])
    far = jnp.where(same, x_ref[...], xc_ref[...])
    contract = (((0,), (0,)), ((), ()))
    out_ref[at.task] = lax.dot_general(own, d_ref[...], contract, preferred_element_type=f32)
    rows = d_ref.shape[0]
    d_far = dx_ref[rows // 2 : rows // 2 + rows, :]
    out_ref[1 - at.task] = lax.dot_general(far, d_far, contract, preferred_element_type=f32)


def on_device(pairs, planes, *operands):
    (
        conv_input,
        group,
        conv_weight,
        conv_bias,
        stitch_pool,
        fc_weight,
        fc_bias,
        stitch_fc,
        cotangent,
    ) = operands
    chips = 2 * planes
    place = functools.partial(Place, pairs, planes)
    task = Place(pairs, planes).task
    few = conv_input.shape[0]
    images = 2 * few
    side = conv_input.shape[2]
    channels_in = conv_input.shape[4]
    channels = conv_bias.shape[1]
    pool = (side - 3) // 2 + 1
    units = fc_bias.shape[1]
    features = pool * pool * channels
    part = features // 2
    slab = images * WIDTH
    own_rows = conv_weight.shape[1]
    chip_rows = 2 * own_rows
    half = channels // 2

    def links(where):
        pairs_of = []
        for b in range(2 * pairs):
            for m in range(4 * planes):
                to = where(b, m // 4, (m // 2) % 2, m % 2)
                if to is not None:
                    far_b, z, y, c = to
                    far_m = ((z % planes) * 2 + y) * 2 + c
                    pairs_of.append((b * 4 * planes + m, far_b * 4 * planes + far_m))
        return pairs_of

    def move(value, dx=0, dz=0, dy=0, dc=0):
        where = lambda b, z, y, c: ((b + pairs * dx) % (2 * pairs), z + dz, y ^ dy, c ^ dc)
        return lax.ppermute(value, BOTH, links(where))

    def pick(array, index, axis=0):
        return lax.dynamic_index_in_dim(array, index, axis, keepdims=False)

    def ordered(flag, mine, other, axis=0):
        return jnp.where(
            flag == 0,
            jnp.concatenate([mine, other], axis=axis),
            jnp.concatenate([other, mine], axis=axis),
        )

    def after(value, *others):
        return lax.optimization_barrier((value, *others))[0]

    shifts = []
    for near in range(1, planes // 2 + 1):
        shifts.extend(sorted({near, planes - near}))

    def gather_chips(block):
        rows = [[block, move(block, dy=1)]] + [None] * (planes - 1)
        here = {k: move(block, dz=k) for k in shifts}
        for k in shifts:
            first = after(here[k], rows[0][1]) if k == shifts[0] else here[k]
            rows[k] = [here[k], move(first, dy=1)]
        return [piece for pair in rows for piece in pair]

    weight_mine, weight_other = call(
        functools.partial(split_weights, place),
        (shape_of((own_rows, half), bf16), shape_of((own_rows, half), bf16)),
        (conv_weight,),
    )
    weight_block = call(
        functools.partial(join_cores, place),
        shape_of((chip_rows, half), bf16),
        (weight_mine, move(weight_other, dc=1)),
    )
    wide = (side, few, WIDTH, channels_in)
    picture_own, picture_send, cot_send = call(
        functools.partial(split_inputs, place),
        (
            shape_of(wide, bf16),
            shape_of(wide, bf16),
            shape_of((4 * planes, images, units), bf16),
        ),
        (group, conv_input, cotangent),
        scalars=1,
    )
    picture_far = move(picture_send, dx=1)
    weight_blocks = gather_chips(after(weight_block, picture_send))
    weight_far = [move(block, dc=1) for block in weight_blocks]
    stacked, stacked_t, groups = call(
        functools.partial(widen, place, side),
        (
            shape_of(((side + 2) * slab, 3 * channels_in), bf16),
            shape_of((3 * channels_in, (side + 2) * slab), bf16),
            shape_of((images, channels), f32),
        ),
        (picture_own, picture_far),
    )

    cot_send = after(cot_send, weight_blocks[1])
    cot_own = lax.all_to_all(cot_send, "mp", split_axis=0, concat_axis=0, tiled=True)
    cot_far = move(after(cot_own, picture_far), dx=1)

    window = np.zeros((pool * images, slab), np.float32)
    for q in range(pool):
        for n in range(images):
            window[q * images + n, n * WIDTH + 2 * q : n * WIDTH + 2 * q + 3] = 1.0
    window_t = jnp.asarray(window.T, bf16)
    stacked = after(stacked, stacked_t)
    conv_pre, pooled_mine, pooled_other, kernel = call(
        functools.partial(conv_forward, place, side, pool, images),
        (
            shape_of((side * slab, channels), f32),
            shape_of((images, part), bf16),
            shape_of((images, part), bf16),
            shape_of((chips * chip_rows, channels), bf16),
        ),
        (groups, stacked, conv_bias, *weight_blocks, *weight_far),
        (pltpu.VMEM((pool, channels // 128, slab, 128), f32),),
    )

    pooled_mine = after(pooled_mine, cot_far)
    pooled_x = move(pooled_mine, dx=1)
    pooled_xc = move(pooled_other, dx=1, dc=1)
    pooled_c = move(pooled_other, dc=1)
    pooled = (pooled_mine, pooled_c, pooled_x, pooled_xc)
    piece = (2 * images, part)
    rows_all = chips * 2 * images
    blocks = gather_chips(
        call(functools.partial(stitch_block, place), shape_of(piece, bf16), (*pooled, stitch_pool))
    )

    up = call(
        functools.partial(cot_rows, place),
        shape_of((2, rows_all, units), f32),
        (cot_own, cot_far),
    )

    fc_mine, fc_other = call(
        functools.partial(split_fc, place),
        (shape_of((part, units), bf16), shape_of((part, units), bf16)),
        (after(fc_weight, pooled_mine),),
        (DMA((2,)),),
        blocks=None,
        any_first=True,
    )
    fc_other = move(fc_other, dc=1)

    slope, kernel_back = call(
        slope_and_back,
        (
            shape_of(conv_pre.shape, f32),
            shape_of((9 * channels, channels_in), bf16),
        ),
        (conv_pre, kernel),
    )

    gathered, far_term = call(
        fc_far,
        (shape_of((rows_all, part), bf16), shape_of((rows_all, units), f32)),
        (*blocks, after(fc_other, slope, kernel_back, up)),
    )
    far_back = move(far_term, dc=1)
    own_term = call(fc_own, shape_of((rows_all, units), f32), (gathered, fc_mine))
    d_fc, hidden, x_pack, fc_sums = call(
        functools.partial(fc_middle, place),
        (
            shape_of((rows_all, units), bf16),
            shape_of((rows_all // 2, units), f32),
            shape_of((rows_all // 2 + rows_all + 16, units), bf16),
            shape_of((16, units), f32),
        ),
        (own_term, far_back, fc_bias, stitch_fc, up),
    )
    d_fc_far = move(d_fc, dc=1)
    outs = call(
        fc_back,
        tuple(shape_of(piece, bf16 if j % 2 else f32) for j in range(chips)),
        (d_fc, d_fc_far, fc_mine, fc_other),
    )
    kept, sent = outs[0::2], outs[1::2]

    order = shifts[::-1] + [0]
    arrived = {k: move(sent[k], dy=1) for k in order}
    passed = {}
    for k in order[:-1]:
        low = call(add_rows, (shape_of(piece, bf16),), (kept[k], arrived[k]))[0]
        passed[k] = move(low, dz=-k)
    cross = lambda b, z, y, c: ((b + pairs) % (2 * pairs), z, y, c) if c != b // pairs else None
    features_x = lax.ppermute(gathered, BOTH, links(cross))
    x_came = move(after(x_pack, features_x), dx=1)
    features_c = move(after(gathered, features_x), dc=1)
    d_total, d_mine, d_mine_low, d_other = call(
        functools.partial(block_total, place),
        (
            shape_of(piece, f32),
            shape_of((images, part), f32),
            shape_of((images, part), bf16),
            shape_of((images, part), bf16),
        ),
        (after(kept[0], features_x), arrived[0], *[passed[k] for k in order[:-1]]),
    )

    d_x = move(d_mine_low, dx=1)
    d_xc = move(d_other, dx=1, dc=1)
    d_c = move(d_other, dc=1)
    ride = 2 * images * units // half
    riding = shape_of((planes, ride, half), bf16)
    out_keep, out_send = call(
        functools.partial(mix_output, place),
        (riding, riding),
        (hidden, after(x_came, d_xc), stitch_fc),
    )
    stitch_sums = call(
        functools.partial(stitch_terms, place),
        shape_of((8, channels), f32),
        (after(d_total, d_other), *pooled),
    )
    d_conv, d_bias = call(
        functools.partial(conv_slope, place, side, pool, images),
        (shape_of((side * slab, channels), bf16), shape_of((1, channels), f32)),
        (groups, d_mine, d_c, d_x, d_xc, stitch_pool, slope, window_t),
    )

    full = chip_rows + EXTRA
    stack = (chips, full, half)
    keep, send = call(
        functools.partial(kernel_grad, place, slab),
        (shape_of(stack, f32), shape_of(stack, bf16)),
        (stacked_t, after(d_conv, out_send), d_bias, stitch_sums),
        (pltpu.VMEM((chips * chip_rows, channels), f32),),
    )
    got = move(send, dc=1)
    features_xc = move(after(features_x, d_conv), dc=1)
    thin = (side, few, WIDTH, channels_in)
    pad = (pltpu.VMEM(((side + 2) * slab // 2, 3 * channels), bf16),)
    back_send = call(
        functools.partial(picture_grad, place, True, side, slab),
        shape_of(thin, bf16),
        (after(d_conv, send), kernel_back),
        pad,
    )
    flat = (full + ride, half)
    sent = call(
        sum_pieces,
        tuple(shape_of(flat, bf16) for _ in range(planes)),
        (keep, after(got, back_send, features_c, features_xc), out_send),
    )
    arrived = {k: move(sent[k], dy=1) for k in order}
    parts = {}
    for k in order:
        parts[k] = low = call(
            functools.partial(sum_three, k),
            shape_of((full + 2 * ride, half), bf16 if k else f32),
            (keep, got, arrived[k], out_keep),
        )
        if k:
            last_sum = low
            parts[k] = move(low, dz=-k)
    late = arrived[order[0]]

    back_far = move(back_send, dx=1)
    back_own = call(
        functools.partial(picture_grad, place, False, side, slab),
        shape_of(thin, bf16),
        (after(d_conv, last_sum), kernel_back),
        pad,
    )
    input_grad = call(
        functools.partial(picture_finish, place),
        shape_of(conv_input.shape, bf16),
        (group, back_own, back_far),
        scalars=1,
    )

    def both(own, axis=0):
        own = jnp.expand_dims(own, axis)
        return ordered(task, own, jnp.zeros_like(own), axis=axis)

    d_fc_last = after(d_fc, last_sum)
    steps = 3
    wide_spec = pl.BlockSpec((rows_all, part // steps), lambda i: (0, i))
    whole_spec = [pl.BlockSpec(a.shape, lambda i: (0, 0)) for a in (d_fc, x_came)]
    fc_weight_grad = pl.pallas_call(
        functools.partial(fc_grad, place),
        out_shape=shape_of((2, part, units), f32),
        grid=(steps,),
        in_specs=[wide_spec] * 4 + whole_spec,
        out_specs=pl.BlockSpec((2, part // steps, units), lambda i: (0, i, 0)),
        cost_estimate=cost(fc_grad),
        compiler_params=pltpu.CompilerParams(vmem_limit_bytes=24 * MIB),
    )(gathered, features_c, features_x, features_xc, d_fc_last, x_came)
    tall = -(-(own_rows + EXTRA) // 16) * 16
    k_mine, k_other, k_pack, out_own = call(
        functools.partial(kernel_total, place),
        (
            shape_of((tall, half), bf16),
            shape_of((tall, half), bf16),
            shape_of((tall + chips * ride // 2, half), bf16),
            shape_of((chips, images, units), f32),
        ),
        (after(parts[0], fc_weight_grad, input_grad), *[parts[planes - k] for k in range(1, planes)]),
        (pltpu.VMEM((chip_rows, half), f32), pltpu.VMEM((planes, 8, half), f32)),
    )
    k_x = move(k_mine, dx=1)
    k_xc = move(k_other, dx=1, dc=1)
    k_c = move(k_pack, dc=1)
    output, fc_bias_grad, stitch_fc_grad = call(
        functools.partial(output_finish, place),
        (
            shape_of(cotangent.shape, bf16),
            shape_of((2, units), f32),
            shape_of((2, 2, units), f32),
        ),
        (out_own, k_c, fc_sums, x_came),
        (pltpu.VMEM((images, cotangent.shape[2]), f32),),
    )
    conv_weight_grad, conv_bias_grad, stitch_pool_grad = call(
        functools.partial(kernel_finish, place),
        (
            shape_of((2, own_rows, channels), f32),
            shape_of((2, channels), f32),
            shape_of((2, 2, channels), f32),
        ),
        (k_mine, k_c, k_x, k_xc),
    )

    if pairs > 1:
        fc_weight_grad = lax.psum_scatter(
            ordered(task, fc_weight_grad, jnp.zeros_like(fc_weight_grad), axis=1),
            "batch",
            scatter_dimension=1,
            tiled=True,
        )
        conv_weight_grad, conv_bias_grad, stitch_pool_grad, fc_bias_grad = lax.psum(
            tuple(
                both(pick(value, task))
                for value in (conv_weight_grad, conv_bias_grad, stitch_pool_grad, fc_bias_grad)
            ),
            "batch",
        )
        stitch_fc_grad = lax.psum(both(pick(stitch_fc_grad, task, 1), axis=1), "batch")
    return (
        output,
        input_grad,
        conv_weight_grad,
        conv_bias_grad,
        stitch_pool_grad,
        fc_weight_grad,
        fc_bias_grad,
        stitch_fc_grad,
    )


def solution(mesh):
    pairs = mesh.shape["batch"] // 2
    planes = mesh.shape["mp"] // 4
    in_specs = (
        P(BOTH, None, None, None, None),
        P(BOTH),
        P(None, "mp", None),
        P(),
        P(),
        P(None, None, "mp"),
        P(None, "mp"),
        P(None, None, "mp"),
        P(BOTH, None, None),
    )
    out_specs = (
        P(BOTH, None, None),
        P(BOTH, None, None, None, None),
        P(None, "mp", None),
        P(),
        P(),
        P(None, "batch", "mp"),
        P(None, "mp"),
        P(None, None, "mp"),
    )
    return jax.shard_map(
        functools.partial(on_device, pairs, planes),
        mesh=mesh,
        in_specs=in_specs,
        out_specs=out_specs,
        check_vma=False,
    )
```

```python
import functools

import jax
import jax.numpy as jnp
import numpy as np
from jax import lax
from jax.experimental import pallas as pl
from jax.experimental.pallas import tpu as pltpu
from jax.sharding import PartitionSpec as P

BOTH = ("batch", "mp")
WIDTH = 16
EXTRA = 16
ROOT_HALF = 0.7071067811865476
ROOT_TWO_PI_INV = 0.3989422804014327
VMEM = pl.BlockSpec(memory_space=pltpu.VMEM)
SMEM = pl.BlockSpec(memory_space=pltpu.SMEM)
ANY = pl.BlockSpec(memory_space=pl.ANY)
DMA = pltpu.SemaphoreType.DMA
MIB = 1024 * 1024
FLOPS_PER_US = 1100000000
bf16, f32 = jnp.bfloat16, jnp.float32
shape_of = jax.ShapeDtypeStruct


MICROS = dict(
    split_weights=0.3,
    join_cores=0.3,
    split_fc=1.5,
    split_inputs=1.0,
    cot_cores=0.3,
    cot_join=0.3,
    cot_planes=0.3,
    widen=2,
    conv_forward=7.5,
    stitch_block=0.3,
    cot_rows=0.3,
    slope_and_back=1.7,
    fc_far=0.5,
    fc_own=0.5,
    fc_middle=0.3,
    fc_back=1.6,
    add_rows=0.3,
    block_total=0.3,
    mix_output=0.3,
    stitch_terms=0.3,
    conv_slope=0.6,
    kernel_grad=3.7,
    picture_grad=2.2,
    sum_pieces=0.3,
    sum_three=0.3,
    output_aside=0.3,
    output_cores=0.3,
    picture_finish=0.8,
    output_finish=0.8,
    kernel_total=0.4,
    kernel_finish=0.8,
    fc_grad=4.8,
)


def cost(body):
    name = getattr(body, "func", body).__name__
    return pl.CostEstimate(
        flops=int(MICROS[name] * FLOPS_PER_US), bytes_accessed=1, transcendentals=0
    )


def call(body, out_shape, operands, scratch=(), scalars=0, room=4, blocks=None, any_first=False):
    held = [*operands[scalars + any_first :], *jax.tree.leaves(out_shape), *scratch]
    held = [a for a in held if hasattr(a, "shape") and jnp.issubdtype(a.dtype, jnp.number)]
    need = sum(int(np.prod(a.shape)) * jnp.dtype(a.dtype).itemsize for a in held)
    need = min(need, 40 * MIB)
    steps = {}
    out_specs = jax.tree.map(lambda _: VMEM, out_shape)
    if blocks is not None:
        steps = dict(grid=(1,))
        out_specs = pl.BlockSpec(out_shape.shape, lambda i: (0,) * len(out_shape.shape))
    return pl.pallas_call(
        body,
        out_shape=out_shape,
        **steps,
        in_specs=blocks
        or [SMEM] * scalars + [ANY] * any_first + [VMEM] * (len(operands) - scalars - any_first),
        out_specs=out_specs,
        scratch_shapes=scratch,
        cost_estimate=cost(body),
        compiler_params=pltpu.CompilerParams(vmem_limit_bytes=need * 5 // 4 + room * MIB),
    )(*operands)


class Place:
    def __init__(self, pairs, planes):
        batch_at, mp_at = lax.axis_index("batch"), lax.axis_index("mp")
        self.planes = planes
        self.task = lax.div(batch_at, pairs)
        self.core = lax.rem(mp_at, 2)
        self.y = lax.rem(lax.div(mp_at, 2), 2)
        self.z = lax.div(mp_at, 4)

    def chip(self, kz, ky):
        y = self.y if ky == 0 else 1 - self.y
        return lax.rem(self.z + (self.planes - kz), self.planes) * 2 + y


def phi_cdf(value):
    return 0.5 * (1.0 + lax.erf(value * ROOT_HALF))


def gelu_slope(value):
    return phi_cdf(value) + value * ROOT_TWO_PI_INV * jnp.exp(-0.5 * value * value)


def split_high_low(value):
    high = value.astype(bf16)
    return high, (value - high.astype(f32)).astype(bf16)


def window_sum(q_ref, value):
    high, low = split_high_low(value)
    return jnp.dot(q_ref[...], high, preferred_element_type=f32) + jnp.dot(
        q_ref[...], low, preferred_element_type=f32
    )


def split_weights(place, w_ref, mine_ref, other_ref):
    at = place()
    half = mine_ref.shape[1]
    for ref, core in ((mine_ref, at.core), (other_ref, 1 - at.core)):
        lanes = pl.ds(pl.multiple_of(core * half, half), half)
        ref[...] = w_ref[at.task, :, lanes]


def join_cores(place, mine_ref, other_ref, out_ref):
    at = place()
    mine, other = mine_ref[...].astype(f32), other_ref[...].astype(f32)
    low, high = jnp.where(at.core == 0, mine, other), jnp.where(at.core == 0, other, mine)
    out_ref[...] = jnp.concatenate([low, high], axis=0).astype(bf16)


def split_fc(place, w_ref, mine_ref, other_ref, sems):
    at = place()
    part = mine_ref.shape[0]
    copies = []
    for i, (ref, core) in enumerate(((mine_ref, at.core), (other_ref, 1 - at.core))):
        rows = pl.ds(pl.multiple_of(core * part, part), part)
        copies.append(pltpu.make_async_copy(w_ref.at[at.task, rows, :], ref, sems.at[i]))
        copies[-1].start()
    for copy in copies:
        copy.wait()


def split_inputs(place, g_ref, x_ref, cot_ref, own_ref, far_ref, out_ref):
    at = place()
    few, _, side, _, depth = x_ref.shape
    units = out_ref.shape[2]
    columns = lax.broadcasted_iota(jnp.int32, (side, depth), 0)
    value = cot_ref[...].astype(f32)
    rows = jnp.concatenate([value[i, t : t + 1] for t in range(2) for i in range(few)], axis=0)
    for ref in (own_ref, far_ref):
        ref[...] = jnp.zeros_like(ref)
    for n in range(few):
        limit = side - 2 * g_ref[n]
        mark = jnp.broadcast_to(g_ref[n], (1, depth)).astype(f32)
        for y in range(side):
            reach = jnp.where(y < limit, limit, 0)
            mask = jnp.where(columns < reach, 1.0, 0.0).astype(bf16)
            for ref, task in ((own_ref, at.task), (far_ref, 1 - at.task)):
                picture = x_ref[n, task, y] * mask
                if y:
                    ref[y, n, 0:side, :] = picture
                else:
                    gap = jnp.zeros((WIDTH - side - 1, depth), f32)
                    ref[y, n] = jnp.concatenate(
                        [picture.astype(f32), gap, mark], axis=0
                    ).astype(bf16)
    for m in range(out_ref.shape[0]):
        out_ref[m] = rows[:, m * units : (m + 1) * units].astype(bf16)


def widen(place, side, own_ref, far_ref, x3_ref, xt_ref, group_ref):
    at = place()
    _, few, _, depth = own_ref.shape
    channels = group_ref.shape[1]
    marks = []
    for ref in (own_ref, far_ref):
        last = [ref[0, n].astype(f32)[WIDTH - 1 :, :channels] for n in range(few)]
        marks.append(jnp.concatenate(last, axis=0))
    group_ref[...] = jnp.where(
        at.task == 0, jnp.concatenate(marks, axis=0), jnp.concatenate(marks[::-1], axis=0)
    )
    inside = lax.rem(lax.broadcasted_iota(jnp.int32, (few * WIDTH, depth), 0), WIDTH) < side
    block = few * WIDTH
    slab = 2 * block
    for edge in (0, side + 1):
        x3_ref[edge * slab : (edge + 1) * slab, :] = jnp.zeros((slab, 3 * depth), bf16)
        xt_ref[:, edge * slab : (edge + 1) * slab] = jnp.zeros((3 * depth, slab), bf16)
    for y in range(side):
        own = own_ref[y].reshape(block, depth).astype(f32)
        far = far_ref[y].reshape(block, depth).astype(f32)
        first = at.task == 0
        if y == 0:
            own, far = jnp.where(inside, own, 0.0), jnp.where(inside, far, 0.0)
        wide = jnp.concatenate(
            [jnp.where(first, own, far), jnp.where(first, far, own)], axis=0
        )
        rows = slice((y + 1) * slab, (y + 2) * slab)
        turned = wide.T
        for kx in range(3):
            lanes = slice(kx * depth, (kx + 1) * depth)
            shift = (1 - kx) % slab
            x3_ref[rows, lanes] = (pltpu.roll(wide, shift, 0) if shift else wide).astype(bf16)
            xt_ref[lanes, rows] = (pltpu.roll(turned, shift, 1) if shift else turned).astype(bf16)


def conv_forward(place, side, pool, images, *refs):
    g_ref, x_ref, b_ref = refs[:3]
    blocks = refs[3:-5]
    pre_ref, mine_ref, other_ref, w_ref, sum_ref = refs[-5:]
    at = place()
    chips = len(blocks) // 2
    rows, half = blocks[0].shape
    here = pl.ds(pl.multiple_of(at.core * half, half), half)
    there = pl.ds(pl.multiple_of((1 - at.core) * half, half), half)
    for j in range(chips):
        to = pl.ds(pl.multiple_of(at.chip(j // 2, j % 2) * rows, 16), rows)
        w_ref[to, here] = blocks[j][...]
        w_ref[to, there] = blocks[chips + j][...]
    slab = images * WIDTH
    depth = x_ref.shape[1]
    channels = w_ref.shape[1]
    acts, pooled = {}, {}
    bias = jnp.where(at.task == 0, b_ref[0:1, :], b_ref[1:2, :])
    group = g_ref[...]
    for start in range(0, side, 4):
        rows = min(4, side - start)
        total = None
        for ky in range(3):
            part = jnp.dot(
                x_ref[(start + ky) * slab : (start + ky + rows) * slab, :],
                w_ref[ky * depth : (ky + 1) * depth, :],
                preferred_element_type=f32,
            )
            total = part if total is None else total + part
        total = total + bias
        pre_ref[start * slab : (start + rows) * slab, :] = total
        act = total * phi_cdf(total)
        for row in range(rows):
            acts[start + row] = act[row * slab : (row + 1) * slab, :]
        for p in range(pool):
            if not (start <= 2 * p + 2 < start + rows):
                continue
            rows_sum = acts[2 * p] + acts[2 * p + 1] + acts[2 * p + 2]
            for tile in range(channels // 128):
                sum_ref[p, tile, 0:slab, :] = rows_sum[:, tile * 128 : (tile + 1) * 128]
            for q in range(pool):
                kept = jnp.where(max(p, q) + group < pool, 1.0 / 9.0, 0.0)
                cell = None
                for x in range(2 * q, 2 * q + 3):
                    spot = pl.ds(x, images, stride=WIDTH)
                    column = jnp.concatenate(
                        [sum_ref[p, tile, spot, :] for tile in range(channels // 128)], axis=1
                    )
                    cell = column if cell is None else cell + column
                pooled[p, q] = cell * kept
    low = at.core == 0
    for p in range(pool // 2):
        for q in range(pool):
            zero, one = pooled[p, q], pooled[p + pool // 2, q]
            lanes = slice((p * pool + q) * channels, (p * pool + q + 1) * channels)
            mine_ref[:, lanes] = jnp.where(low, zero, one).astype(bf16)
            other_ref[:, lanes] = jnp.where(low, one, zero).astype(bf16)


def slope_and_back(pre_ref, w_ref, slope_ref, back_ref):
    slope_ref[...] = gelu_slope(pre_ref[...])
    taps = 9
    depth = w_ref.shape[0] // taps
    channels = w_ref.shape[1]
    for tap in range(taps):
        far = taps - 1 - tap
        back_ref[tap * channels : (tap + 1) * channels, :] = (
            w_ref[far * depth : (far + 1) * depth, :].astype(f32).T.astype(bf16)
        )


def cot_rows(place, own_ref, far_ref, up_ref):
    at = place()
    first = at.task == 0
    low_rows = lax.broadcasted_iota(jnp.int32, own_ref.shape[1:], 0) < 4
    for j in range(own_ref.shape[0] // 2):
        chip = at.chip(j // 2, j % 2)
        for c in range(2):
            own = own_ref[2 * chip + c].astype(f32)
            far = far_ref[2 * chip + c].astype(f32)
            low = jnp.where(first, own, far)
            high = jnp.where(first, far, own)
            zero = jnp.where(low_rows, low, pltpu.roll(high, 4, 0))
            one = jnp.where(low_rows, pltpu.roll(low, 4, 0), high)
            here = slice((2 * j + c) * 8, (2 * j + c + 1) * 8)
            up_ref[0, here, :] = jnp.where(first, zero, one)
            up_ref[1, here, :] = jnp.where(first, one, zero)


def stitch_mix(at, ref, t, u):
    row = ref[t]
    return jnp.where(u == 0, row[0:1, :], row[1:2, :])


def core_rows(at, mine, other):
    mine, other = mine.astype(f32), other.astype(f32)
    first = at.core == 0
    return jnp.concatenate(
        [jnp.where(first, mine, other), jnp.where(first, other, mine)], axis=0
    )


def stitch_block(place, mine_ref, c_ref, x_ref, xc_ref, st_ref, out_ref):
    at = place()
    channels = st_ref.shape[2]
    near = stitch_mix(at, st_ref, at.task, at.task)
    far = stitch_mix(at, st_ref, at.task, 1 - at.task)
    for cell in range(out_ref.shape[1] // channels):
        lanes = slice(cell * channels, (cell + 1) * channels)
        own = core_rows(at, mine_ref[:, lanes], c_ref[:, lanes])
        other = core_rows(at, x_ref[:, lanes], xc_ref[:, lanes])
        out_ref[:, lanes] = (near * own + far * other).astype(bf16)


def fc_far(*refs):
    blocks = refs[:-3]
    w_ref, all_ref, out_ref = refs[-3:]
    rows = blocks[0].shape[0]
    for j, block in enumerate(blocks):
        all_ref[j * rows : (j + 1) * rows, :] = block[...]
    out_ref[...] = jnp.dot(all_ref[...], w_ref[...], preferred_element_type=f32)


def fc_own(x_ref, w_ref, out_ref):
    out_ref[...] = jnp.dot(x_ref[...], w_ref[...], preferred_element_type=f32)


def four_rows(task, value, groups):
    rows = lax.broadcasted_iota(jnp.int32, (8, value.shape[1]), 0) < 4
    packed = []
    for g in range(0, groups, 2):
        one, two = value[g * 8 : g * 8 + 8], value[g * 8 + 8 : g * 8 + 16]
        zero = jnp.where(rows, one, pltpu.roll(two, 4, 0))
        last = jnp.where(rows, pltpu.roll(one, 4, 0), two)
        packed.append(jnp.where(task == 0, zero, last))
    return jnp.concatenate(packed, axis=0)


def fc_middle(
    place, own_ref, back_ref, bias_ref, mix_ref, up_ref, d_ref, hidden_ref, pack_ref, sums_ref
):
    at = place()
    first = at.task == 0
    bias = jnp.where(first, bias_ref[0:1, :], bias_ref[1:2, :])
    pre = own_ref[...] + back_ref[...] + bias
    cdf = phi_cdf(pre)
    hidden = pre * cdf
    groups = hidden.shape[0] // 8
    hidden_ref[...] = four_rows(at.task, hidden, groups)
    slope = cdf + pre * ROOT_TWO_PI_INV * jnp.exp(-0.5 * pre * pre)
    mine, other = up_ref[0], up_ref[1]
    d_hidden = stitch_mix(at, mix_ref, at.task, at.task) * mine
    d_hidden += stitch_mix(at, mix_ref, 1 - at.task, at.task) * other
    d_fc = (slope * d_hidden).astype(bf16)
    d_ref[...] = d_fc
    by_mine = jnp.sum(mine * hidden, axis=0, keepdims=True)
    by_other = jnp.sum(other * hidden, axis=0, keepdims=True)
    sums = jnp.concatenate(
        [
            jnp.sum(d_fc.astype(f32), axis=0, keepdims=True),
            jnp.where(first, by_mine, by_other),
            jnp.where(first, by_other, by_mine),
            jnp.zeros((5, by_mine.shape[1]), f32),
        ],
        axis=0,
    )
    high, low = split_high_low(sums)
    sums = jnp.concatenate([high.astype(f32), low.astype(f32)], axis=0)
    sums_ref[...] = sums
    rows = d_ref.shape[0]
    pack_ref[0 : rows // 2, :] = four_rows(1 - at.task, hidden, groups).astype(bf16)
    pack_ref[rows // 2 : rows // 2 + rows, :] = d_fc
    pack_ref[rows // 2 + rows :, :] = sums.astype(bf16)


def folded_lanes(value, lanes):
    return jnp.concatenate(
        [value[:, at : at + lanes] for at in range(0, value.shape[1], lanes)], axis=0
    )


def mix_output(place, own_ref, far_ref, mix_ref, keep_ref, send_ref):
    at = place()
    rows = lax.broadcasted_iota(jnp.int32, (8, own_ref.shape[1]), 0) < 4
    own_all = own_ref[...]
    far_all = far_ref[0 : own_all.shape[0], :].astype(f32)
    sums = []
    for t in range(2):
        sums.append(
            stitch_mix(at, mix_ref, t, at.task) * own_all
            + stitch_mix(at, mix_ref, t, 1 - at.task) * far_all
        )
    for kz in range(keep_ref.shape[0]):
        for ky, out in enumerate((keep_ref, send_ref)):
            here = slice((2 * kz + ky) * 8, (2 * kz + ky) * 8 + 8)
            zero, one = sums[0][here], sums[1][here]
            value = jnp.concatenate(
                [
                    jnp.where(rows, zero, pltpu.roll(one, 4, 0)),
                    jnp.where(rows, pltpu.roll(zero, 4, 0), one),
                ],
                axis=0,
            )
            out[kz] = folded_lanes(value, out.shape[2]).astype(bf16)


def output_finish(place, keep_ref, came_ref, sums_ref, far_ref, out_ref, bias_ref, st_ref, all_ref):
    at = place()
    units = keep_ref.shape[2]
    folds = units // came_ref.shape[1]
    first_row = came_ref.shape[0] - 8 * folds * keep_ref.shape[0]
    came_all = came_ref[first_row:, :].astype(f32)
    for j in range(keep_ref.shape[0]):
        chip = at.chip(j // 2, j % 2)
        mine = pl.ds(pl.multiple_of((2 * chip + at.core) * units, units), units)
        all_ref[:, mine] = keep_ref[j]
        other = pl.ds(pl.multiple_of((2 * chip + 1 - at.core) * units, units), units)
        rows = [8 * (folds * j + f) for f in range(folds)]
        all_ref[:, other] = jnp.concatenate([came_all[i : i + 8] for i in rows], axis=1)
    for i in range(4):
        out_ref[i] = jnp.concatenate(
            [all_ref[i : i + 1, :], all_ref[4 + i : 5 + i, :]], axis=0
        ).astype(bf16)
    first = at.task == 0
    own, far = sums_ref[...], far_ref[far_ref.shape[0] - 16 :, :].astype(f32)
    own, far = own[0:8] + own[8:16], far[0:8] + far[8:16]
    zero, one = jnp.where(first, own, far), jnp.where(first, far, own)
    bias_ref[0:1, :] = zero[0:1]
    bias_ref[1:2, :] = one[0:1]
    for t in range(2):
        st_ref[t] = jnp.concatenate([zero[1 + t : 2 + t], one[1 + t : 2 + t]], axis=0)


def fc_back(d_ref, far_ref, w_ref, wf_ref, *outs):
    chips = len(outs)
    rows = outs[0].shape[0]
    contract = (((1,), (1,)), ((), ()))
    total = lax.dot_general(d_ref[...], w_ref[...], contract, preferred_element_type=f32)
    total += lax.dot_general(far_ref[...], wf_ref[...], contract, preferred_element_type=f32)
    for j, out in enumerate(outs):
        out[...] = total[j * rows : (j + 1) * rows, :].astype(out.dtype)


def add_rows(keep_ref, got_ref, *outs):
    total = keep_ref[...] + got_ref[...].astype(f32)
    for out in outs:
        out[...] = total.astype(out.dtype)


def block_total(place, keep_ref, *refs):
    at = place()
    total_ref, mine_ref, mine_low_ref, other_ref = refs[-4:]
    total = keep_ref[...]
    for ref in refs[:-4]:
        total = total + ref[...].astype(f32)
    total_ref[...] = total
    images = mine_ref.shape[0]
    low, high = total[:images], total[images:]
    mine = jnp.where(at.core == 0, low, high)
    mine_ref[...] = mine
    mine_low_ref[...] = mine.astype(bf16)
    other_ref[...] = jnp.where(at.core == 0, high, low).astype(bf16)


def stitch_terms(place, total_ref, mine_ref, c_ref, x_ref, xc_ref, out_ref):
    at = place()
    channels = out_ref.shape[1]
    own = far = None
    for cell in range(total_ref.shape[1] // channels):
        lanes = slice(cell * channels, (cell + 1) * channels)
        grad = total_ref[:, lanes]
        one = grad * core_rows(at, mine_ref[:, lanes], c_ref[:, lanes])
        two = grad * core_rows(at, x_ref[:, lanes], xc_ref[:, lanes])
        own = one if own is None else own + one
        far = two if far is None else far + two
    out_ref[...] = jnp.concatenate(
        [
            jnp.sum(own, axis=0, keepdims=True),
            jnp.sum(far, axis=0, keepdims=True),
            jnp.zeros((6, channels), f32),
        ],
        axis=0,
    )


def conv_slope(place, side, pool, images, *refs):
    (g_ref, mine_ref, c_ref, x_ref, xc_ref, st_ref, slope_ref, q_ref) = refs[:8]
    d_ref, bias_ref = refs[8:]
    at = place()
    slab = images * WIDTH
    channels = slope_ref.shape[1]
    group = g_ref[...]

    near = stitch_mix(at, st_ref, at.task, at.task)
    far = stitch_mix(at, st_ref, 1 - at.task, at.task)
    spread = []
    for p in range(pool):
        mine_here = at.core == (2 * p) // pool
        cells = []
        for q in range(pool):
            lanes = ((p % (pool // 2)) * pool + q) * channels
            lanes = slice(lanes, lanes + channels)
            kept = jnp.where(max(p, q) + group < pool, 1.0 / 9.0, 0.0)
            one = near * mine_ref[:, lanes] + far * x_ref[:, lanes].astype(f32)
            two = near * c_ref[:, lanes].astype(f32) + far * xc_ref[:, lanes].astype(f32)
            cells.append(jnp.where(mine_here, one, two) * kept)
        spread.append(window_sum(q_ref, jnp.concatenate(cells, axis=0)))
    total = jnp.zeros((8, channels), f32)
    for y in range(side):
        act = None
        for p in range(pool):
            if 2 * p <= y <= 2 * p + 2:
                act = spread[p] if act is None else act + spread[p]
        grad = (act * slope_ref[y * slab : (y + 1) * slab, :]).astype(bf16)
        d_ref[y * slab : (y + 1) * slab, :] = grad
        total = total + jnp.sum(grad.astype(f32).reshape(-1, 8, channels), axis=0)
    bias_ref[...] = jnp.sum(total, axis=0, keepdims=True)


def kernel_grad(place, slab, xt_ref, d_ref, bias_ref, st_ref, *refs):
    keep_ref, send_ref, scr_ref = refs
    at = place()
    depth = xt_ref.shape[0]
    chips, full, half = keep_ref.shape
    rows = full - EXTRA
    count = d_ref.shape[0]
    for ky in range(3):
        scr_ref[ky * depth : (ky + 1) * depth, :] = jnp.dot(
            xt_ref[:, ky * slab : ky * slab + count], d_ref[...], preferred_element_type=f32
        )
    small = jnp.concatenate([bias_ref[...], st_ref[0:2, :]], axis=0)
    small = jnp.concatenate(
        [small[:, :half], jnp.zeros((1, half), f32), small[:, half:], jnp.zeros((1, half), f32)],
        axis=0,
    )
    high, low = split_high_low(small)
    extra = jnp.concatenate([high.astype(f32), low.astype(f32)], axis=0)
    here = pl.ds(pl.multiple_of(at.core * half, half), half)
    there = pl.ds(pl.multiple_of((1 - at.core) * half, half), half)
    for j in range(chips):
        to = pl.ds(pl.multiple_of(at.chip(j // 2, j % 2) * rows, 16), rows)
        keep_ref[j, 0:rows, :] = scr_ref[to, here]
        send_ref[j, 0:rows, :] = scr_ref[to, there].astype(bf16)
        keep_ref[j, rows:full, :] = extra
        send_ref[j, rows:full, :] = extra.astype(bf16)


def folded(extra):
    value = extra[:8] + extra[8:]
    high, low = split_high_low(value)
    return jnp.concatenate([high.astype(f32), low.astype(f32)], axis=0)


def sum_pieces(keep_ref, got_ref, output_ref, *outs):
    full = keep_ref.shape[1]
    rows = full - EXTRA
    for kz, out in enumerate(outs):
        total = keep_ref[2 * kz + 1] + got_ref[2 * kz + 1].astype(f32)
        out[0:rows, :] = total[:rows].astype(bf16)
        out[rows:full, :] = folded(total[rows:]).astype(bf16)
        out[full:, :] = output_ref[kz]


def sum_three(k, keep_ref, got_ref, came_ref, output_ref, out_ref):
    full = keep_ref.shape[1]
    rows = full - EXTRA
    more = output_ref.shape[1]
    total = keep_ref[2 * k] + got_ref[2 * k].astype(f32)
    total = jnp.concatenate([total[:rows], folded(total[rows:])], axis=0)
    total = total + came_ref[0:full, :].astype(f32)
    out_ref[0:rows, :] = total[:rows].astype(out_ref.dtype)
    out_ref[rows:full, :] = folded(total[rows:]).astype(out_ref.dtype)
    out_ref[full : full + more, :] = output_ref[k].astype(out_ref.dtype)
    out_ref[full + more :, :] = came_ref[full:, :].astype(out_ref.dtype)


def kernel_total(place, *refs):
    parts, (mine_ref, other_ref, pack_ref, keep_ref, scr_ref, small_ref) = refs[:-6], refs[-6:]
    at = place()
    rows, half = scr_ref.shape
    full = rows + EXTRA
    total = None
    riders = []
    for k, part in enumerate(parts):
        value = part[...].astype(f32)
        total = value[:rows] if total is None else total + value[:rows]
        small_ref[k] = value[rows : rows + 8] + value[rows + 8 : full]
        more = (value.shape[0] - full) // 2
        for y in range(2):
            piece = value[full + more * y : full + more * (y + 1)]
            low = [piece[i : i + 8] for i in range(0, more, 16)]
            high = [piece[i + 8 : i + 16] for i in range(0, more, 16)]
            zero = at.core == 0
            keep_ref[2 * k + y] = jnp.concatenate(
                [jnp.where(zero, a, b) for a, b in zip(low, high, strict=True)], axis=1
            )
            riders += [jnp.where(zero, b, a) for a, b in zip(low, high, strict=True)]
    scr_ref[...] = total
    small = None
    for z in range(len(parts)):
        piece = small_ref[lax.rem(at.z + (len(parts) - z), len(parts))]
        small = piece if small is None else small + piece
    high, low = split_high_low(small)
    tail = jnp.zeros((mine_ref.shape[0] - rows // 2 - EXTRA, half), f32)
    for ref, c in ((mine_ref, at.core), (other_ref, 1 - at.core)):
        piece = scr_ref[pl.ds(pl.multiple_of(c * (rows // 2), 8), rows // 2), :]
        value = [high.astype(f32), low.astype(f32), piece] + [tail] * (tail.shape[0] > 0)
        ref[...] = jnp.concatenate(value, axis=0).astype(bf16)
    pack_ref[0 : other_ref.shape[0], :] = other_ref[...]
    pack_ref[other_ref.shape[0] :, :] = jnp.concatenate(riders, axis=0).astype(bf16)


def kernel_finish(place, mine_ref, c_ref, x_ref, xc_ref, grad_ref, bias_ref, stitch_ref):
    at = place()
    rows = grad_ref.shape[1]
    half = grad_ref.shape[2] // 2
    first = at.task == 0
    low_core = at.core == 0

    def lanes(one, two):
        return jnp.concatenate(
            [jnp.where(low_core, one, two), jnp.where(low_core, two, one)], axis=1
        )

    own = lanes(mine_ref[...].astype(f32), c_ref[0 : mine_ref.shape[0], :].astype(f32))
    far = lanes(x_ref[...].astype(f32), xc_ref[...].astype(f32))
    grad_ref[0] = jnp.where(first, own, far)[EXTRA : EXTRA + rows, :]
    grad_ref[1] = jnp.where(first, far, own)[EXTRA : EXTRA + rows, :]

    def small(ref):
        value = ref[...].astype(f32)
        value = value[0:8] + value[8:16]
        return jnp.concatenate([value[0:4], value[4:8]], axis=1)

    own, far = small(mine_ref), small(x_ref)
    bias_ref[0:1, :] = jnp.where(first, own, far)[0:1, :]
    bias_ref[1:2, :] = jnp.where(first, far, own)[0:1, :]
    own_pair = jnp.where(first, own[1:3], jnp.concatenate([own[2:3], own[1:2]], axis=0))
    far_pair = jnp.where(first, jnp.concatenate([far[2:3], far[1:2]], axis=0), far[1:3])
    stitch_ref[0] = jnp.where(first, own_pair, far_pair)
    stitch_ref[1] = jnp.where(first, far_pair, own_pair)


def picture_grad(place, far, side, slab, d_ref, w_ref, out_ref, pad_ref):
    at = place()
    channels = d_ref.shape[1]
    depth = 3 * channels
    block = slab // 2
    first = (1 - at.task if far else at.task) * block
    blank = jnp.zeros((block, depth), bf16)
    pad_ref[0:block, :] = blank
    pad_ref[(side + 1) * block :, :] = blank
    for y in range(side):
        here = pl.ds(pl.multiple_of(y * slab + first, 16), block)
        wide = d_ref[here, :].astype(f32)
        rows = slice((y + 1) * block, (y + 2) * block)
        pad_ref[rows, 0:channels] = pltpu.roll(wide, 1, 0).astype(bf16)
        pad_ref[rows, channels : 2 * channels] = wide.astype(bf16)
        pad_ref[rows, 2 * channels :] = pltpu.roll(wide, block - 1, 0).astype(bf16)
    for start in range(0, side, 7):
        rows = min(7, side - start)
        total = None
        for ky in range(3):
            part = jnp.dot(
                pad_ref[(start + ky) * block : (start + ky + rows) * block, :],
                w_ref[ky * depth : (ky + 1) * depth, :],
                preferred_element_type=f32,
            )
            total = part if total is None else total + part
        for row in range(rows):
            value = total[row * block : (row + 1) * block].astype(bf16)
            out_ref[start + row] = value.reshape(out_ref.shape[1:])


def picture_finish(place, g_ref, own_ref, far_ref, out_ref):
    at = place()
    side, few, _, depth = own_ref.shape
    columns = lax.broadcasted_iota(jnp.int32, (side, depth), 0)
    for n in range(few):
        limit = side - 2 * g_ref[n]
        for y in range(side):
            reach = jnp.where(y < limit, limit, 0)
            mask = jnp.where(columns < reach, 1.0, 0.0).astype(bf16)
            out_ref[n, at.task, y] = own_ref[y, n, 0:side, :] * mask
            out_ref[n, 1 - at.task, y] = far_ref[y, n, 0:side, :] * mask


def fc_grad(place, own_ref, oc_ref, x_ref, xc_ref, d_ref, dx_ref, out_ref):
    at = place()
    same = at.core == at.task
    own = jnp.where(same, own_ref[...], oc_ref[...])
    far = jnp.where(same, x_ref[...], xc_ref[...])
    contract = (((0,), (0,)), ((), ()))
    out_ref[at.task] = lax.dot_general(own, d_ref[...], contract, preferred_element_type=f32)
    rows = d_ref.shape[0]
    d_far = dx_ref[rows // 2 : rows // 2 + rows, :]
    out_ref[1 - at.task] = lax.dot_general(far, d_far, contract, preferred_element_type=f32)


def on_device(pairs, planes, *operands):
    (
        conv_input,
        group,
        conv_weight,
        conv_bias,
        stitch_pool,
        fc_weight,
        fc_bias,
        stitch_fc,
        cotangent,
    ) = operands
    chips = 2 * planes
    place = functools.partial(Place, pairs, planes)
    task = Place(pairs, planes).task
    few = conv_input.shape[0]
    images = 2 * few
    side = conv_input.shape[2]
    channels_in = conv_input.shape[4]
    channels = conv_bias.shape[1]
    pool = (side - 3) // 2 + 1
    units = fc_bias.shape[1]
    features = pool * pool * channels
    part = features // 2
    slab = images * WIDTH
    own_rows = conv_weight.shape[1]
    chip_rows = 2 * own_rows
    half = channels // 2

    def links(where):
        pairs_of = []
        for b in range(2 * pairs):
            for m in range(4 * planes):
                to = where(b, m // 4, (m // 2) % 2, m % 2)
                if to is not None:
                    far_b, z, y, c = to
                    far_m = ((z % planes) * 2 + y) * 2 + c
                    pairs_of.append((b * 4 * planes + m, far_b * 4 * planes + far_m))
        return pairs_of

    def move(value, dx=0, dz=0, dy=0, dc=0):
        where = lambda b, z, y, c: ((b + pairs * dx) % (2 * pairs), z + dz, y ^ dy, c ^ dc)
        return lax.ppermute(value, BOTH, links(where))

    def pick(array, index, axis=0):
        return lax.dynamic_index_in_dim(array, index, axis, keepdims=False)

    def ordered(flag, mine, other, axis=0):
        return jnp.where(
            flag == 0,
            jnp.concatenate([mine, other], axis=axis),
            jnp.concatenate([other, mine], axis=axis),
        )

    def after(value, *others):
        return lax.optimization_barrier((value, *others))[0]

    shifts = []
    for near in range(1, planes // 2 + 1):
        shifts.extend(sorted({near, planes - near}))

    def gather_chips(block):
        rows = [[block, move(block, dy=1)]] + [None] * (planes - 1)
        here = {k: move(block, dz=k) for k in shifts}
        for k in shifts:
            first = after(here[k], rows[0][1]) if k == shifts[0] else here[k]
            rows[k] = [here[k], move(first, dy=1)]
        return [piece for pair in rows for piece in pair]

    weight_mine, weight_other = call(
        functools.partial(split_weights, place),
        (shape_of((own_rows, half), bf16), shape_of((own_rows, half), bf16)),
        (conv_weight,),
    )
    weight_block = call(
        functools.partial(join_cores, place),
        shape_of((chip_rows, half), bf16),
        (weight_mine, move(weight_other, dc=1)),
    )
    wide = (side, few, WIDTH, channels_in)
    picture_own, picture_send, cot_send = call(
        functools.partial(split_inputs, place),
        (
            shape_of(wide, bf16),
            shape_of(wide, bf16),
            shape_of((4 * planes, images, units), bf16),
        ),
        (after(group, weight_block), conv_input, cotangent),
        scalars=1,
    )
    picture_far = move(picture_send, dx=1)
    weight_blocks = gather_chips(weight_block)
    weight_far = [move(block, dc=1) for block in weight_blocks]
    stacked, stacked_t, groups = call(
        functools.partial(widen, place, side),
        (
            shape_of(((side + 2) * slab, 3 * channels_in), bf16),
            shape_of((3 * channels_in, (side + 2) * slab), bf16),
            shape_of((images, channels), f32),
        ),
        (picture_own, picture_far),
    )

    cot_send = after(cot_send, weight_blocks[1])
    cot_own = lax.all_to_all(cot_send, "mp", split_axis=0, concat_axis=0, tiled=True)
    cot_far = move(after(cot_own, picture_far), dx=1)

    window = np.zeros((pool * images, slab), np.float32)
    for q in range(pool):
        for n in range(images):
            window[q * images + n, n * WIDTH + 2 * q : n * WIDTH + 2 * q + 3] = 1.0
    window_t = jnp.asarray(window.T, bf16)
    stacked = after(stacked, stacked_t)
    conv_pre, pooled_mine, pooled_other, kernel = call(
        functools.partial(conv_forward, place, side, pool, images),
        (
            shape_of((side * slab, channels), f32),
            shape_of((images, part), bf16),
            shape_of((images, part), bf16),
            shape_of((chips * chip_rows, channels), bf16),
        ),
        (groups, stacked, conv_bias, *weight_blocks, *weight_far),
        (pltpu.VMEM((pool, channels // 128, slab + WIDTH, 128), f32),),
    )

    pooled_mine = after(pooled_mine, cot_far)
    pooled_x = move(pooled_mine, dx=1)
    pooled_xc = move(pooled_other, dx=1, dc=1)
    pooled_c = move(pooled_other, dc=1)
    pooled = (pooled_mine, pooled_c, pooled_x, pooled_xc)
    piece = (2 * images, part)
    rows_all = chips * 2 * images
    blocks = gather_chips(
        call(functools.partial(stitch_block, place), shape_of(piece, bf16), (*pooled, stitch_pool))
    )

    up = call(
        functools.partial(cot_rows, place),
        shape_of((2, rows_all, units), f32),
        (cot_own, cot_far),
    )

    fc_mine, fc_other = call(
        functools.partial(split_fc, place),
        (shape_of((part, units), bf16), shape_of((part, units), bf16)),
        (after(fc_weight, pooled_mine),),
        (DMA((2,)),),
        blocks=None,
        any_first=True,
    )
    fc_other = move(fc_other, dc=1)

    slope, kernel_back = call(
        slope_and_back,
        (
            shape_of(conv_pre.shape, f32),
            shape_of((9 * channels, channels_in), bf16),
        ),
        (conv_pre, kernel),
    )

    gathered, far_term = call(
        fc_far,
        (shape_of((rows_all, part), bf16), shape_of((rows_all, units), f32)),
        (*blocks, after(fc_other, slope, kernel_back, up)),
    )
    far_back = move(far_term, dc=1)
    own_term = call(fc_own, shape_of((rows_all, units), f32), (gathered, fc_mine))
    d_fc, hidden, x_pack, fc_sums = call(
        functools.partial(fc_middle, place),
        (
            shape_of((rows_all, units), bf16),
            shape_of((rows_all // 2, units), f32),
            shape_of((rows_all // 2 + rows_all + 16, units), bf16),
            shape_of((16, units), f32),
        ),
        (own_term, far_back, fc_bias, stitch_fc, up),
    )
    d_fc_far = move(d_fc, dc=1)
    outs = call(
        fc_back,
        tuple(shape_of(piece, bf16 if j % 2 else f32) for j in range(chips)),
        (d_fc, d_fc_far, fc_mine, fc_other),
    )
    kept, sent = outs[0::2], outs[1::2]

    order = shifts[::-1] + [0]
    arrived = {k: move(sent[k], dy=1) for k in order}
    passed = {}
    for k in order[:-1]:
        low = call(add_rows, (shape_of(piece, bf16),), (kept[k], arrived[k]))[0]
        passed[k] = move(low, dz=-k)
    cross = lambda b, z, y, c: ((b + pairs) % (2 * pairs), z, y, c) if c != b // pairs else None
    features_x = lax.ppermute(after(gathered, outs[1]), BOTH, links(cross))
    x_came = move(after(x_pack, passed[order[0]]), dx=1)
    features_c = move(after(gathered, features_x), dc=1)
    d_total, d_mine, d_mine_low, d_other = call(
        functools.partial(block_total, place),
        (
            shape_of(piece, f32),
            shape_of((images, part), f32),
            shape_of((images, part), bf16),
            shape_of((images, part), bf16),
        ),
        (after(kept[0], features_x), arrived[0], *[passed[k] for k in order[:-1]]),
    )

    d_x = move(d_mine_low, dx=1)
    d_xc = move(d_other, dx=1, dc=1)
    d_c = move(d_other, dc=1)
    ride = 2 * images * units // half
    riding = shape_of((planes, ride, half), bf16)
    out_keep, out_send = call(
        functools.partial(mix_output, place),
        (riding, riding),
        (hidden, after(x_came, d_xc), stitch_fc),
    )
    stitch_sums = call(
        functools.partial(stitch_terms, place),
        shape_of((8, channels), f32),
        (after(d_total, d_other), *pooled),
    )
    d_conv, d_bias = call(
        functools.partial(conv_slope, place, side, pool, images),
        (shape_of((side * slab, channels), bf16), shape_of((1, channels), f32)),
        (groups, d_mine, d_c, d_x, d_xc, stitch_pool, slope, window_t),
    )

    full = chip_rows + EXTRA
    stack = (chips, full, half)
    keep, send = call(
        functools.partial(kernel_grad, place, slab),
        (shape_of(stack, f32), shape_of(stack, bf16)),
        (stacked_t, after(d_conv, out_send), d_bias, stitch_sums),
        (pltpu.VMEM((chips * chip_rows, channels), f32),),
    )
    got = move(send, dc=1)
    features_xc = move(after(features_x, d_conv), dc=1)
    thin = (side, few, WIDTH, channels_in)
    pad = (pltpu.VMEM(((side + 2) * slab // 2, 3 * channels), bf16),)
    back_send = call(
        functools.partial(picture_grad, place, True, side, slab),
        shape_of(thin, bf16),
        (after(d_conv, send), kernel_back),
        pad,
    )
    flat = (full + ride, half)
    sent = call(
        sum_pieces,
        tuple(shape_of(flat, bf16) for _ in range(planes)),
        (keep, after(got, back_send, features_c, features_xc), out_send),
    )
    arrived = {k: move(sent[k], dy=1) for k in order}
    parts = {}
    for k in order:
        parts[k] = low = call(
            functools.partial(sum_three, k),
            shape_of((full + 2 * ride, half), bf16 if k else f32),
            (keep, got, arrived[k], out_keep),
        )
        if k:
            last_sum = low
            parts[k] = move(low, dz=-k)
    late = arrived[order[0]]

    back_far = move(back_send, dx=1)
    back_own = call(
        functools.partial(picture_grad, place, False, side, slab),
        shape_of(thin, bf16),
        (after(d_conv, last_sum), kernel_back),
        pad,
    )
    input_grad = call(
        functools.partial(picture_finish, place),
        shape_of(conv_input.shape, bf16),
        (group, back_own, back_far),
        scalars=1,
    )

    def both(own, axis=0):
        own = jnp.expand_dims(own, axis)
        return ordered(task, own, jnp.zeros_like(own), axis=axis)

    d_fc_last = after(d_fc, last_sum)
    steps = 3
    wide_spec = pl.BlockSpec((rows_all, part // steps), lambda i: (0, i))
    whole_spec = [pl.BlockSpec(a.shape, lambda i: (0, 0)) for a in (d_fc, x_came)]
    fc_weight_grad = pl.pallas_call(
        functools.partial(fc_grad, place),
        out_shape=shape_of((2, part, units), f32),
        grid=(steps,),
        in_specs=[wide_spec] * 4 + whole_spec,
        out_specs=pl.BlockSpec((2, part // steps, units), lambda i: (0, i, 0)),
        cost_estimate=cost(fc_grad),
        compiler_params=pltpu.CompilerParams(vmem_limit_bytes=24 * MIB),
    )(gathered, features_c, features_x, features_xc, d_fc_last, x_came)
    tall = -(-(own_rows + EXTRA) // 16) * 16
    k_mine, k_other, k_pack, out_own = call(
        functools.partial(kernel_total, place),
        (
            shape_of((tall, half), bf16),
            shape_of((tall, half), bf16),
            shape_of((tall + chips * ride // 2, half), bf16),
            shape_of((chips, images, units), f32),
        ),
        (after(parts[0], fc_weight_grad, input_grad), *[parts[planes - k] for k in range(1, planes)]),
        (pltpu.VMEM((chip_rows, half), f32), pltpu.VMEM((planes, 8, half), f32)),
    )
    k_x = move(k_mine, dx=1)
    k_xc = move(k_other, dx=1, dc=1)
    k_c = move(k_pack, dc=1)
    output, fc_bias_grad, stitch_fc_grad = call(
        functools.partial(output_finish, place),
        (
            shape_of(cotangent.shape, bf16),
            shape_of((2, units), f32),
            shape_of((2, 2, units), f32),
        ),
        (out_own, k_c, fc_sums, x_came),
        (pltpu.VMEM((images, cotangent.shape[2]), f32),),
    )
    conv_weight_grad, conv_bias_grad, stitch_pool_grad = call(
        functools.partial(kernel_finish, place),
        (
            shape_of((2, own_rows, channels), f32),
            shape_of((2, channels), f32),
            shape_of((2, 2, channels), f32),
        ),
        (k_mine, k_c, k_x, k_xc),
    )

    if pairs > 1:
        fc_weight_grad = lax.psum_scatter(
            ordered(task, fc_weight_grad, jnp.zeros_like(fc_weight_grad), axis=1),
            "batch",
            scatter_dimension=1,
            tiled=True,
        )
        conv_weight_grad, conv_bias_grad, stitch_pool_grad, fc_bias_grad = lax.psum(
            tuple(
                both(pick(value, task))
                for value in (conv_weight_grad, conv_bias_grad, stitch_pool_grad, fc_bias_grad)
            ),
            "batch",
        )
        stitch_fc_grad = lax.psum(both(pick(stitch_fc_grad, task, 1), axis=1), "batch")
    return (
        output,
        input_grad,
        conv_weight_grad,
        conv_bias_grad,
        stitch_pool_grad,
        fc_weight_grad,
        fc_bias_grad,
        stitch_fc_grad,
    )


def solution(mesh):
    pairs = mesh.shape["batch"] // 2
    planes = mesh.shape["mp"] // 4
    in_specs = (
        P(BOTH, None, None, None, None),
        P(BOTH),
        P(None, "mp", None),
        P(),
        P(),
        P(None, None, "mp"),
        P(None, "mp"),
        P(None, None, "mp"),
        P(BOTH, None, None),
    )
    out_specs = (
        P(BOTH, None, None),
        P(BOTH, None, None, None, None),
        P(None, "mp", None),
        P(),
        P(),
        P(None, "batch", "mp"),
        P(None, "mp"),
        P(None, None, "mp"),
    )
    return jax.shard_map(
        functools.partial(on_device, pairs, planes),
        mesh=mesh,
        in_specs=in_specs,
        out_specs=out_specs,
        check_vma=False,
    )
```

```python
import functools

import jax
import jax.numpy as jnp
import numpy as np
from jax import lax
from jax.experimental import pallas as pl
from jax.experimental.pallas import tpu as pltpu
from jax.sharding import PartitionSpec as P

BOTH = ("batch", "mp")
WIDTH = 16
EXTRA = 16
ROOT_HALF = 0.7071067811865476
ROOT_TWO_PI_INV = 0.3989422804014327
VMEM = pl.BlockSpec(memory_space=pltpu.VMEM)
SMEM = pl.BlockSpec(memory_space=pltpu.SMEM)
ANY = pl.BlockSpec(memory_space=pl.ANY)
DMA = pltpu.SemaphoreType.DMA
MIB = 1024 * 1024
FLOPS_PER_US = 1100000000
bf16, f32 = jnp.bfloat16, jnp.float32
shape_of = jax.ShapeDtypeStruct


MICROS = dict(
    split_weights=0.3,
    join_cores=0.3,
    split_fc=1.5,
    split_inputs=1.0,
    cot_cores=0.3,
    cot_join=0.3,
    cot_planes=0.3,
    widen=2,
    conv_forward=7.5,
    stitch_block=0.3,
    cot_rows=0.3,
    slope_and_back=1.7,
    fc_far=0.5,
    fc_own=0.5,
    fc_middle=0.3,
    fc_back=1.6,
    add_rows=0.3,
    block_total=0.3,
    mix_output=0.3,
    stitch_terms=0.3,
    conv_slope=0.6,
    kernel_grad=3.7,
    picture_grad=2.2,
    sum_pieces=0.3,
    sum_three=0.3,
    output_aside=0.3,
    output_cores=0.3,
    picture_finish=0.8,
    output_finish=0.8,
    kernel_total=0.4,
    kernel_finish=0.8,
    fc_grad=4.8,
)


def cost(body):
    name = getattr(body, "func", body).__name__
    return pl.CostEstimate(
        flops=int(MICROS[name] * FLOPS_PER_US), bytes_accessed=1, transcendentals=0
    )


def call(body, out_shape, operands, scratch=(), scalars=0, room=4, blocks=None, any_first=False):
    held = [*operands[scalars + any_first :], *jax.tree.leaves(out_shape), *scratch]
    held = [a for a in held if hasattr(a, "shape") and jnp.issubdtype(a.dtype, jnp.number)]
    need = sum(int(np.prod(a.shape)) * jnp.dtype(a.dtype).itemsize for a in held)
    need = min(need, 40 * MIB)
    steps = {}
    out_specs = jax.tree.map(lambda _: VMEM, out_shape)
    if blocks is not None:
        steps = dict(grid=(1,))
        out_specs = pl.BlockSpec(out_shape.shape, lambda i: (0,) * len(out_shape.shape))
    return pl.pallas_call(
        body,
        out_shape=out_shape,
        **steps,
        in_specs=blocks
        or [SMEM] * scalars + [ANY] * any_first + [VMEM] * (len(operands) - scalars - any_first),
        out_specs=out_specs,
        scratch_shapes=scratch,
        cost_estimate=cost(body),
        compiler_params=pltpu.CompilerParams(vmem_limit_bytes=need * 5 // 4 + room * MIB),
    )(*operands)


class Place:
    def __init__(self, pairs, planes):
        batch_at, mp_at = lax.axis_index("batch"), lax.axis_index("mp")
        self.planes = planes
        self.task = lax.div(batch_at, pairs)
        self.core = lax.rem(mp_at, 2)
        self.y = lax.rem(lax.div(mp_at, 2), 2)
        self.z = lax.div(mp_at, 4)

    def chip(self, kz, ky):
        y = self.y if ky == 0 else 1 - self.y
        return lax.rem(self.z + (self.planes - kz), self.planes) * 2 + y


def phi_cdf(value):
    return 0.5 * (1.0 + lax.erf(value * ROOT_HALF))


def gelu_slope(value):
    return phi_cdf(value) + value * ROOT_TWO_PI_INV * jnp.exp(-0.5 * value * value)


def split_high_low(value):
    high = value.astype(bf16)
    return high, (value - high.astype(f32)).astype(bf16)


def window_sum(q_ref, value):
    high, low = split_high_low(value)
    return jnp.dot(q_ref[...], high, preferred_element_type=f32) + jnp.dot(
        q_ref[...], low, preferred_element_type=f32
    )


def split_weights(place, w_ref, mine_ref, other_ref):
    at = place()
    half = mine_ref.shape[1]
    for ref, core in ((mine_ref, at.core), (other_ref, 1 - at.core)):
        lanes = pl.ds(pl.multiple_of(core * half, half), half)
        ref[...] = w_ref[at.task, :, lanes]


def join_cores(place, mine_ref, other_ref, out_ref):
    at = place()
    mine, other = mine_ref[...].astype(f32), other_ref[...].astype(f32)
    low, high = jnp.where(at.core == 0, mine, other), jnp.where(at.core == 0, other, mine)
    out_ref[...] = jnp.concatenate([low, high], axis=0).astype(bf16)


def split_fc(place, w_ref, mine_ref, other_ref, sems):
    at = place()
    part = mine_ref.shape[0]
    copies = []
    for i, (ref, core) in enumerate(((mine_ref, at.core), (other_ref, 1 - at.core))):
        rows = pl.ds(pl.multiple_of(core * part, part), part)
        copies.append(pltpu.make_async_copy(w_ref.at[at.task, rows, :], ref, sems.at[i]))
        copies[-1].start()
    for copy in copies:
        copy.wait()


def split_inputs(place, g_ref, x_ref, cot_ref, own_ref, far_ref, out_ref):
    at = place()
    few, _, side, _, depth = x_ref.shape
    units = out_ref.shape[2]
    columns = lax.broadcasted_iota(jnp.int32, (side, depth), 0)
    value = cot_ref[...].astype(f32)
    rows = jnp.concatenate([value[i, t : t + 1] for t in range(2) for i in range(few)], axis=0)
    for ref in (own_ref, far_ref):
        ref[...] = jnp.zeros_like(ref)
    for n in range(few):
        limit = side - 2 * g_ref[n]
        mark = jnp.broadcast_to(g_ref[n], (1, depth)).astype(f32)
        for y in range(side):
            reach = jnp.where(y < limit, limit, 0)
            mask = jnp.where(columns < reach, 1.0, 0.0).astype(bf16)
            for ref, task in ((own_ref, at.task), (far_ref, 1 - at.task)):
                picture = x_ref[n, task, y] * mask
                if y:
                    ref[y, n, 0:side, :] = picture
                else:
                    gap = jnp.zeros((WIDTH - side - 1, depth), f32)
                    ref[y, n] = jnp.concatenate(
                        [picture.astype(f32), gap, mark], axis=0
                    ).astype(bf16)
    for m in range(out_ref.shape[0]):
        out_ref[m] = rows[:, m * units : (m + 1) * units].astype(bf16)


def widen(place, side, own_ref, far_ref, x3_ref, xt_ref, group_ref):
    at = place()
    _, few, _, depth = own_ref.shape
    channels = group_ref.shape[1]
    marks = []
    for ref in (own_ref, far_ref):
        last = [ref[0, n].astype(f32)[WIDTH - 1 :, :channels] for n in range(few)]
        marks.append(jnp.concatenate(last, axis=0))
    group_ref[...] = jnp.where(
        at.task == 0, jnp.concatenate(marks, axis=0), jnp.concatenate(marks[::-1], axis=0)
    )
    inside = lax.rem(lax.broadcasted_iota(jnp.int32, (few * WIDTH, depth), 0), WIDTH) < side
    block = few * WIDTH
    slab = 2 * block
    for edge in (0, side + 1):
        x3_ref[edge * slab : (edge + 1) * slab, :] = jnp.zeros((slab, 3 * depth), bf16)
        xt_ref[:, edge * slab : (edge + 1) * slab] = jnp.zeros((3 * depth, slab), bf16)
    for y in range(side):
        own = own_ref[y].reshape(block, depth).astype(f32)
        far = far_ref[y].reshape(block, depth).astype(f32)
        first = at.task == 0
        if y == 0:
            own, far = jnp.where(inside, own, 0.0), jnp.where(inside, far, 0.0)
        wide = jnp.concatenate(
            [jnp.where(first, own, far), jnp.where(first, far, own)], axis=0
        )
        rows = slice((y + 1) * slab, (y + 2) * slab)
        turned = wide.T
        for kx in range(3):
            lanes = slice(kx * depth, (kx + 1) * depth)
            shift = (1 - kx) % slab
            x3_ref[rows, lanes] = (pltpu.roll(wide, shift, 0) if shift else wide).astype(bf16)
            xt_ref[lanes, rows] = (pltpu.roll(turned, shift, 1) if shift else turned).astype(bf16)


def conv_forward(place, side, pool, images, *refs):
    g_ref, x_ref, b_ref = refs[:3]
    blocks = refs[3:-5]
    pre_ref, mine_ref, other_ref, w_ref, sum_ref = refs[-5:]
    at = place()
    chips = len(blocks) // 2
    rows, half = blocks[0].shape
    here = pl.ds(pl.multiple_of(at.core * half, half), half)
    there = pl.ds(pl.multiple_of((1 - at.core) * half, half), half)
    for j in range(chips):
        to = pl.ds(pl.multiple_of(at.chip(j // 2, j % 2) * rows, 16), rows)
        w_ref[to, here] = blocks[j][...]
        w_ref[to, there] = blocks[chips + j][...]
    slab = images * WIDTH
    depth = x_ref.shape[1]
    channels = w_ref.shape[1]
    acts, pooled = {}, {}
    bias = jnp.where(at.task == 0, b_ref[0:1, :], b_ref[1:2, :])
    group = g_ref[...]
    for start in range(0, side, 4):
        rows = min(4, side - start)
        total = None
        for ky in range(3):
            part = jnp.dot(
                x_ref[(start + ky) * slab : (start + ky + rows) * slab, :],
                w_ref[ky * depth : (ky + 1) * depth, :],
                preferred_element_type=f32,
            )
            total = part if total is None else total + part
        total = total + bias
        pre_ref[start * slab : (start + rows) * slab, :] = total
        act = total * phi_cdf(total)
        for row in range(rows):
            acts[start + row] = act[row * slab : (row + 1) * slab, :]
        for p in range(pool):
            if not (start <= 2 * p + 2 < start + rows):
                continue
            rows_sum = acts[2 * p] + acts[2 * p + 1] + acts[2 * p + 2]
            for tile in range(channels // 128):
                sum_ref[p, tile, 0:slab, :] = rows_sum[:, tile * 128 : (tile + 1) * 128]
            for q in range(pool):
                kept = jnp.where(max(p, q) + group < pool, 1.0 / 9.0, 0.0)
                cell = None
                for x in range(2 * q, 2 * q + 3):
                    spot = pl.ds(x, images, stride=WIDTH)
                    column = jnp.concatenate(
                        [sum_ref[p, tile, spot, :] for tile in range(channels // 128)], axis=1
                    )
                    cell = column if cell is None else cell + column
                pooled[p, q] = cell * kept
    low = at.core == 0
    for p in range(pool // 2):
        for q in range(pool):
            zero, one = pooled[p, q], pooled[p + pool // 2, q]
            lanes = slice((p * pool + q) * channels, (p * pool + q + 1) * channels)
            mine_ref[:, lanes] = jnp.where(low, zero, one).astype(bf16)
            other_ref[:, lanes] = jnp.where(low, one, zero).astype(bf16)


def slope_and_back(pre_ref, w_ref, slope_ref, back_ref):
    slope_ref[...] = gelu_slope(pre_ref[...])
    taps = 9
    depth = w_ref.shape[0] // taps
    channels = w_ref.shape[1]
    for tap in range(taps):
        far = taps - 1 - tap
        back_ref[tap * channels : (tap + 1) * channels, :] = (
            w_ref[far * depth : (far + 1) * depth, :].astype(f32).T.astype(bf16)
        )


def cot_rows(place, own_ref, far_ref, up_ref):
    at = place()
    first = at.task == 0
    low_rows = lax.broadcasted_iota(jnp.int32, own_ref.shape[1:], 0) < 4
    for j in range(own_ref.shape[0] // 2):
        chip = at.chip(j // 2, j % 2)
        for c in range(2):
            own = own_ref[2 * chip + c].astype(f32)
            far = far_ref[2 * chip + c].astype(f32)
            low = jnp.where(first, own, far)
            high = jnp.where(first, far, own)
            zero = jnp.where(low_rows, low, pltpu.roll(high, 4, 0))
            one = jnp.where(low_rows, pltpu.roll(low, 4, 0), high)
            here = slice((2 * j + c) * 8, (2 * j + c + 1) * 8)
            up_ref[0, here, :] = jnp.where(first, zero, one)
            up_ref[1, here, :] = jnp.where(first, one, zero)


def stitch_mix(at, ref, t, u):
    row = ref[t]
    return jnp.where(u == 0, row[0:1, :], row[1:2, :])


def core_rows(at, mine, other):
    mine, other = mine.astype(f32), other.astype(f32)
    first = at.core == 0
    return jnp.concatenate(
        [jnp.where(first, mine, other), jnp.where(first, other, mine)], axis=0
    )


def stitch_block(place, mine_ref, c_ref, x_ref, xc_ref, st_ref, out_ref):
    at = place()
    channels = st_ref.shape[2]
    near = stitch_mix(at, st_ref, at.task, at.task)
    far = stitch_mix(at, st_ref, at.task, 1 - at.task)
    for cell in range(out_ref.shape[1] // channels):
        lanes = slice(cell * channels, (cell + 1) * channels)
        own = core_rows(at, mine_ref[:, lanes], c_ref[:, lanes])
        other = core_rows(at, x_ref[:, lanes], xc_ref[:, lanes])
        out_ref[:, lanes] = (near * own + far * other).astype(bf16)


def fc_far(*refs):
    blocks = refs[:-3]
    w_ref, all_ref, out_ref = refs[-3:]
    rows = blocks[0].shape[0]
    for j, block in enumerate(blocks):
        all_ref[j * rows : (j + 1) * rows, :] = block[...]
    out_ref[...] = jnp.dot(all_ref[...], w_ref[...], preferred_element_type=f32)


def fc_own(x_ref, w_ref, out_ref):
    out_ref[...] = jnp.dot(x_ref[...], w_ref[...], preferred_element_type=f32)


def four_rows(task, value, groups):
    rows = lax.broadcasted_iota(jnp.int32, (8, value.shape[1]), 0) < 4
    packed = []
    for g in range(0, groups, 2):
        one, two = value[g * 8 : g * 8 + 8], value[g * 8 + 8 : g * 8 + 16]
        zero = jnp.where(rows, one, pltpu.roll(two, 4, 0))
        last = jnp.where(rows, pltpu.roll(one, 4, 0), two)
        packed.append(jnp.where(task == 0, zero, last))
    return jnp.concatenate(packed, axis=0)


def fc_middle(
    place, own_ref, back_ref, bias_ref, mix_ref, up_ref, d_ref, hidden_ref, pack_ref, sums_ref
):
    at = place()
    first = at.task == 0
    bias = jnp.where(first, bias_ref[0:1, :], bias_ref[1:2, :])
    pre = own_ref[...] + back_ref[...] + bias
    cdf = phi_cdf(pre)
    hidden = pre * cdf
    groups = hidden.shape[0] // 8
    hidden_ref[...] = four_rows(at.task, hidden, groups)
    slope = cdf + pre * ROOT_TWO_PI_INV * jnp.exp(-0.5 * pre * pre)
    mine, other = up_ref[0], up_ref[1]
    d_hidden = stitch_mix(at, mix_ref, at.task, at.task) * mine
    d_hidden += stitch_mix(at, mix_ref, 1 - at.task, at.task) * other
    d_fc = (slope * d_hidden).astype(bf16)
    d_ref[...] = d_fc
    by_mine = jnp.sum(mine * hidden, axis=0, keepdims=True)
    by_other = jnp.sum(other * hidden, axis=0, keepdims=True)
    sums = jnp.concatenate(
        [
            jnp.sum(d_fc.astype(f32), axis=0, keepdims=True),
            jnp.where(first, by_mine, by_other),
            jnp.where(first, by_other, by_mine),
            jnp.zeros((5, by_mine.shape[1]), f32),
        ],
        axis=0,
    )
    high, low = split_high_low(sums)
    sums = jnp.concatenate([high.astype(f32), low.astype(f32)], axis=0)
    sums_ref[...] = sums
    rows = d_ref.shape[0]
    pack_ref[0 : rows // 2, :] = four_rows(1 - at.task, hidden, groups).astype(bf16)
    pack_ref[rows // 2 : rows // 2 + rows, :] = d_fc
    pack_ref[rows // 2 + rows :, :] = sums.astype(bf16)


def folded_lanes(value, lanes):
    return jnp.concatenate(
        [value[:, at : at + lanes] for at in range(0, value.shape[1], lanes)], axis=0
    )


def mix_output(place, own_ref, far_ref, mix_ref, keep_ref, send_ref):
    at = place()
    rows = lax.broadcasted_iota(jnp.int32, (8, own_ref.shape[1]), 0) < 4
    own_all = own_ref[...]
    far_all = far_ref[0 : own_all.shape[0], :].astype(f32)
    sums = []
    for t in range(2):
        sums.append(
            stitch_mix(at, mix_ref, t, at.task) * own_all
            + stitch_mix(at, mix_ref, t, 1 - at.task) * far_all
        )
    for kz in range(keep_ref.shape[0]):
        for ky, out in enumerate((keep_ref, send_ref)):
            here = slice((2 * kz + ky) * 8, (2 * kz + ky) * 8 + 8)
            zero, one = sums[0][here], sums[1][here]
            value = jnp.concatenate(
                [
                    jnp.where(rows, zero, pltpu.roll(one, 4, 0)),
                    jnp.where(rows, pltpu.roll(zero, 4, 0), one),
                ],
                axis=0,
            )
            out[kz] = folded_lanes(value, out.shape[2]).astype(bf16)


def output_finish(place, keep_ref, came_ref, sums_ref, far_ref, out_ref, bias_ref, st_ref, all_ref):
    at = place()
    units = keep_ref.shape[2]
    folds = units // came_ref.shape[1]
    first_row = came_ref.shape[0] - 8 * folds * keep_ref.shape[0]
    came_all = came_ref[first_row:, :].astype(f32)
    for j in range(keep_ref.shape[0]):
        chip = at.chip(j // 2, j % 2)
        mine = pl.ds(pl.multiple_of((2 * chip + at.core) * units, units), units)
        all_ref[:, mine] = keep_ref[j]
        other = pl.ds(pl.multiple_of((2 * chip + 1 - at.core) * units, units), units)
        rows = [8 * (folds * j + f) for f in range(folds)]
        all_ref[:, other] = jnp.concatenate([came_all[i : i + 8] for i in rows], axis=1)
    for i in range(4):
        out_ref[i] = jnp.concatenate(
            [all_ref[i : i + 1, :], all_ref[4 + i : 5 + i, :]], axis=0
        ).astype(bf16)
    first = at.task == 0
    own, far = sums_ref[...], far_ref[far_ref.shape[0] - 16 :, :].astype(f32)
    own, far = own[0:8] + own[8:16], far[0:8] + far[8:16]
    zero, one = jnp.where(first, own, far), jnp.where(first, far, own)
    bias_ref[0:1, :] = zero[0:1]
    bias_ref[1:2, :] = one[0:1]
    for t in range(2):
        st_ref[t] = jnp.concatenate([zero[1 + t : 2 + t], one[1 + t : 2 + t]], axis=0)


def fc_back(d_ref, far_ref, w_ref, wf_ref, *outs):
    chips = len(outs)
    rows = outs[0].shape[0]
    contract = (((1,), (1,)), ((), ()))
    total = lax.dot_general(d_ref[...], w_ref[...], contract, preferred_element_type=f32)
    total += lax.dot_general(far_ref[...], wf_ref[...], contract, preferred_element_type=f32)
    for j, out in enumerate(outs):
        out[...] = total[j * rows : (j + 1) * rows, :].astype(out.dtype)


def add_rows(keep_ref, got_ref, *outs):
    total = keep_ref[...] + got_ref[...].astype(f32)
    for out in outs:
        out[...] = total.astype(out.dtype)


def block_total(place, keep_ref, *refs):
    at = place()
    total_ref, mine_ref, mine_low_ref, other_ref = refs[-4:]
    total = keep_ref[...]
    for ref in refs[:-4]:
        total = total + ref[...].astype(f32)
    total_ref[...] = total
    images = mine_ref.shape[0]
    low, high = total[:images], total[images:]
    mine = jnp.where(at.core == 0, low, high)
    mine_ref[...] = mine
    mine_low_ref[...] = mine.astype(bf16)
    other_ref[...] = jnp.where(at.core == 0, high, low).astype(bf16)


def stitch_terms(place, total_ref, mine_ref, c_ref, x_ref, xc_ref, out_ref):
    at = place()
    channels = out_ref.shape[1]
    own = far = None
    for cell in range(total_ref.shape[1] // channels):
        lanes = slice(cell * channels, (cell + 1) * channels)
        grad = total_ref[:, lanes]
        one = grad * core_rows(at, mine_ref[:, lanes], c_ref[:, lanes])
        two = grad * core_rows(at, x_ref[:, lanes], xc_ref[:, lanes])
        own = one if own is None else own + one
        far = two if far is None else far + two
    out_ref[...] = jnp.concatenate(
        [
            jnp.sum(own, axis=0, keepdims=True),
            jnp.sum(far, axis=0, keepdims=True),
            jnp.zeros((6, channels), f32),
        ],
        axis=0,
    )


def conv_slope(place, side, pool, images, *refs):
    (g_ref, mine_ref, c_ref, x_ref, xc_ref, st_ref, slope_ref, q_ref) = refs[:8]
    d_ref, bias_ref = refs[8:]
    at = place()
    slab = images * WIDTH
    channels = slope_ref.shape[1]
    group = g_ref[...]

    near = stitch_mix(at, st_ref, at.task, at.task)
    far = stitch_mix(at, st_ref, 1 - at.task, at.task)
    spread = []
    for p in range(pool):
        mine_here = at.core == (2 * p) // pool
        cells = []
        for q in range(pool):
            lanes = ((p % (pool // 2)) * pool + q) * channels
            lanes = slice(lanes, lanes + channels)
            kept = jnp.where(max(p, q) + group < pool, 1.0 / 9.0, 0.0)
            one = near * mine_ref[:, lanes] + far * x_ref[:, lanes].astype(f32)
            two = near * c_ref[:, lanes].astype(f32) + far * xc_ref[:, lanes].astype(f32)
            cells.append(jnp.where(mine_here, one, two) * kept)
        spread.append(window_sum(q_ref, jnp.concatenate(cells, axis=0)))
    total = jnp.zeros((8, channels), f32)
    for y in range(side):
        act = None
        for p in range(pool):
            if 2 * p <= y <= 2 * p + 2:
                act = spread[p] if act is None else act + spread[p]
        grad = (act * slope_ref[y * slab : (y + 1) * slab, :]).astype(bf16)
        d_ref[y * slab : (y + 1) * slab, :] = grad
        total = total + jnp.sum(grad.astype(f32).reshape(-1, 8, channels), axis=0)
    bias_ref[...] = jnp.sum(total, axis=0, keepdims=True)


def kernel_grad(place, slab, xt_ref, d_ref, bias_ref, st_ref, *refs):
    keep_ref, send_ref, scr_ref = refs
    at = place()
    depth = xt_ref.shape[0]
    chips, full, half = keep_ref.shape
    rows = full - EXTRA
    count = d_ref.shape[0]
    for ky in range(3):
        scr_ref[ky * depth : (ky + 1) * depth, :] = jnp.dot(
            xt_ref[:, ky * slab : ky * slab + count], d_ref[...], preferred_element_type=f32
        )
    small = jnp.concatenate([bias_ref[...], st_ref[0:2, :]], axis=0)
    small = jnp.concatenate(
        [small[:, :half], jnp.zeros((1, half), f32), small[:, half:], jnp.zeros((1, half), f32)],
        axis=0,
    )
    high, low = split_high_low(small)
    extra = jnp.concatenate([high.astype(f32), low.astype(f32)], axis=0)
    here = pl.ds(pl.multiple_of(at.core * half, half), half)
    there = pl.ds(pl.multiple_of((1 - at.core) * half, half), half)
    for j in range(chips):
        to = pl.ds(pl.multiple_of(at.chip(j // 2, j % 2) * rows, 16), rows)
        keep_ref[j, 0:rows, :] = scr_ref[to, here]
        send_ref[j, 0:rows, :] = scr_ref[to, there].astype(bf16)
        keep_ref[j, rows:full, :] = extra
        send_ref[j, rows:full, :] = extra.astype(bf16)


def folded(extra):
    value = extra[:8] + extra[8:]
    high, low = split_high_low(value)
    return jnp.concatenate([high.astype(f32), low.astype(f32)], axis=0)


def sum_pieces(keep_ref, got_ref, output_ref, *outs):
    full = keep_ref.shape[1]
    rows = full - EXTRA
    for kz, out in enumerate(outs):
        total = keep_ref[2 * kz + 1] + got_ref[2 * kz + 1].astype(f32)
        out[0:rows, :] = total[:rows].astype(bf16)
        out[rows:full, :] = folded(total[rows:]).astype(bf16)
        out[full:, :] = output_ref[kz]


def sum_three(k, keep_ref, got_ref, came_ref, output_ref, out_ref):
    full = keep_ref.shape[1]
    rows = full - EXTRA
    more = output_ref.shape[1]
    total = keep_ref[2 * k] + got_ref[2 * k].astype(f32)
    total = jnp.concatenate([total[:rows], folded(total[rows:])], axis=0)
    total = total + came_ref[0:full, :].astype(f32)
    out_ref[0:rows, :] = total[:rows].astype(out_ref.dtype)
    out_ref[rows:full, :] = folded(total[rows:]).astype(out_ref.dtype)
    out_ref[full : full + more, :] = output_ref[k].astype(out_ref.dtype)
    out_ref[full + more :, :] = came_ref[full:, :].astype(out_ref.dtype)


def kernel_total(place, *refs):
    parts, (mine_ref, other_ref, pack_ref, keep_ref, scr_ref, small_ref) = refs[:-6], refs[-6:]
    at = place()
    rows, half = scr_ref.shape
    full = rows + EXTRA
    total = None
    riders = []
    for k, part in enumerate(parts):
        value = part[...].astype(f32)
        total = value[:rows] if total is None else total + value[:rows]
        small_ref[k] = value[rows : rows + 8] + value[rows + 8 : full]
        more = (value.shape[0] - full) // 2
        for y in range(2):
            piece = value[full + more * y : full + more * (y + 1)]
            low = [piece[i : i + 8] for i in range(0, more, 16)]
            high = [piece[i + 8 : i + 16] for i in range(0, more, 16)]
            zero = at.core == 0
            keep_ref[2 * k + y] = jnp.concatenate(
                [jnp.where(zero, a, b) for a, b in zip(low, high, strict=True)], axis=1
            )
            riders += [jnp.where(zero, b, a) for a, b in zip(low, high, strict=True)]
    scr_ref[...] = total
    small = None
    for z in range(len(parts)):
        piece = small_ref[lax.rem(at.z + (len(parts) - z), len(parts))]
        small = piece if small is None else small + piece
    high, low = split_high_low(small)
    tail = jnp.zeros((mine_ref.shape[0] - rows // 2 - EXTRA, half), f32)
    for ref, c in ((mine_ref, at.core), (other_ref, 1 - at.core)):
        piece = scr_ref[pl.ds(pl.multiple_of(c * (rows // 2), 8), rows // 2), :]
        value = [high.astype(f32), low.astype(f32), piece] + [tail] * (tail.shape[0] > 0)
        ref[...] = jnp.concatenate(value, axis=0).astype(bf16)
    pack_ref[0 : other_ref.shape[0], :] = other_ref[...]
    pack_ref[other_ref.shape[0] :, :] = jnp.concatenate(riders, axis=0).astype(bf16)


def kernel_finish(place, mine_ref, c_ref, x_ref, xc_ref, grad_ref, bias_ref, stitch_ref):
    at = place()
    rows = grad_ref.shape[1]
    half = grad_ref.shape[2] // 2
    first = at.task == 0
    low_core = at.core == 0

    def lanes(one, two):
        return jnp.concatenate(
            [jnp.where(low_core, one, two), jnp.where(low_core, two, one)], axis=1
        )

    own = lanes(mine_ref[...].astype(f32), c_ref[0 : mine_ref.shape[0], :].astype(f32))
    far = lanes(x_ref[...].astype(f32), xc_ref[...].astype(f32))
    grad_ref[0] = jnp.where(first, own, far)[EXTRA : EXTRA + rows, :]
    grad_ref[1] = jnp.where(first, far, own)[EXTRA : EXTRA + rows, :]

    def small(ref):
        value = ref[...].astype(f32)
        value = value[0:8] + value[8:16]
        return jnp.concatenate([value[0:4], value[4:8]], axis=1)

    own, far = small(mine_ref), small(x_ref)
    bias_ref[0:1, :] = jnp.where(first, own, far)[0:1, :]
    bias_ref[1:2, :] = jnp.where(first, far, own)[0:1, :]
    own_pair = jnp.where(first, own[1:3], jnp.concatenate([own[2:3], own[1:2]], axis=0))
    far_pair = jnp.where(first, jnp.concatenate([far[2:3], far[1:2]], axis=0), far[1:3])
    stitch_ref[0] = jnp.where(first, own_pair, far_pair)
    stitch_ref[1] = jnp.where(first, far_pair, own_pair)


def picture_grad(place, far, side, slab, d_ref, w_ref, out_ref, pad_ref):
    at = place()
    channels = d_ref.shape[1]
    depth = 3 * channels
    block = slab // 2
    first = (1 - at.task if far else at.task) * block
    blank = jnp.zeros((block, depth), bf16)
    pad_ref[0:block, :] = blank
    pad_ref[(side + 1) * block :, :] = blank
    for y in range(side):
        here = pl.ds(pl.multiple_of(y * slab + first, 16), block)
        wide = d_ref[here, :].astype(f32)
        rows = slice((y + 1) * block, (y + 2) * block)
        pad_ref[rows, 0:channels] = pltpu.roll(wide, 1, 0).astype(bf16)
        pad_ref[rows, channels : 2 * channels] = wide.astype(bf16)
        pad_ref[rows, 2 * channels :] = pltpu.roll(wide, block - 1, 0).astype(bf16)
    for start in range(0, side, 7):
        rows = min(7, side - start)
        total = None
        for ky in range(3):
            part = jnp.dot(
                pad_ref[(start + ky) * block : (start + ky + rows) * block, :],
                w_ref[ky * depth : (ky + 1) * depth, :],
                preferred_element_type=f32,
            )
            total = part if total is None else total + part
        for row in range(rows):
            value = total[row * block : (row + 1) * block].astype(bf16)
            out_ref[start + row] = value.reshape(out_ref.shape[1:])


def picture_finish(place, g_ref, own_ref, far_ref, out_ref):
    at = place()
    side, few, _, depth = own_ref.shape
    columns = lax.broadcasted_iota(jnp.int32, (side, depth), 0)
    for n in range(few):
        limit = side - 2 * g_ref[n]
        for y in range(side):
            reach = jnp.where(y < limit, limit, 0)
            mask = jnp.where(columns < reach, 1.0, 0.0).astype(bf16)
            out_ref[n, at.task, y] = own_ref[y, n, 0:side, :] * mask
            out_ref[n, 1 - at.task, y] = far_ref[y, n, 0:side, :] * mask


def fc_grad(place, own_ref, oc_ref, x_ref, xc_ref, d_ref, dx_ref, out_ref):
    at = place()
    same = at.core == at.task
    own = jnp.where(same, own_ref[...], oc_ref[...])
    far = jnp.where(same, x_ref[...], xc_ref[...])
    contract = (((0,), (0,)), ((), ()))
    out_ref[at.task] = lax.dot_general(own, d_ref[...], contract, preferred_element_type=f32)
    rows = d_ref.shape[0]
    d_far = dx_ref[rows // 2 : rows // 2 + rows, :]
    out_ref[1 - at.task] = lax.dot_general(far, d_far, contract, preferred_element_type=f32)


def on_device(pairs, planes, *operands):
    (
        conv_input,
        group,
        conv_weight,
        conv_bias,
        stitch_pool,
        fc_weight,
        fc_bias,
        stitch_fc,
        cotangent,
    ) = operands
    chips = 2 * planes
    place = functools.partial(Place, pairs, planes)
    task = Place(pairs, planes).task
    few = conv_input.shape[0]
    images = 2 * few
    side = conv_input.shape[2]
    channels_in = conv_input.shape[4]
    channels = conv_bias.shape[1]
    pool = (side - 3) // 2 + 1
    units = fc_bias.shape[1]
    features = pool * pool * channels
    part = features // 2
    slab = images * WIDTH
    own_rows = conv_weight.shape[1]
    chip_rows = 2 * own_rows
    half = channels // 2

    def links(where):
        pairs_of = []
        for b in range(2 * pairs):
            for m in range(4 * planes):
                to = where(b, m // 4, (m // 2) % 2, m % 2)
                if to is not None:
                    far_b, z, y, c = to
                    far_m = ((z % planes) * 2 + y) * 2 + c
                    pairs_of.append((b * 4 * planes + m, far_b * 4 * planes + far_m))
        return pairs_of

    def move(value, dx=0, dz=0, dy=0, dc=0):
        where = lambda b, z, y, c: ((b + pairs * dx) % (2 * pairs), z + dz, y ^ dy, c ^ dc)
        return lax.ppermute(value, BOTH, links(where))

    def pick(array, index, axis=0):
        return lax.dynamic_index_in_dim(array, index, axis, keepdims=False)

    def ordered(flag, mine, other, axis=0):
        return jnp.where(
            flag == 0,
            jnp.concatenate([mine, other], axis=axis),
            jnp.concatenate([other, mine], axis=axis),
        )

    def after(value, *others):
        return lax.optimization_barrier((value, *others))[0]

    shifts = []
    for near in range(1, planes // 2 + 1):
        shifts.extend(sorted({near, planes - near}))

    def gather_chips(block):
        rows = [[block, move(block, dy=1)]] + [None] * (planes - 1)
        here = {k: move(block, dz=k) for k in shifts}
        for k in shifts:
            first = after(here[k], rows[0][1]) if k == shifts[0] else here[k]
            rows[k] = [here[k], move(first, dy=1)]
        return [piece for pair in rows for piece in pair]

    weight_mine, weight_other = call(
        functools.partial(split_weights, place),
        (shape_of((own_rows, half), bf16), shape_of((own_rows, half), bf16)),
        (conv_weight,),
    )
    weight_block = call(
        functools.partial(join_cores, place),
        shape_of((chip_rows, half), bf16),
        (weight_mine, move(weight_other, dc=1)),
    )
    wide = (side, few, WIDTH, channels_in)
    picture_own, picture_send, cot_send = call(
        functools.partial(split_inputs, place),
        (
            shape_of(wide, bf16),
            shape_of(wide, bf16),
            shape_of((4 * planes, images, units), bf16),
        ),
        (after(group, weight_block), conv_input, cotangent),
        scalars=1,
    )
    picture_far = move(picture_send, dx=1)
    weight_blocks = gather_chips(weight_block)
    weight_far = [move(block, dc=1) for block in weight_blocks]
    stacked, stacked_t, groups = call(
        functools.partial(widen, place, side),
        (
            shape_of(((side + 2) * slab, 3 * channels_in), bf16),
            shape_of((3 * channels_in, (side + 2) * slab), bf16),
            shape_of((images, channels), f32),
        ),
        (picture_own, picture_far),
    )

    cot_send = after(cot_send, weight_blocks[1])
    cot_own = lax.all_to_all(cot_send, "mp", split_axis=0, concat_axis=0, tiled=True)
    cot_far = move(after(cot_own, picture_far), dx=1)

    window = np.zeros((pool * images, slab), np.float32)
    for q in range(pool):
        for n in range(images):
            window[q * images + n, n * WIDTH + 2 * q : n * WIDTH + 2 * q + 3] = 1.0
    window_t = jnp.asarray(window.T, bf16)
    stacked = after(stacked, stacked_t)
    conv_pre, pooled_mine, pooled_other, kernel = call(
        functools.partial(conv_forward, place, side, pool, images),
        (
            shape_of((side * slab, channels), f32),
            shape_of((images, part), bf16),
            shape_of((images, part), bf16),
            shape_of((chips * chip_rows, channels), bf16),
        ),
        (groups, stacked, conv_bias, *weight_blocks, *weight_far),
        (pltpu.VMEM((pool, channels // 128, slab + WIDTH, 128), f32),),
    )

    pooled_mine = after(pooled_mine, cot_far)
    pooled_x = move(pooled_mine, dx=1)
    pooled_xc = move(pooled_other, dx=1, dc=1)
    pooled_c = move(pooled_other, dc=1)
    pooled = (pooled_mine, pooled_c, pooled_x, pooled_xc)
    piece = (2 * images, part)
    rows_all = chips * 2 * images
    blocks = gather_chips(
        call(functools.partial(stitch_block, place), shape_of(piece, bf16), (*pooled, stitch_pool))
    )

    up = call(
        functools.partial(cot_rows, place),
        shape_of((2, rows_all, units), f32),
        (cot_own, cot_far),
    )

    fc_mine, fc_other = call(
        functools.partial(split_fc, place),
        (shape_of((part, units), bf16), shape_of((part, units), bf16)),
        (after(fc_weight, pooled_mine),),
        (DMA((2,)),),
        blocks=None,
        any_first=True,
    )
    fc_other = move(fc_other, dc=1)

    slope, kernel_back = call(
        slope_and_back,
        (
            shape_of(conv_pre.shape, f32),
            shape_of((9 * channels, channels_in), bf16),
        ),
        (conv_pre, kernel),
    )

    gathered, far_term = call(
        fc_far,
        (shape_of((rows_all, part), bf16), shape_of((rows_all, units), f32)),
        (*blocks, after(fc_other, slope, kernel_back, up)),
    )
    far_back = move(far_term, dc=1)
    own_term = call(fc_own, shape_of((rows_all, units), f32), (gathered, fc_mine))
    d_fc, hidden, x_pack, fc_sums = call(
        functools.partial(fc_middle, place),
        (
            shape_of((rows_all, units), bf16),
            shape_of((rows_all // 2, units), f32),
            shape_of((rows_all // 2 + rows_all + 16, units), bf16),
            shape_of((16, units), f32),
        ),
        (own_term, far_back, fc_bias, stitch_fc, up),
    )
    d_fc_far = move(d_fc, dc=1)
    outs = call(
        fc_back,
        tuple(shape_of(piece, bf16 if j % 2 else f32) for j in range(chips)),
        (d_fc, d_fc_far, fc_mine, fc_other),
    )
    kept, sent = outs[0::2], outs[1::2]

    order = shifts[::-1] + [0]
    arrived = {k: move(sent[k], dy=1) for k in order}
    passed = {}
    for k in order[:-1]:
        low = call(add_rows, (shape_of(piece, bf16),), (kept[k], arrived[k]))[0]
        passed[k] = move(low, dz=-k)
    cross = lambda b, z, y, c: ((b + pairs) % (2 * pairs), z, y, c) if c != b // pairs else None
    features_x = lax.ppermute(after(gathered, outs[1]), BOTH, links(cross))
    x_came = move(after(x_pack, passed[order[0]]), dx=1)
    features_c = move(after(gathered, features_x), dc=1)
    d_total, d_mine, d_mine_low, d_other = call(
        functools.partial(block_total, place),
        (
            shape_of(piece, f32),
            shape_of((images, part), f32),
            shape_of((images, part), bf16),
            shape_of((images, part), bf16),
        ),
        (after(kept[0], features_x), arrived[0], *[passed[k] for k in order[:-1]]),
    )

    d_x = move(d_mine_low, dx=1)
    d_xc = move(d_other, dx=1, dc=1)
    d_c = move(d_other, dc=1)
    ride = 2 * images * units // half
    riding = shape_of((planes, ride, half), bf16)
    out_keep, out_send = call(
        functools.partial(mix_output, place),
        (riding, riding),
        (hidden, after(x_came, d_xc), stitch_fc),
    )
    stitch_sums = call(
        functools.partial(stitch_terms, place),
        shape_of((8, channels), f32),
        (d_total, *pooled),
    )
    d_conv, d_bias = call(
        functools.partial(conv_slope, place, side, pool, images),
        (shape_of((side * slab, channels), bf16), shape_of((1, channels), f32)),
        (groups, d_mine, d_c, d_x, d_xc, stitch_pool, slope, window_t),
    )

    full = chip_rows + EXTRA
    stack = (chips, full, half)
    keep, send = call(
        functools.partial(kernel_grad, place, slab),
        (shape_of(stack, f32), shape_of(stack, bf16)),
        (stacked_t, after(d_conv, out_send), d_bias, stitch_sums),
        (pltpu.VMEM((chips * chip_rows, channels), f32),),
    )
    got = move(send, dc=1)
    features_xc = move(after(features_x, d_conv), dc=1)
    thin = (side, few, WIDTH, channels_in)
    pad = (pltpu.VMEM(((side + 2) * slab // 2, 3 * channels), bf16),)
    back_send = call(
        functools.partial(picture_grad, place, True, side, slab),
        shape_of(thin, bf16),
        (after(d_conv, send), kernel_back),
        pad,
    )
    flat = (full + ride, half)
    sent = call(
        sum_pieces,
        tuple(shape_of(flat, bf16) for _ in range(planes)),
        (keep, after(got, back_send, features_c, features_xc), out_send),
    )
    arrived = {k: move(sent[k], dy=1) for k in order}
    parts = {}
    for k in order:
        parts[k] = low = call(
            functools.partial(sum_three, k),
            shape_of((full + 2 * ride, half), bf16 if k else f32),
            (keep, got, arrived[k], out_keep),
        )
        if k:
            last_sum = low
            parts[k] = move(low, dz=-k)
    late = arrived[order[0]]

    back_far = move(back_send, dx=1)
    back_own = call(
        functools.partial(picture_grad, place, False, side, slab),
        shape_of(thin, bf16),
        (after(d_conv, last_sum), kernel_back),
        pad,
    )
    input_grad = call(
        functools.partial(picture_finish, place),
        shape_of(conv_input.shape, bf16),
        (group, back_own, back_far),
        scalars=1,
    )

    def both(own, axis=0):
        own = jnp.expand_dims(own, axis)
        return ordered(task, own, jnp.zeros_like(own), axis=axis)

    d_fc_last = after(d_fc, last_sum)
    steps = 3
    wide_spec = pl.BlockSpec((rows_all, part // steps), lambda i: (0, i))
    whole_spec = [pl.BlockSpec(a.shape, lambda i: (0, 0)) for a in (d_fc, x_came)]
    fc_weight_grad = pl.pallas_call(
        functools.partial(fc_grad, place),
        out_shape=shape_of((2, part, units), f32),
        grid=(steps,),
        in_specs=[wide_spec] * 4 + whole_spec,
        out_specs=pl.BlockSpec((2, part // steps, units), lambda i: (0, i, 0)),
        cost_estimate=cost(fc_grad),
        compiler_params=pltpu.CompilerParams(vmem_limit_bytes=24 * MIB),
    )(gathered, features_c, features_x, features_xc, d_fc_last, x_came)
    tall = -(-(own_rows + EXTRA) // 16) * 16
    k_mine, k_other, k_pack, out_own = call(
        functools.partial(kernel_total, place),
        (
            shape_of((tall, half), bf16),
            shape_of((tall, half), bf16),
            shape_of((tall + chips * ride // 2, half), bf16),
            shape_of((chips, images, units), f32),
        ),
        (after(parts[0], fc_weight_grad, input_grad), *[parts[planes - k] for k in range(1, planes)]),
        (pltpu.VMEM((chip_rows, half), f32), pltpu.VMEM((planes, 8, half), f32)),
    )
    k_x = move(k_mine, dx=1)
    k_xc = move(k_other, dx=1, dc=1)
    k_c = move(k_pack, dc=1)
    output, fc_bias_grad, stitch_fc_grad = call(
        functools.partial(output_finish, place),
        (
            shape_of(cotangent.shape, bf16),
            shape_of((2, units), f32),
            shape_of((2, 2, units), f32),
        ),
        (out_own, k_c, fc_sums, x_came),
        (pltpu.VMEM((images, cotangent.shape[2]), f32),),
    )
    conv_weight_grad, conv_bias_grad, stitch_pool_grad = call(
        functools.partial(kernel_finish, place),
        (
            shape_of((2, own_rows, channels), f32),
            shape_of((2, channels), f32),
            shape_of((2, 2, channels), f32),
        ),
        (k_mine, k_c, k_x, k_xc),
    )

    if pairs > 1:
        fc_weight_grad = lax.psum_scatter(
            ordered(task, fc_weight_grad, jnp.zeros_like(fc_weight_grad), axis=1),
            "batch",
            scatter_dimension=1,
            tiled=True,
        )
        conv_weight_grad, conv_bias_grad, stitch_pool_grad, fc_bias_grad = lax.psum(
            tuple(
                both(pick(value, task))
                for value in (conv_weight_grad, conv_bias_grad, stitch_pool_grad, fc_bias_grad)
            ),
            "batch",
        )
        stitch_fc_grad = lax.psum(both(pick(stitch_fc_grad, task, 1), axis=1), "batch")
    return (
        output,
        input_grad,
        conv_weight_grad,
        conv_bias_grad,
        stitch_pool_grad,
        fc_weight_grad,
        fc_bias_grad,
        stitch_fc_grad,
    )


def solution(mesh):
    pairs = mesh.shape["batch"] // 2
    planes = mesh.shape["mp"] // 4
    in_specs = (
        P(BOTH, None, None, None, None),
        P(BOTH),
        P(None, "mp", None),
        P(),
        P(),
        P(None, None, "mp"),
        P(None, "mp"),
        P(None, None, "mp"),
        P(BOTH, None, None),
    )
    out_specs = (
        P(BOTH, None, None),
        P(BOTH, None, None, None, None),
        P(None, "mp", None),
        P(),
        P(),
        P(None, "batch", "mp"),
        P(None, "mp"),
        P(None, None, "mp"),
    )
    return jax.shard_map(
        functools.partial(on_device, pairs, planes),
        mesh=mesh,
        in_specs=in_specs,
        out_specs=out_specs,
        check_vma=False,
    )
```
